32 devices in a mesh: batch: 4 (over y, core), blk: 8 (over z, x).
Axes of the slice: x: 2, y: 2, z: 4, core: 2. Of those that a mesh axis runs over, the one named last changes fastest.
Arguments:
- source: bfloat16 [8, 1024, 512], P('batch', 'blk'), may hold values from -6 to 6
- target: bfloat16 [8, 1024, 512], P('batch', 'blk'), may hold values from -6 to 6
- src_lengths: int32 [8, 32], P('batch'), may hold values from 1 to 770, as said below
- tgt_lengths: int32 [8, 32], P('batch'), may hold values from 1 to 770, as said below
- pairing: int32 [8, 32], P('batch'), may hold values from 0 to 31, each once within a row
- enc_w_input: bfloat16 [3, 512, 512], replicated, may hold values from -0.25 to 0.25
- enc_b_query: float32 [512], replicated, may hold values from -4 to 4
- enc_b_value: float32 [512], replicated, may hold values from -0.75 to 0.75
- enc_w_out: bfloat16 [512, 512], replicated, may hold values from -4 to 4
- enc_b_out: float32 [512], replicated, may hold values from -4 to 4
- enc_gains: float32 [2, 512], replicated, may hold values from 0.5 to 1.5
- enc_shifts: float32 [2, 512], replicated, may hold values from -4 to 4
- enc_w_up: bfloat16 [512, 2048], replicated, may hold values from -0.25 to 0.25
- enc_b_up: float32 [2048], replicated, may hold values from -4 to 4
- enc_w_down: bfloat16 [2048, 512], replicated, may hold values from -0.125 to 0.125
- enc_b_down: float32 [512], replicated, may hold values from -4 to 4
- dec_w_input: bfloat16 [3, 512, 512], replicated, may hold values from -0.25 to 0.25
- dec_b_query: float32 [512], replicated, may hold values from -4 to 4
- dec_b_value: float32 [512], replicated, may hold values from -0.75 to 0.75
- dec_w_out: bfloat16 [512, 512], replicated, may hold values from -4 to 4
- dec_b_out: float32 [512], replicated, may hold values from -4 to 4
- cross_w_input: bfloat16 [3, 512, 512], replicated, may hold values from -0.25 to 0.25
- cross_b_query: float32 [512], replicated, may hold values from -4 to 4
- cross_b_value: float32 [512], replicated, may hold values from -0.75 to 0.75
- cross_w_out: bfloat16 [512, 512], replicated, may hold values from -4 to 4
- cross_b_out: float32 [512], replicated, may hold values from -4 to 4
- dec_gains: float32 [3, 512], replicated, may hold values from 0.5 to 1.5
- dec_shifts: float32 [3, 512], replicated, may hold values from -4 to 4
- dec_w_up: bfloat16 [512, 2048], replicated, may hold values from -0.25 to 0.25
- dec_b_up: float32 [2048], replicated, may hold values from -4 to 4
- dec_w_down: bfloat16 [2048, 512], replicated, may hold values from -0.125 to 0.125
- dec_b_down: float32 [512], replicated, may hold values from -4 to 4
- cotangent: bfloat16 [8, 1024, 512], P('batch', 'blk'), may hold values from -6 to 6
Outputs:
- enc_out: bfloat16 [8, 1024, 512], P('batch', 'blk')
- dec_out: bfloat16 [8, 1024, 512], P('batch', 'blk')
- source_grad: float32 [8, 1024, 512], P('batch', 'blk')
- target_grad: float32 [8, 1024, 512], P('batch', 'blk')
- grad_enc_w_input: float32 [3, 512, 512], P(None, 'blk')
- grad_enc_b_query: float32 [512], replicated
- grad_enc_b_value: float32 [512], replicated
- grad_enc_w_out: float32 [512, 512], P('blk')
- grad_enc_b_out: float32 [512], replicated
- grad_enc_gains: float32 [2, 512], replicated
- grad_enc_shifts: float32 [2, 512], replicated
- grad_enc_w_up: float32 [512, 2048], P('blk')
- grad_enc_b_up: float32 [2048], replicated
- grad_enc_w_down: float32 [2048, 512], P('blk')
- grad_enc_b_down: float32 [512], replicated
- grad_dec_w_input: float32 [3, 512, 512], P(None, 'blk')
- grad_dec_b_query: float32 [512], replicated
- grad_dec_b_value: float32 [512], replicated
- grad_dec_w_out: float32 [512, 512], P('blk')
- grad_dec_b_out: float32 [512], replicated
- grad_cross_w_input: float32 [3, 512, 512], P(None, 'blk')
- grad_cross_b_query: float32 [512], replicated
- grad_cross_b_value: float32 [512], replicated
- grad_cross_w_out: float32 [512, 512], P('blk')
- grad_cross_b_out: float32 [512], replicated
- grad_dec_gains: float32 [3, 512], replicated
- grad_dec_shifts: float32 [3, 512], replicated
- grad_dec_w_up: float32 [512, 2048], P('blk')
- grad_dec_b_up: float32 [2048], replicated
- grad_dec_w_down: float32 [2048, 512], P('blk')
- grad_dec_b_down: float32 [512], replicated
The draws below stay inside these ranges and needn't reach their ends.
Inputs may be any that keep to these rules, and one draw needn't show every extreme that they name: `src_lengths`: each row's entries sum to 1024; in each group of 2 streams along batch, one stream has a sentence of exactly the largest length. `tgt_lengths`: each row's entries sum to 1024; in each group of 2 streams along batch, one stream has a sentence of exactly the largest length. `pairing`: each row holds every number of 0 to 31 once.
All inputs are finite; a program needn't handle non-finite values.
Results may differ from the reference program's by a relative error of at most 0.04.
Values may be sent and summed in bfloat16 or wider, within the bound.
No kernel may reach another device: no remote copies, remote signals or barrier semaphores. Data moves between devices by JAX's collectives and lax.ppermute only.
A program may use at most 256 MiB of HBM per device.

```python
import math
import jax
import jax.numpy as jnp
from jax import lax

D = 512
H = 8
FF = 2048
TOK_DEV = 128
SEQ_DEV = 2
SEGS = 32
LENGTH = 1024
STREAMS = 8


def stream_lengths(key):
    pick_key, cut_key = jax.random.split(key)
    groups = STREAMS // SEQ_DEV
    chosen = jax.random.randint(pick_key, (groups,), 0, SEQ_DEV)
    spanning = jnp.arange(STREAMS, dtype=jnp.int32) % SEQ_DEV == jnp.repeat(chosen, SEQ_DEV)
    lower_count = (SEGS - 1) // 2
    upper_count = SEGS - 1 - lower_count
    first_fixed = TOK_DEV - 1
    second_fixed = LENGTH - TOK_DEV + 1

    def one_row(row_key, spanning_row):
        spread_key, first_key, second_key = jax.random.split(row_key, 3)
        extra = jax.random.permutation(spread_key, LENGTH - 3)[:SEGS - 3] + 1
        extra = extra + (extra >= first_fixed).astype(jnp.int32)
        extra = extra + (extra >= second_fixed).astype(jnp.int32)
        fixed_pair = jnp.array([first_fixed, second_fixed], jnp.int32)
        anywhere = jnp.concatenate([extra.astype(jnp.int32), fixed_pair])
        lower_cuts = jax.random.permutation(first_key, TOK_DEV - 2)[:lower_count - 1] + 1
        upper_cuts = jax.random.permutation(second_key, TOK_DEV - 2)[:upper_count - 1] + (second_fixed + 1)
        spanning_cuts = jnp.concatenate([lower_cuts.astype(jnp.int32), upper_cuts.astype(jnp.int32), fixed_pair])
        cut_points = jnp.where(spanning_row, spanning_cuts, anywhere)
        cut_points = jnp.sort(cut_points).astype(jnp.int32)
        borders = jnp.concatenate([jnp.zeros((1,), jnp.int32), cut_points, jnp.full((1,), LENGTH, jnp.int32)])
        return borders[1:] - borders[:-1]
    return jax.vmap(one_row)(jax.random.split(cut_key, STREAMS), spanning)


def draw_src_lengths(key, part):
    key = jax.random.fold_in(key, 7)
    return stream_lengths(key)


def draw_tgt_lengths(key, part):
    key = jax.random.fold_in(key, 11)
    return stream_lengths(key)


def shard_levels(rng, shape, pieces, least, largest):
    level = 1.0
    for axis_at, shards_of in pieces:
        steps = jax.random.uniform(jax.random.fold_in(jax.random.fold_in(rng, 6), axis_at), (shards_of,), jnp.float32, least / len(pieces), largest / len(pieces))
        level = level * jnp.repeat(jnp.exp(steps), shape[axis_at] // shards_of).reshape((-1,) + (1,) * (len(shape) - 1 - axis_at))
    return level


def bell_draw(own_key, shape, scale, limit, cuts=(), kind=jnp.bfloat16):
    level = shard_levels(own_key, shape, cuts, -0.22, 0.18) if cuts else 1.0
    values = jax.random.normal(own_key, shape, jnp.float32) * scale * level
    return jnp.minimum(jnp.maximum(values, -limit), limit).astype(kind)


def setup_inputs(seed: int = 0) -> dict:
    arg_keys = jax.random.split(jax.random.key(seed), 34)
    source = bell_draw(arg_keys[0], (STREAMS, LENGTH, D), 1.0, 6.0, ((0, 4), (1, 8)))
    target = bell_draw(arg_keys[1], (STREAMS, LENGTH, D), 1.0, 6.0, ((0, 4), (1, 8)))
    src_lengths = draw_src_lengths(jax.random.fold_in(arg_keys[33], 71), 0)
    tgt_lengths = draw_tgt_lengths(jax.random.fold_in(arg_keys[33], 71), 0)
    pairing = jax.vmap(lambda own: jax.random.permutation(own, SEGS))(jax.random.split(arg_keys[4], STREAMS)).reshape((STREAMS, SEGS)).astype(jnp.int32)
    enc_w_input = bell_draw(arg_keys[5], (3, D, D), D ** -0.5, 0.25)
    enc_b_query = bell_draw(arg_keys[6], (D,), 0.3, 4.0, (), jnp.float32)
    enc_b_value = bell_draw(arg_keys[7], (D,), 0.05, 0.75, (), jnp.float32)
    enc_w_out = bell_draw(arg_keys[8], (D, D), 2 ** -0.5, 4.0)
    enc_b_out = bell_draw(arg_keys[9], (D,), 0.3, 4.0, (), jnp.float32)
    enc_gains = jnp.clip(1.0 + 0.1 * jax.random.normal(arg_keys[10], (2, D), jnp.float32), 0.5, 1.5)
    enc_shifts = bell_draw(arg_keys[11], (2, D), 0.3, 4.0, (), jnp.float32)
    enc_w_up = bell_draw(arg_keys[12], (D, FF), D ** -0.5, 0.25)
    enc_b_up = bell_draw(arg_keys[13], (FF,), 0.3, 4.0, (), jnp.float32)
    enc_w_down = bell_draw(arg_keys[14], (FF, D), FF ** -0.5, 0.125)
    enc_b_down = bell_draw(arg_keys[15], (D,), 0.3, 4.0, (), jnp.float32)
    dec_w_input = bell_draw(arg_keys[16], (3, D, D), D ** -0.5, 0.25)
    dec_b_query = bell_draw(arg_keys[17], (D,), 0.3, 4.0, (), jnp.float32)
    dec_b_value = bell_draw(arg_keys[18], (D,), 0.05, 0.75, (), jnp.float32)
    dec_w_out = bell_draw(arg_keys[19], (D, D), 2 ** -0.5, 4.0)
    dec_b_out = bell_draw(arg_keys[20], (D,), 0.3, 4.0, (), jnp.float32)
    cross_w_input = bell_draw(arg_keys[21], (3, D, D), D ** -0.5, 0.25)
    cross_b_query = bell_draw(arg_keys[22], (D,), 0.3, 4.0, (), jnp.float32)
    cross_b_value = bell_draw(arg_keys[23], (D,), 0.05, 0.75, (), jnp.float32)
    cross_w_out = bell_draw(arg_keys[24], (D, D), 2 ** -0.5, 4.0)
    cross_b_out = bell_draw(arg_keys[25], (D,), 0.3, 4.0, (), jnp.float32)
    dec_gains = jnp.clip(1.0 + 0.1 * jax.random.normal(arg_keys[26], (3, D), jnp.float32), 0.5, 1.5)
    dec_shifts = bell_draw(arg_keys[27], (3, D), 0.3, 4.0, (), jnp.float32)
    dec_w_up = bell_draw(arg_keys[28], (D, FF), D ** -0.5, 0.25)
    dec_b_up = bell_draw(arg_keys[29], (FF,), 0.3, 4.0, (), jnp.float32)
    dec_w_down = bell_draw(arg_keys[30], (FF, D), FF ** -0.5, 0.125)
    dec_b_down = bell_draw(arg_keys[31], (D,), 0.3, 4.0, (), jnp.float32)
    cotangent = bell_draw(arg_keys[32], (STREAMS, LENGTH, D), 1.0, 6.0, ((0, 4), (1, 8)))
    return {"source": source, "target": target, "src_lengths": src_lengths, "tgt_lengths": tgt_lengths, "pairing": pairing, "enc_w_input": enc_w_input, "enc_b_query": enc_b_query, "enc_b_value": enc_b_value, "enc_w_out": enc_w_out, "enc_b_out": enc_b_out, "enc_gains": enc_gains, "enc_shifts": enc_shifts, "enc_w_up": enc_w_up, "enc_b_up": enc_b_up, "enc_w_down": enc_w_down, "enc_b_down": enc_b_down, "dec_w_input": dec_w_input, "dec_b_query": dec_b_query, "dec_b_value": dec_b_value, "dec_w_out": dec_w_out, "dec_b_out": dec_b_out, "cross_w_input": cross_w_input, "cross_b_query": cross_b_query, "cross_b_value": cross_b_value, "cross_w_out": cross_w_out, "cross_b_out": cross_b_out, "dec_gains": dec_gains, "dec_shifts": dec_shifts, "dec_w_up": dec_w_up, "dec_b_up": dec_b_up, "dec_w_down": dec_w_down, "dec_b_down": dec_b_down, "cotangent": cotangent}


@jax.custom_vjp
def low(v):
    return lax.optimization_barrier(v.astype(jnp.bfloat16)).astype(jnp.float32)

@jax.custom_vjp
def low_back(v):
    return v

def low_keep(v):
    return (low(v), None)

def low_pass(kept, grad):
    return (grad,)

def back_keep(v):
    return (v, None)

def back_low(kept, grad):
    return (low(grad),)
low.defvjp(low_keep, low_pass)
low_back.defvjp(back_keep, back_low)

def multiply(left, right):
    return jnp.dot(left, right, precision=lax.Precision.HIGHEST)

def both_ways(values):
    return low_back(low(values))

def norm_rows(values, gain, shift):
    centred = values - lax.optimization_barrier(jnp.mean(values, axis=-1, keepdims=True))
    spread = lax.optimization_barrier(jnp.mean(centred * centred, axis=-1, keepdims=True))
    return centred * lax.rsqrt(spread + 1e-05) * gain + shift

def segment_ids(seg_ends, amount):
    places = jnp.arange(amount, dtype=jnp.int32)
    return lax.optimization_barrier(jnp.sum((seg_ends[None, :] <= places[:, None]).astype(jnp.int32), axis=1, dtype=jnp.int32))

def attention(query_all, key_all, value_all, query_map, key_segs):
    block_size = math.gcd(LENGTH, 512)
    head_size = D // H
    factor = 1.0 / math.sqrt(head_size)
    key_heads = key_all.reshape(LENGTH, H, head_size)
    value_heads = value_all.reshape(LENGTH, H, head_size)

    def one_block(inputs):
        query_block, query_marks = inputs
        query_heads = query_block.reshape(block_size, H, head_size)
        scores = jnp.einsum('qhd,khd->qhk', query_heads, key_heads, precision=lax.Precision.HIGHEST) * factor
        scores = low_back(scores)
        allowed = query_marks[:, None, None] == key_segs[None, None, :]
        scores = jnp.where(allowed, scores, -1e+30)
        row_peak = lax.optimization_barrier(jnp.max(scores, axis=2, keepdims=True))
        weights = jnp.where(allowed, jnp.exp(scores - row_peak), 0.0)
        row_total = lax.optimization_barrier(jnp.sum(weights, axis=2, keepdims=True))
        weights_low = low(weights / row_total)
        combined = jnp.einsum('qhk,khd->qhd', weights_low, value_heads, precision=lax.Precision.HIGHEST)
        return combined.reshape(block_size, D)
    blocks = (query_all.reshape(LENGTH // block_size, block_size, D), query_map.reshape(LENGTH // block_size, block_size))
    return lax.map(jax.checkpoint(one_block), blocks).reshape(LENGTH, D)

def attend(query_in, key_in, query_map, key_segs, weights):
    w_input, b_query, b_value, w_out, b_out = weights
    query_all = both_ways(multiply(query_in, w_input[0]) + b_query)
    key_all = both_ways(multiply(key_in, w_input[1]))
    value_all = both_ways(multiply(key_in, w_input[2]) + b_value)
    attended = both_ways(attention(query_all, key_all, value_all, query_map, key_segs))
    return low_back(multiply(attended, w_out) + b_out)

def feed(values, w_up, b_up, w_down, b_down):
    pre_act = low_back(multiply(low(values), w_up) + b_up)
    activated = jax.nn.gelu(pre_act, approximate=False)
    return low_back(multiply(low(activated), w_down) + b_down)

def layers(source, target, src_segs, tgt_segs, pair_segs, weights):
    enc = weights[:11]
    dec = weights[11:]
    first_norm = norm_rows(source + attend(source, source, src_segs, src_segs, enc[0:5]), enc[5][0], enc[6][0])
    encoded = norm_rows(first_norm + feed(first_norm, enc[7], enc[8], enc[9], enc[10]), enc[5][1], enc[6][1])
    memory = low(encoded)
    upper_norm = norm_rows(target + attend(target, target, tgt_segs, tgt_segs, dec[0:5]), dec[10][0], dec[11][0])
    crossed = norm_rows(upper_norm + attend(low(upper_norm), memory, pair_segs, src_segs, dec[5:10]), dec[10][1], dec[11][1])
    decoded = norm_rows(crossed + feed(crossed, dec[12], dec[13], dec[14], dec[15]), dec[10][2], dec[11][2])
    return (encoded, decoded)

def reference(source, target, src_lengths, tgt_lengths, pairing, enc_w_input, enc_b_query, enc_b_value, enc_w_out, enc_b_out, enc_gains, enc_shifts, enc_w_up, enc_b_up, enc_w_down, enc_b_down, dec_w_input, dec_b_query, dec_b_value, dec_w_out, dec_b_out, cross_w_input, cross_b_query, cross_b_value, cross_w_out, cross_b_out, dec_gains, dec_shifts, dec_w_up, dec_b_up, dec_w_down, dec_b_down, cotangent):
    params = tuple((item.astype(jnp.float32) for item in (enc_w_input, enc_b_query, enc_b_value, enc_w_out, enc_b_out, enc_gains, enc_shifts, enc_w_up, enc_b_up, enc_w_down, enc_b_down, dec_w_input, dec_b_query, dec_b_value, dec_w_out, dec_b_out, cross_w_input, cross_b_query, cross_b_value, cross_w_out, cross_b_out, dec_gains, dec_shifts, dec_w_up, dec_b_up, dec_w_down, dec_b_down)))

    def one_stream(sums, inputs):
        src_row, tgt_row, src_len, tgt_len, pair_row, cot_row = inputs
        src_segs = segment_ids(jnp.cumsum(src_len, dtype=jnp.int32), LENGTH)
        tgt_segs = segment_ids(jnp.cumsum(tgt_len, dtype=jnp.int32), LENGTH)
        pair_segs = jnp.take(pair_row, tgt_segs).astype(jnp.int32)

        def forward(src_values, tgt_values, *weights):
            return layers(src_values, tgt_values, src_segs, tgt_segs, pair_segs, weights)
        (encoded, decoded), pull = jax.vjp(forward, src_row.astype(jnp.float32), tgt_row.astype(jnp.float32), *params)
        grads = pull((jnp.zeros_like(encoded), cot_row.astype(jnp.float32)))
        updated = tuple((total + term for total, term in zip(sums, grads[2:])))
        return (updated, (encoded.astype(jnp.bfloat16), decoded.astype(jnp.bfloat16), grads[0], grads[1]))
    start_sums = tuple((jnp.zeros_like(item) for item in params))
    sums, (enc_rows, dec_rows, src_grads, tgt_grads) = lax.scan(one_stream, start_sums, (source, target, src_lengths, tgt_lengths, pairing, cotangent))
    return (enc_rows, dec_rows, src_grads, tgt_grads) + tuple(sums)
```

```python
import math

import jax
import jax.numpy as jnp
from jax import lax
from jax.experimental import pallas as pl
from jax.experimental.pallas import tpu as pltpu
from jax.sharding import PartitionSpec as P

H = 8
LANES = 128
MATS = 4
negative = -1e30
bf16 = jnp.bfloat16
f32 = jnp.float32
VMEM_BYTES = 56 * 1024 * 1024


def nn(left, right):
    return lax.dot_general(left, right, (((1,), (0,)), ((), ())), preferred_element_type=f32)


def nt(left, right):
    return lax.dot_general(left, right, (((1,), (1,)), ((), ())), preferred_element_type=f32)


def tn(left, right):
    return lax.dot_general(left, right, (((0,), (0,)), ((), ())), preferred_element_type=f32)


def turned(values):
    return values.astype(f32).T


def norm_forward(rows):
    centred = rows - jnp.mean(rows, axis=-1, keepdims=True)
    spread = jnp.mean(centred * centred, axis=-1, keepdims=True)
    rstd = lax.rsqrt(spread + 1e-05)
    return centred * rstd, rstd


def norm_backward(dy, normed, rstd, gain):
    dn = dy * gain
    dr = (
        dn
        - jnp.mean(dn, axis=-1, keepdims=True)
        - normed * jnp.mean(dn * normed, axis=-1, keepdims=True)
    ) * rstd
    return dr, column_sum(dy * normed), column_sum(dy)


def column_sum(values):
    return jnp.sum(values, axis=0, keepdims=True)


def gelu_pair(values):
    bell = jnp.exp(-0.5 * values * values)
    t = 1.0 / (1.0 + (0.3275911 * math.sqrt(0.5)) * jnp.abs(values))
    poly = 0.5 * 1.061405429
    for number in (-1.453152027, 1.421413741, -0.284496736, 0.254829592):
        poly = poly * t + 0.5 * number
    tail = poly * t * bell
    share = jnp.where(values >= 0, 1.0 - tail, tail)
    return values * share, share + values * bell * (1.0 / math.sqrt(2.0 * math.pi))


class Layout:
    def __init__(self, table, keep, send, blocks):
        self.table, self.keep, self.send, self.blocks = table, keep, send, blocks

    def put(self, values, mat, group, block0=0, count=None):
        count = self.blocks if count is None else count
        low = values.astype(bf16)
        rows = low.shape[0] // count
        rel = lax.bitwise_xor(self.table[0], mat)
        y_rel = lax.bitwise_and(rel, 1)
        half = self.blocks // 2

        def fill(ref):
            for number in range(count):
                place = self.table[1 + block0 + number]
                ref[y_rel * 2 + place // half, place % half, group] = low[
                    number * rows : (number + 1) * rows
                ]

        pl.when(rel < 2)(lambda: fill(self.keep))
        pl.when(rel >= 2)(lambda: fill(self.send))


def head_masks(axis, shape, head_size):
    places = lax.broadcasted_iota(jnp.int32, shape, axis)
    return [places // head_size == number for number in range(LANES // head_size)]


def attn_forward_kernel(cross, part_count, *refs):
    refs = list(refs)
    take = lambda: refs.pop(0)
    parts = [take() for _ in range(part_count)]
    if cross:
        prev_norm, prev_gain, prev_shift = take(), take(), take()
    seg_query, seg_key = take(), take()
    w_input, b_query, b_value, w_out, b_out = [take() for _ in range(5)]
    if not cross:
        x_all = take()
    q_out, k_out, v_out, att_out, lse_out, norm_out, rstd_out = [take() for _ in range(7)]
    own_rows = q_out.shape[0]
    width = q_out.shape[1]
    head_size = width // H
    at = 0
    for part in parts:
        rows = part.shape[0]
        piece = part[...]
        k_out[at : at + rows] = nn(piece, w_input[1]).astype(bf16)
        v_out[at : at + rows] = (nn(piece, w_input[2]) + b_value[...]).astype(bf16)
        if not cross:
            x_all[at : at + rows] = piece
        at += rows
    if cross:
        resid = prev_norm[...] * prev_gain[...] + prev_shift[...]
        xq = resid.astype(bf16)
    else:
        xq = x_all[0:own_rows]
        resid = xq.astype(f32)
    factor = 1.0 / math.sqrt(head_size)
    q = (nn(xq, w_input[0]) + b_query[...]).astype(bf16)
    q_out[...] = (q.astype(f32) * factor).astype(bf16)
    bias = jnp.where(seg_query[...] == seg_key[...], 0.0, negative)
    masks = head_masks(1, (own_rows, LANES), head_size)
    lse_all = jnp.zeros((own_rows, LANES), f32)
    lane = lax.broadcasted_iota(jnp.int32, (own_rows, LANES), 1)
    for pair in range(width // LANES):
        cols = slice(pair * LANES, (pair + 1) * LANES)
        q_pair, k_pair, v_pair = q_out[:, cols], k_out[:, cols], v_out[:, cols]
        merged = None
        for number, mask in enumerate(masks):
            q_head = jnp.where(mask, q_pair, jnp.zeros_like(q_pair))
            scores = nt(q_head, k_pair) + bias
            peak = jnp.max(scores, axis=1, keepdims=True)
            weights = jnp.exp(scores - peak)
            total = jnp.sum(weights, axis=1, keepdims=True)
            out = nn(weights.astype(bf16), v_pair) * (1.0 / total)
            merged = out if merged is None else jnp.where(mask, out, merged)
            head = pair * len(masks) + number
            lse_all = jnp.where(lane == head, peak + jnp.log(total), lse_all)
        att_out[:, cols] = merged
    lse_out[...] = lse_all
    branch = nn(att_out[...].astype(bf16), w_out[...]) + b_out[...]
    normed, rstd = norm_forward(resid + branch)
    norm_out[...] = normed
    rstd_out[...] = rstd


def ffn_forward_kernel(*refs):
    (norm_in, gain_in, shift_in, w_up, b_up, w_down, b_down, gain, shift) = refs[:9]
    act_out, slope_out, norm_out, rstd_out, low_out = refs[9:]
    width = norm_in.shape[1]
    values = norm_in[...] * gain_in[...] + shift_in[...]
    low = values.astype(bf16)
    total = values + b_down[...]
    for at in range(0, w_up.shape[1], width):
        cols = slice(at, at + width)
        act, slope = gelu_pair(nn(low, w_up[:, cols]) + b_up[:, cols])
        act_low = act.astype(bf16)
        act_out[:, cols] = act_low
        slope_out[:, cols] = slope.astype(bf16)
        total = total + nn(act_low, w_down[cols, :])
    normed, rstd = norm_forward(total)
    norm_out[...] = normed
    rstd_out[...] = rstd
    low_out[...] = (normed * gain[...] + shift[...]).astype(bf16)


def ffn_backward_kernel(part_count, blocks, table, *refs):
    parts = refs[:part_count]
    (norm_two, rstd_two, gain_two, norm_in, gain_in, shift_in) = refs[part_count : part_count + 6]
    act, slope, w_up, w_down, d_out, keep, send, vec = refs[part_count + 6 :]
    own_rows, width = norm_in.shape
    layout = Layout(table, keep, send, blocks)
    dy = parts[0][...].astype(f32)
    for part in parts[1:]:
        dy = dy + part[0:own_rows].astype(f32)
    dr, d_gain, d_shift = norm_backward(dy, norm_two[...], rstd_two[...], gain_two[...])
    d_ffn = dr.astype(bf16)
    vec[0:1] = d_gain
    vec[1:2] = d_shift
    vec[2:3] = column_sum(d_ffn.astype(f32))
    low = (norm_in[...] * gain_in[...] + shift_in[...]).astype(bf16)
    total = dr
    per_blk = w_down.shape[0] // blocks
    chunk = per_blk // MATS
    for number in range(MATS):
        at = number * width
        cols = slice(at, at + width)
        d_act = nt(d_ffn, w_down[cols, :])
        d_pre = (d_act * slope[:, cols].astype(f32)).astype(bf16)
        vec[3 + number : 4 + number] = column_sum(d_pre.astype(f32))
        total = total + nt(d_pre, w_up[:, cols])
        layout.put(tn(low, d_pre), number, 0)
        down = tn(act[:, cols], d_ffn)
        for row in range(0, width, chunk):
            block, mat = (at + row) // per_blk, (at + row) % per_blk // chunk
            layout.put(down[row : row + chunk], mat, 1, block, 1)
    vec[7:8] = jnp.zeros_like(vec[7:8])
    d_out[...] = total


def attn_backward_kernel(cross, part_count, blocks, table, *refs):
    refs = list(refs)
    take = lambda: refs.pop(0)
    parts = [take() for _ in range(part_count)]
    normed, rstd, gain = take(), take(), take()
    att, lse, q8, k, v = [take() for _ in range(5)]
    if cross:
        prev_norm, prev_gain, prev_shift = take(), take(), take()
    mem_count = take()
    xk_parts = [take() for _ in range(mem_count)]
    w_input, w_out, seg_query, seg_key = [take() for _ in range(4)]
    d_own = take()
    d_key_own = take() if cross else None
    d_mid, d_far, keep, send, vec, dk_buf, dv_buf, dq_buf = [take() for _ in range(8)]
    own_rows, width = normed.shape
    keys = k.shape[0]
    head_size = width // H
    factor = 1.0 / math.sqrt(head_size)
    layout = Layout(table, keep, send, blocks)
    dy = parts[0][...].astype(f32)
    for part in parts[1:]:
        dy = dy + part[0:own_rows].astype(f32)
    dr, d_gain, d_shift = norm_backward(dy, normed[...], rstd[...], gain[...])
    d_branch = dr.astype(bf16)
    vec[0:1] = d_gain
    vec[1:2] = d_shift
    vec[2:3] = column_sum(d_branch.astype(f32))
    att_rows = att[...]
    layout.put(tn(att_rows.astype(bf16), d_branch), 3, 0)
    do_turned = nt(w_out[...], d_branch).astype(bf16)
    delta = jnp.sum(
        (do_turned.astype(f32) * att_rows.T).reshape(H, head_size, own_rows), axis=1
    )
    lse_turned = lse[...].T
    q_turned = turned(q8[...]).astype(bf16)
    bias = jnp.where(seg_key[...] == seg_query[...], 0.0, negative)
    masks = head_masks(0, (LANES, own_rows), head_size)
    for pair in range(width // LANES):
        cols = slice(pair * LANES, (pair + 1) * LANES)
        k_pair, v_pair = k[:, cols], v[:, cols]
        k_turned = turned(k_pair).astype(bf16)
        q_pair, do_pair = q_turned[cols], do_turned[cols]
        dk_pair, dv_pair = None, None
        for number, mask in enumerate(masks):
            head = pair * len(masks) + number
            zero = jnp.zeros_like(q_pair)
            q_head = jnp.where(mask, q_pair, zero)
            do_head = jnp.where(mask, do_pair, zero)
            probs = jnp.exp(nn(k_pair, q_head) + bias - lse_turned[head : head + 1])
            d_prob = nn(v_pair, do_head)
            d_score = (probs * (d_prob - delta[head : head + 1])).astype(bf16)
            dv_term = nt(probs.astype(bf16), do_head)
            dk_term = nt(d_score, q_head)
            dv_pair = dv_term if dv_pair is None else dv_pair + dv_term
            dk_pair = dk_term if dk_pair is None else dk_pair + dk_term
            rows = slice(head * head_size, (head + 1) * head_size)
            dq_buf[rows] = nn(k_turned[number * head_size : (number + 1) * head_size], d_score)
        dk_buf[:, cols] = dk_pair.astype(bf16)
        dv_buf[:, cols] = dv_pair.astype(bf16)
    dq = (dq_buf[...].T * factor).astype(bf16)
    if cross:
        xq = (prev_norm[...] * prev_gain[...] + prev_shift[...]).astype(bf16)
    else:
        xq = xk_parts[0][0:own_rows]
    d_query_in = nt(dq, w_input[0])
    dk, dv = dk_buf[...], dv_buf[...]
    d_key_in = nt(dk, w_input[1]) + nt(dv, w_input[2])
    if cross:
        d_own[...] = dr + d_query_in
        d_key_own[...] = d_key_in[0:own_rows]
    else:
        d_own[...] = dr + d_query_in + d_key_in[0:own_rows]
    d_mid[...] = d_key_in[own_rows : keys // 2]
    d_far[...] = d_key_in[keys // 2 :].astype(bf16)
    layout.put(tn(xq, dq), 0, 0)
    grad_key, grad_value = None, None
    at = 0
    for part in xk_parts:
        rows = part.shape[0]
        piece = part[...]
        key_term, value_term = tn(piece, dk[at : at + rows]), tn(piece, dv[at : at + rows])
        grad_key = key_term if grad_key is None else grad_key + key_term
        grad_value = value_term if grad_value is None else grad_value + value_term
        at += rows
    layout.put(grad_key, 1, 0)
    layout.put(grad_value, 2, 0)
    vec[3:4] = column_sum(dq.astype(f32))
    vec[4:5] = column_sum(dv.astype(f32))
    vec[5:8] = jnp.zeros_like(vec[5:8])


def sum_split_kernel(count, pieces, *refs):
    inputs, outputs = refs[:count], refs[count:]
    rows = inputs[0].shape[0] // pieces
    for number, out in enumerate(outputs):
        place = slice(number * rows, (number + 1) * rows)
        total = inputs[0][place].astype(f32)
        for ref in inputs[1:]:
            total = total + ref[place].astype(f32)
        out[...] = total.astype(out.dtype).reshape(out.shape)


def unpack_kernel(kinds, table, *refs):
    mats, refs = refs[:MATS], list(refs[MATS:])
    scratch = refs.pop()
    for rel in range(MATS):
        scratch[lax.bitwise_xor(table[0], rel)] = mats[rel][...].astype(f32)
    width = mats[0].shape[2]
    rows = mats[0].shape[1]
    for group, kind in enumerate(kinds):
        if kind == "attn":
            w_input, w_out = refs.pop(0), refs.pop(0)
            for mat in range(MATS - 1):
                w_input[mat] = scratch[mat, group]
            w_out[...] = scratch[MATS - 1, group]
        elif kind == "up":
            out = refs.pop(0)
            for mat in range(MATS):
                out[:, mat * width : (mat + 1) * width] = scratch[mat, group]
        else:
            out = refs.pop(0)
            for mat in range(MATS):
                out[mat * rows : (mat + 1) * rows] = scratch[mat, group]


def call(kernel, outs, args, scalars=0, scratch=(), name=None):
    vmem = pl.BlockSpec(memory_space=pltpu.VMEM)
    smem = pl.BlockSpec(memory_space=pltpu.SMEM)
    return pl.pallas_call(
        kernel,
        out_shape=tuple(jax.ShapeDtypeStruct(shape, kind) for shape, kind in outs),
        in_specs=[smem] * scalars + [vmem] * (len(args) - scalars),
        out_specs=tuple(vmem for _ in outs),
        scratch_shapes=list(scratch),
        compiler_params=pltpu.CompilerParams(vmem_limit_bytes=VMEM_BYTES),
        name=name,
    )(*args)


def on_device(
    source,
    target,
    src_lengths,
    tgt_lengths,
    pairing,
    enc_w_input,
    enc_b_query,
    enc_b_value,
    enc_w_out,
    enc_b_out,
    enc_gains,
    enc_shifts,
    enc_w_up,
    enc_b_up,
    enc_w_down,
    enc_b_down,
    dec_w_input,
    dec_b_query,
    dec_b_value,
    dec_w_out,
    dec_b_out,
    cross_w_input,
    cross_b_query,
    cross_b_value,
    cross_w_out,
    cross_b_out,
    dec_gains,
    dec_shifts,
    dec_w_up,
    dec_b_up,
    dec_w_down,
    dec_b_down,
    cotangent,
):
    streams, tok, width = source.shape
    n_batch, n_blk = lax.axis_size("batch"), lax.axis_size("blk")
    half = n_blk // 2
    mids = n_blk // 4
    own_rows = 2 * tok
    total_rows = n_blk * tok
    near_rows = total_rows // 2
    chunk_rows = width // n_blk
    ff = enc_w_up.shape[1]
    b, i = lax.axis_index("batch"), lax.axis_index("blk")
    core, y_bit = b & 1, (b >> 1) & 1
    hi, mid, lo = i // half, (i % half) // 2, i & 1

    def move(values, where):
        pairs = []
        for from_b in range(n_batch):
            for from_i in range(n_blk):
                to_b, to_i = where(from_b, from_i)
                pairs.append((from_b * n_blk + from_i, to_b * n_blk + to_i))
        return lax.ppermute(values, ("batch", "blk"), pairs)

    def regroup(values, d_mid, d_lo):
        def where(fb, fi):
            f_hi, f_mid, f_lo, f_core = fi // half, (fi % half) // 2, fi & 1, fb & 1
            return ((fb & ~1) | f_hi, f_core * half + (f_mid ^ d_mid) * 2 + (f_lo ^ d_lo))

        return move(values, where)

    to_core = lambda values: move(values, lambda fb, fi: (fb ^ 1, fi))
    to_mid = lambda values, d_mid: move(values, lambda fb, fi: (fb, fi ^ (2 * d_mid)))
    to_bits = lambda values, d_b, d_i: move(values, lambda fb, fi: (fb ^ d_b, fi ^ d_i))

    def stream_of(values, number):
        return lax.dynamic_index_in_dim(values, number, 0, keepdims=False)

    def gather_stream(values):
        near = [
            regroup(stream_of(values, lo ^ d_lo), d_mid, d_lo)
            for d_mid in range(mids)
            for d_lo in range(2)
        ]
        return near + [to_core(piece) for piece in near]

    src_parts = gather_stream(source)
    tgt_parts = gather_stream(target)
    cot_parts = [regroup(stream_of(cotangent, lo ^ d_lo), 0, d_lo) for d_lo in range(2)]
    cot = jnp.concatenate(cot_parts, axis=0)

    lists = jnp.stack([src_lengths, tgt_lengths, pairing])
    far_lists = to_core(lists)
    mine = lax.dynamic_index_in_dim(jnp.where(hi == core, lists, far_lists), lo, 1, keepdims=False)
    sentences = mine.shape[1]
    numbers = jnp.arange(sentences, dtype=jnp.int32)
    ends = jnp.sum(
        jnp.where(numbers[None, :, None] <= numbers[None, None, :], mine[:2, :, None], 0),
        axis=1,
        dtype=jnp.int32,
    )
    blocks = jnp.stack(
        [
            (core ^ d_core) * half + (mid ^ d_mid) * 2 + (lo ^ d_lo)
            for d_core in range(2)
            for d_mid in range(mids)
            for d_lo in range(2)
        ]
    ).astype(jnp.int32)
    places = (blocks[:, None] * tok + jnp.arange(tok, dtype=jnp.int32)[None, :]).reshape(-1)
    segs = jnp.sum(
        (ends[:, None, :] <= places[None, :, None]).astype(jnp.int32), axis=2, dtype=jnp.int32
    )
    src_key, tgt_key = segs[0], segs[1]
    src_own, tgt_own = src_key[:own_rows], tgt_key[:own_rows]
    pair_own = jnp.sum(
        jnp.where(tgt_own[:, None] == numbers[None, :], mine[2][None, :], 0),
        axis=1,
        dtype=jnp.int32,
    )
    row = lambda values: values.reshape(1, -1)
    col = lambda values: values.reshape(-1, 1)

    bit_count = n_blk.bit_length() - 1
    order = []
    for number in range(n_blk):
        rel = number ^ i
        order.append(
            sum(((rel >> bit) & 1) << (bit_count - 1 - bit) for bit in range(bit_count))
        )
    table = jnp.stack([2 * core + y_bit] + order).astype(jnp.int32)

    def attn_forward(parts, weights, seg_query, seg_key, prev=None):
        w_input, b_query, b_value, w_out, b_out = weights
        cross = prev is not None
        outs = [] if cross else [((total_rows, width), bf16)]
        outs += [
            ((own_rows, width), bf16),
            ((total_rows, width), bf16),
            ((total_rows, width), bf16),
            ((own_rows, width), f32),
            ((own_rows, LANES), f32),
            ((own_rows, width), f32),
            ((own_rows, 1), f32),
        ]
        args = list(parts) + (list(prev) if cross else [])
        args += [col(seg_query), row(seg_key), w_input, row(b_query), row(b_value), w_out, row(b_out)]
        return call(
            lambda *refs: attn_forward_kernel(cross, len(parts), *refs), outs, args, name="attn_forward"
        )

    def ffn_forward(normed, gain_in, shift_in, weights, gain, shift):
        w_up, b_up, w_down, b_down = weights
        outs = [
            ((own_rows, ff), bf16),
            ((own_rows, ff), bf16),
            ((own_rows, width), f32),
            ((own_rows, 1), f32),
            ((own_rows, width), bf16),
        ]
        args = [normed, row(gain_in), row(shift_in), w_up, row(b_up), w_down, row(b_down), row(gain), row(shift)]
        return call(ffn_forward_kernel, outs, args, name="ffn_forward")

    def packed(groups):
        return ((4, n_blk // 2, groups, chunk_rows, width), bf16)

    def ffn_backward(parts, norm_two, rstd_two, gain_two, norm_in, gain_in, shift_in, act, slope, w_up, w_down):
        outs = [((own_rows, width), f32), packed(2), packed(2), ((8, width), f32)]
        args = [table] + list(parts)
        args += [norm_two, rstd_two, row(gain_two), norm_in, row(gain_in), row(shift_in), act, slope, w_up, w_down]
        return call(
            lambda *refs: ffn_backward_kernel(len(parts), n_blk, *refs),
            outs,
            args,
            scalars=1,
            name="ffn_backward",
        )

    def attn_backward(parts, normed, rstd, gain, att, lse, q8, k, v, xk_parts, w_input, w_out, seg_query, seg_key, prev=None):
        cross = prev is not None
        outs = [((own_rows, width), f32)]
        if cross:
            outs.append(((own_rows, width), f32))
        outs += [
            ((near_rows - own_rows, width), f32),
            ((near_rows, width), bf16),
            packed(1),
            packed(1),
            ((8, width), f32),
        ]
        args = [table] + list(parts) + [normed, rstd, row(gain), att, lse, q8, k, v]
        args += list(prev) if cross else []
        before = len(args)
        args += list(xk_parts) + [w_input, w_out, row(seg_query), col(seg_key)]

        def kernel(*refs):
            refs = list(refs)
            refs.insert(before, len(xk_parts))
            attn_backward_kernel(cross, len(parts), n_blk, *refs)

        return call(
            kernel,
            outs,
            args,
            scalars=1,
            scratch=[
                pltpu.VMEM((total_rows, width), bf16),
                pltpu.VMEM((total_rows, width), bf16),
                pltpu.VMEM((width, own_rows), f32),
            ],
            name="attn_backward",
        )

    def sum_split(inputs, pieces, shape, kind=bf16):
        return call(
            lambda *refs: sum_split_kernel(len(inputs), pieces, *refs),
            [(shape, kind)] * pieces,
            list(inputs),
            name="sum_split",
        )

    def return_home(low_rows):
        got = [regroup(low_rows[d_lo * tok : (d_lo + 1) * tok], 0, d_lo) for d_lo in range(2)]
        flipped = lo == 1
        return jnp.stack([jnp.where(flipped, got[1], got[0]), jnp.where(flipped, got[0], got[1])])

    def spread_keys(d_mid_rows, d_far):
        got = to_core(d_far)
        terms = [got]
        for d_mid in range(1, mids):
            place = slice((d_mid - 1) * own_rows, d_mid * own_rows)
            far_place = slice(d_mid * own_rows, (d_mid + 1) * own_rows)
            low = (d_mid_rows[place] + got[far_place].astype(f32)).astype(bf16)
            terms.append(to_mid(low, d_mid))
        return terms

    def reduce_mats(keep, send):
        groups = keep.shape[2]
        got = to_core(send)
        rest = n_blk // 2
        own, d_i, d_y, d_yi = sum_split(
            [keep.reshape((4 * rest,) + keep.shape[2:]), got.reshape((4 * rest,) + keep.shape[2:])],
            4,
            (rest, groups, chunk_rows, width),
        )
        terms = [own, to_bits(d_i, 0, 1), to_bits(d_y, 2, 0), to_bits(d_yi, 2, 1)]
        bit = 2
        while rest > 1:
            rest //= 2
            own, away = sum_split(terms, 2, (rest, groups, chunk_rows, width))
            terms = [own, to_bits(away, 0, bit)]
            bit *= 2
        (own,) = sum_split(terms, 1, (groups, chunk_rows, width))
        bit = 4
        while bit < n_batch:
            (own,) = sum_split([own[None], to_bits(own, bit, 0)[None]], 1, (groups, chunk_rows, width))
            bit *= 2
        side = to_bits(own, 2, 0)
        return [own, side, to_core(own), to_core(side)]

    enc_attn = (enc_w_input, enc_b_query, enc_b_value, enc_w_out, enc_b_out)
    dec_attn = (dec_w_input, dec_b_query, dec_b_value, dec_w_out, dec_b_out)
    cross_attn = (cross_w_input, cross_b_query, cross_b_value, cross_w_out, cross_b_out)
    enc_ffn = (enc_w_up, enc_b_up, enc_w_down, enc_b_down)
    dec_ffn = (dec_w_up, dec_b_up, dec_w_down, dec_b_down)

    src_all, enc_q, enc_k, enc_v, enc_att, enc_lse, enc_n1, enc_r1 = attn_forward(
        src_parts, enc_attn, src_own, src_key
    )
    enc_act, enc_slope, enc_n2, enc_r2, memory = ffn_forward(
        enc_n1, enc_gains[0], enc_shifts[0], enc_ffn, enc_gains[1], enc_shifts[1]
    )
    mem_near = [memory] + [to_mid(memory, d_mid) for d_mid in range(1, mids)]
    mem_parts = mem_near + [to_core(piece) for piece in mem_near]
    tgt_all, dec_q, dec_k, dec_v, dec_att, dec_lse, dec_n1, dec_r1 = attn_forward(
        tgt_parts, dec_attn, tgt_own, tgt_key
    )
    upper = (dec_n1, row(dec_gains[0]), row(dec_shifts[0]))
    cr_q, cr_k, cr_v, cr_att, cr_lse, dec_n2, dec_r2 = attn_forward(
        mem_parts, cross_attn, pair_own, src_key, upper
    )
    dec_act, dec_slope, dec_n3, dec_r3, dec_low = ffn_forward(
        dec_n2, dec_gains[1], dec_shifts[1], dec_ffn, dec_gains[2], dec_shifts[2]
    )

    d_second, dec_ffn_keep, dec_ffn_send, dec_ffn_vec = ffn_backward(
        [cot], dec_n3, dec_r3, dec_gains[2], dec_n2, dec_gains[1], dec_shifts[1], dec_act, dec_slope, dec_w_up, dec_w_down
    )
    d_upper, d_mem_own, d_mem_mid, d_mem_far, cr_keep, cr_send, cr_vec = attn_backward(
        [d_second], dec_n2, dec_r2, dec_gains[1], cr_att, cr_lse, cr_q, cr_k, cr_v, mem_parts,
        cross_w_input, cross_w_out, pair_own, src_key, upper,
    )
    mem_terms = spread_keys(d_mem_mid, d_mem_far)
    d_tgt_own, d_tgt_mid, d_tgt_far, dec_keep, dec_send, dec_vec = attn_backward(
        [d_upper], dec_n1, dec_r1, dec_gains[0], dec_att, dec_lse, dec_q, dec_k, dec_v, [tgt_all],
        dec_w_input, dec_w_out, tgt_own, tgt_key,
    )
    tgt_terms = spread_keys(d_tgt_mid, d_tgt_far)
    d_first, enc_ffn_keep, enc_ffn_send, enc_ffn_vec = ffn_backward(
        [d_mem_own] + mem_terms, enc_n2, enc_r2, enc_gains[1], enc_n1, enc_gains[0], enc_shifts[0],
        enc_act, enc_slope, enc_w_up, enc_w_down,
    )
    d_src_own, d_src_mid, d_src_far, enc_keep, enc_send, enc_vec = attn_backward(
        [d_first], enc_n1, enc_r1, enc_gains[0], enc_att, enc_lse, enc_q, enc_k, enc_v, [src_all],
        enc_w_input, enc_w_out, src_own, src_key,
    )
    src_terms = spread_keys(d_src_mid, d_src_far)

    def add_terms(own, terms):
        total = own
        for term in terms:
            total = total + term[:own_rows].astype(f32)
        return total.astype(bf16)

    enc_out = return_home(memory)
    dec_out = return_home(dec_low)
    target_grad = return_home(add_terms(d_tgt_own, tgt_terms)).astype(f32)
    source_grad = return_home(add_terms(d_src_own, src_terms)).astype(f32)

    def unpack(kinds, mats):
        outs = []
        for kind in kinds:
            if kind == "attn":
                outs += [((MATS - 1, chunk_rows, width), f32), ((chunk_rows, width), f32)]
            elif kind == "up":
                outs.append(((chunk_rows, MATS * width), f32))
            else:
                outs.append(((MATS * chunk_rows, width), f32))
        return call(
            lambda *refs: unpack_kernel(kinds, *refs),
            outs,
            [table] + list(mats),
            scalars=1,
            scratch=[pltpu.VMEM((MATS,) + mats[0].shape, f32)],
            name="unpack",
        )

    g_dec_up, g_dec_down = unpack(("up", "down"), reduce_mats(dec_ffn_keep, dec_ffn_send))
    g_cr_in, g_cr_out = unpack(("attn",), reduce_mats(cr_keep, cr_send))
    g_dec_in, g_dec_out = unpack(("attn",), reduce_mats(dec_keep, dec_send))
    g_enc_up, g_enc_down = unpack(("up", "down"), reduce_mats(enc_ffn_keep, enc_ffn_send))
    g_enc_in, g_enc_out = unpack(("attn",), reduce_mats(enc_keep, enc_send))

    vecs = jnp.concatenate([dec_ffn_vec, cr_vec, dec_vec, enc_ffn_vec, enc_vec], axis=0)
    bit = 1
    while bit < n_batch:
        vecs = vecs + to_bits(vecs, bit, 0)
        bit *= 2
    bit = 1
    while bit < n_blk:
        vecs = vecs + to_bits(vecs, 0, bit)
        bit *= 2
    v_dec_ffn, v_cr, v_dec, v_enc_ffn, v_enc = [vecs[8 * n : 8 * n + 8] for n in range(5)]

    return (
        enc_out,
        dec_out,
        source_grad,
        target_grad,
        g_enc_in,
        v_enc[3],
        v_enc[4],
        g_enc_out,
        v_enc[2],
        jnp.stack([v_enc[0], v_enc_ffn[0]]),
        jnp.stack([v_enc[1], v_enc_ffn[1]]),
        g_enc_up,
        v_enc_ffn[3:7].reshape(-1),
        g_enc_down,
        v_enc_ffn[2],
        g_dec_in,
        v_dec[3],
        v_dec[4],
        g_dec_out,
        v_dec[2],
        g_cr_in,
        v_cr[3],
        v_cr[4],
        g_cr_out,
        v_cr[2],
        jnp.stack([v_dec[0], v_cr[0], v_dec_ffn[0]]),
        jnp.stack([v_dec[1], v_cr[1], v_dec_ffn[1]]),
        g_dec_up,
        v_dec_ffn[3:7].reshape(-1),
        g_dec_down,
        v_dec_ffn[2],
    )


def solution(mesh):
    rows = P("batch", "blk", None)
    lists = P("batch", None)
    by_row = P("blk", None)
    stacked = P(None, "blk", None)
    whole = P()
    return jax.shard_map(
        on_device,
        mesh=mesh,
        in_specs=(rows, rows, lists, lists, lists) + (whole,) * 27 + (rows,),
        out_specs=(rows, rows, rows, rows)
        + (stacked, whole, whole, by_row, whole, whole, whole, by_row, whole, by_row, whole)
        + (stacked, whole, whole, by_row, whole)
        + (stacked, whole, whole, by_row, whole, whole, whole, by_row, whole, by_row, whole),
        check_vma=False,
    )
```

```python
import math

import jax
import jax.numpy as jnp
from jax import lax
from jax.experimental import pallas as pl
from jax.experimental.pallas import tpu as pltpu
from jax.sharding import PartitionSpec as P

H = 8
LANES = 128
MATS = 4
negative = -1e30
bf16 = jnp.bfloat16
f32 = jnp.float32
ROW_BYTES = 20 * 1024
MOST_BYTES = 60 * 1024 * 1024


def nn(left, right):
    return lax.dot_general(left, right, (((1,), (0,)), ((), ())), preferred_element_type=f32)


def nt(left, right):
    return lax.dot_general(left, right, (((1,), (1,)), ((), ())), preferred_element_type=f32)


def tn(left, right):
    return lax.dot_general(left, right, (((0,), (0,)), ((), ())), preferred_element_type=f32)


def turned(values):
    return values.astype(f32).T


def norm_forward(rows):
    centred = rows - jnp.mean(rows, axis=-1, keepdims=True)
    spread = jnp.mean(centred * centred, axis=-1, keepdims=True)
    rstd = lax.rsqrt(spread + 1e-05)
    return centred * rstd, rstd


def norm_backward(dy, normed, rstd, gain):
    dn = dy * gain
    dr = (
        dn
        - jnp.mean(dn, axis=-1, keepdims=True)
        - normed * jnp.mean(dn * normed, axis=-1, keepdims=True)
    ) * rstd
    return dr, column_sum(dy * normed), column_sum(dy)


def column_sum(values):
    return jnp.sum(values, axis=0, keepdims=True)


def gelu_pair(values):
    bell = jnp.exp(-0.5 * values * values)
    t = 1.0 / (1.0 + (0.3275911 * math.sqrt(0.5)) * jnp.abs(values))
    poly = 0.5 * 1.061405429
    for number in (-1.453152027, 1.421413741, -0.284496736, 0.254829592):
        poly = poly * t + 0.5 * number
    tail = poly * t * bell
    share = jnp.where(values >= 0, 1.0 - tail, tail)
    return values * share, share + values * bell * (1.0 / math.sqrt(2.0 * math.pi))


class Layout:
    def __init__(self, table, keep, send, blocks, y_step, groups):
        self.table, self.keep, self.send = table, keep, send
        self.blocks, self.y_step, self.groups = blocks, y_step, groups

    def put(self, values, mat, group, block0=0, count=None):
        count = self.blocks if count is None else count
        low = values.astype(bf16)
        rows = low.shape[0] // count
        rel = lax.bitwise_xor(self.table[0], mat)
        y_place = lax.bitwise_and(rel, 1) * self.y_step

        def fill(ref):
            for number in range(count):
                place = (y_place + self.table[1 + block0 + number]) * self.groups + group
                ref[place] = low[number * rows : (number + 1) * rows]

        pl.when(rel < 2)(lambda: fill(self.keep))
        pl.when(rel >= 2)(lambda: fill(self.send))


def head_masks(axis, shape, head_size):
    places = lax.broadcasted_iota(jnp.int32, shape, axis)
    return [places // head_size == number for number in range(LANES // head_size)]


def as_column(row):
    return jnp.broadcast_to(row, (LANES, row.shape[1])).T[:, 0:1]


def segments_kernel(tok, place, lists, far, segs):
    count = lists.shape[2]
    total = segs.shape[1]
    row = lambda number: jnp.where(
        place[0] == 1, lists[number, pl.ds(place[1], 1)], far[number, pl.ds(place[1], 1)]
    ).astype(f32)
    at_row = lax.broadcasted_iota(jnp.int32, (count, count), 0)
    at_col = lax.broadcasted_iota(jnp.int32, (count, count), 1)

    def ends(number):
        return jnp.sum(jnp.where(at_col <= at_row, row(number), 0.0), axis=1, keepdims=True)

    spots = jnp.concatenate(
        [
            lax.broadcasted_iota(jnp.int32, (1, tok), 1) + place[2 + number] * tok
            for number in range(total // tok)
        ],
        axis=1,
    ).astype(f32)
    src = jnp.sum((ends(0) <= spots).astype(f32), axis=0, keepdims=True)
    tgt = jnp.sum((ends(1) <= spots).astype(f32), axis=0, keepdims=True)
    partner = jnp.sum(jnp.where(at_col == at_row, row(2), 0.0), axis=1, keepdims=True)
    numbers = lax.broadcasted_iota(jnp.int32, (count, 1), 0).astype(f32)
    segs[0:1] = src
    segs[1:2] = tgt
    segs[2:3] = jnp.sum(jnp.where(numbers == tgt, partner, 0.0), axis=0, keepdims=True)
    segs[3:8] = jnp.zeros((5, total), f32)


def call_kernel(kernel, outs, args, scratch, name, after, passed, vmem_bytes):
    spaces = {"s": pltpu.SMEM, "v": pltpu.VMEM}
    before = len(args) + len(after)

    def body(*refs):
        made = refs[before + len(passed) :]
        kernel(*refs[: len(args)], *made[: len(outs)], *made[len(outs) + len(passed) :])

    any_space = pl.BlockSpec(memory_space=pl.ANY)
    shapes = [jax.ShapeDtypeStruct(shape, kind) for shape, kind in outs]
    shapes += [jax.ShapeDtypeStruct(array.shape, array.dtype) for array in passed]
    return pl.pallas_call(
        body,
        out_shape=tuple(shapes),
        in_specs=[pl.BlockSpec(memory_space=spaces[mode]) for mode, _ in args]
        + [any_space] * (len(after) + len(passed)),
        out_specs=tuple(
            [pl.BlockSpec(memory_space=pltpu.VMEM)] * len(outs) + [any_space] * len(passed)
        ),
        scratch_shapes=list(scratch),
        input_output_aliases={before + at: len(outs) + at for at in range(len(passed))},
        compiler_params=pltpu.CompilerParams(vmem_limit_bytes=vmem_bytes),
        name=name,
    )(*[array for _, array in args], *after, *passed)


def keys_values(parts, w_input, b_value, k_out, v_out):
    at = 0
    for part in parts:
        rows = part.shape[0]
        piece = part[...]
        k_out[at : at + rows] = nn(piece, w_input[1]).astype(bf16)
        v_out[at : at + rows] = (nn(piece, w_input[2]) + b_value[...]).astype(bf16)
        at += rows


def attn_forward(parts, query, segs, seg_rows, weights, q_out, k_out, v_out, att_out, lse_out):
    w_input, b_query, b_value, w_out, b_out = weights
    own_rows, width = q_out.shape
    head_size = width // H
    keys_values(parts, w_input, b_value, k_out, v_out)
    xq = parts[0][0:own_rows] if query is None else query
    factor = 1.0 / math.sqrt(head_size)
    q = (nn(xq, w_input[0]) + b_query[...]).astype(bf16)
    q_out[...] = (q.astype(f32) * factor).astype(bf16)
    seg_query = as_column(segs[seg_rows[0] : seg_rows[0] + 1, 0:own_rows])
    bias = jnp.where(seg_query == segs[seg_rows[1] : seg_rows[1] + 1], 0.0, negative)
    masks = head_masks(1, (own_rows, LANES), head_size)
    lse_all = jnp.zeros((own_rows, LANES), f32)
    lane = lax.broadcasted_iota(jnp.int32, (own_rows, LANES), 1)
    for pair in range(width // LANES):
        cols = slice(pair * LANES, (pair + 1) * LANES)
        q_pair, k_pair, v_pair = q_out[:, cols], k_out[:, cols], v_out[:, cols]
        merged = None
        for number, mask in enumerate(masks):
            q_head = jnp.where(mask, q_pair, jnp.zeros_like(q_pair))
            scores = nt(q_head, k_pair) + bias
            peak = jnp.max(scores, axis=1, keepdims=True)
            weights = jnp.exp(scores - peak)
            total = jnp.sum(weights, axis=1, keepdims=True)
            out = nn(weights.astype(bf16), v_pair) * (1.0 / total)
            merged = out if merged is None else jnp.where(mask, out, merged)
            head = pair * len(masks) + number
            lse_all = jnp.where(lane == head, peak + jnp.log(total), lse_all)
        att_out[:, cols] = merged
    lse_out[...] = lse_all.T[0:H]
    branch = nn(att_out[...].astype(bf16), w_out[...]) + b_out[...]
    return branch + xq.astype(f32) if query is None else branch


def ffn_forward(values, weights, act_out, slope_out):
    w_up, b_up, w_down, b_down = weights
    width = values.shape[1]
    low = values.astype(bf16)
    total = values + b_down[...]
    for at in range(0, w_up.shape[1], width):
        cols = slice(at, at + width)
        act, slope = gelu_pair(nn(low, w_up[:, cols]) + b_up[:, cols])
        act_low = act.astype(bf16)
        act_out[:, cols] = act_low
        slope_out[:, cols] = slope.astype(bf16)
        total = total + nn(act_low, w_down[cols, :])
    return total


def ffn_backward(dr, low, act, slope, w_up, w_down, up, down, blocks, sums):
    width = dr.shape[1]
    d_ffn = dr.astype(bf16)
    sums.append(column_sum(d_ffn.astype(f32)))
    total = dr
    per_blk = w_down.shape[0] // blocks
    chunk = per_blk // MATS
    for number in range(MATS):
        at = number * width
        cols = slice(at, at + width)
        d_act = nt(d_ffn, w_down[cols, :])
        d_pre = (d_act * slope[:, cols].astype(f32)).astype(bf16)
        sums.append(column_sum(d_pre.astype(f32)))
        total = total + nt(d_pre, w_up[:, cols])
        up.put(tn(low, d_pre), number, 0)
        rows = tn(act[:, cols], d_ffn)
        for row in range(0, width, chunk):
            block, mat = (at + row) // per_blk, (at + row) % per_blk // chunk
            down.put(rows[row : row + chunk], mat, down.groups - 1, block, 1)
    return total


def attn_backward(dr, xq, xk_parts, saved, segs, seg_rows, w_input, w_out, layout, group, buffers, sums):
    att, lse, q8, k, v = saved
    dk_buf, dv_buf, dq_buf = buffers
    own_rows, width = dr.shape
    head_size = width // H
    factor = 1.0 / math.sqrt(head_size)
    d_branch = dr.astype(bf16)
    att_rows = att[...]
    layout.put(tn(att_rows.astype(bf16), d_branch), 3, group)
    do_turned = nt(w_out[...], d_branch).astype(bf16)
    delta = jnp.sum((do_turned.astype(f32) * att_rows.T).reshape(H, head_size, own_rows), axis=1)
    lse_turned = lse[...]
    q_turned = turned(q8[...]).astype(bf16)
    seg_key = as_column(segs[seg_rows[1] : seg_rows[1] + 1])
    bias = jnp.where(seg_key == segs[seg_rows[0] : seg_rows[0] + 1, 0:own_rows], 0.0, negative)
    masks = head_masks(0, (LANES, own_rows), head_size)
    for pair in range(width // LANES):
        cols = slice(pair * LANES, (pair + 1) * LANES)
        k_pair, v_pair = k[:, cols], v[:, cols]
        k_turned = turned(k_pair).astype(bf16)
        q_pair, do_pair = q_turned[cols], do_turned[cols]
        dk_pair, dv_pair = None, None
        for number, mask in enumerate(masks):
            head = pair * len(masks) + number
            zero = jnp.zeros_like(q_pair)
            q_head = jnp.where(mask, q_pair, zero)
            do_head = jnp.where(mask, do_pair, zero)
            probs = jnp.exp(nn(k_pair, q_head) + bias - lse_turned[head : head + 1])
            d_prob = nn(v_pair, do_head)
            d_score = (probs * (d_prob - delta[head : head + 1])).astype(bf16)
            dv_term = nt(probs.astype(bf16), do_head)
            dk_term = nt(d_score, q_head)
            dv_pair = dv_term if dv_pair is None else dv_pair + dv_term
            dk_pair = dk_term if dk_pair is None else dk_pair + dk_term
            rows = slice(head * head_size, (head + 1) * head_size)
            dq_buf[rows] = nn(k_turned[number * head_size : (number + 1) * head_size], d_score)
        dk_buf[:, cols] = dk_pair.astype(bf16)
        dv_buf[:, cols] = dv_pair.astype(bf16)
    dq = (dq_buf[...].T * factor).astype(bf16)
    layout.put(tn(xq, dq), 0, group)
    dk, dv = dk_buf[...], dv_buf[...]
    grad_key, grad_value = None, None
    at = 0
    for part in xk_parts:
        rows = part.shape[0]
        piece = part[...]
        key_term, value_term = tn(piece, dk[at : at + rows]), tn(piece, dv[at : at + rows])
        grad_key = key_term if grad_key is None else grad_key + key_term
        grad_value = value_term if grad_value is None else grad_value + value_term
        at += rows
    layout.put(grad_key, 1, group)
    layout.put(grad_value, 2, group)
    sums += [
        column_sum(d_branch.astype(f32)),
        column_sum(dq.astype(f32)),
        column_sum(dv.astype(f32)),
        jnp.zeros((3, width), f32),
    ]
    return nt(dq, w_input[0]), nt(dk, w_input[1]) + nt(dv, w_input[2])


def add_up(parts, own_rows):
    total = parts[0][0:own_rows].astype(f32)
    for part in parts[1:]:
        total = total + part[0:own_rows].astype(f32)
    return total


def pack_kernel(*refs):
    at = 0
    for ref in refs[:-1]:
        refs[-1][at : at + ref.shape[0]] = ref[...]
        at += ref.shape[0]


def self_attn(parts, segs, seg_rows, weights, q, att, lse, norm_one, rstd_one, buffers):
    k, v = buffers
    rows = attn_forward(parts, None, segs, seg_rows, weights, q, k, v, att, lse)
    normed, rstd = norm_forward(rows)
    norm_one[...] = normed
    rstd_one[...] = rstd
    return normed


def enc_forward_kernel(seg_rows, *refs):
    near, far, segs, w_input, b_query, b_value, w_out, b_out = refs[:8]
    gains, shifts, w_up, b_up, w_down, b_down = refs[8:14]
    q, att, lse, norm_one, rstd_one, act, slope, norm_two, rstd_two, low, k, v = refs[14:]
    weights = (w_input, b_query, b_value, w_out, b_out)
    normed = self_attn(
        [near, far], segs, seg_rows, weights, q, att, lse, norm_one, rstd_one, (k, v)
    )
    values = normed * gains[0:1] + shifts[0:1]
    normed, rstd = norm_forward(ffn_forward(values, (w_up, b_up, w_down, b_down), act, slope))
    norm_two[...] = normed
    rstd_two[...] = rstd
    low[...] = (normed * gains[1:2] + shifts[1:2]).astype(bf16)


def dec_forward_kernel(seg_rows, *refs):
    near, far, segs, w_input, b_query, b_value, w_out, b_out = refs[:8]
    q, att, lse, norm_one, rstd_one, k, v = refs[8:]
    weights = (w_input, b_query, b_value, w_out, b_out)
    self_attn([near, far], segs, seg_rows, weights, q, att, lse, norm_one, rstd_one, (k, v))


def cross_forward_kernel(part_count, cot_count, seg_rows, blocks, y_step, table, *refs):
    refs = list(refs)
    parts, refs = refs[:part_count], refs[part_count:]
    cots, refs = refs[:cot_count], refs[cot_count:]
    prev_norm, segs, w_input, b_query, b_value, w_out, b_out, gains, shifts = refs[:9]
    w_up, b_up, w_down, b_down = refs[9:13]
    q, k, v, att, lse, norm_two_out, rstd_two_out, d_second = refs[13:21]
    homes = refs[21:23]
    keep, send, vecs, act, slope = refs[23:]
    own_rows = prev_norm.shape[0]
    upper = prev_norm[...] * gains[0:1] + shifts[0:1]
    weights = (w_input, b_query, b_value, w_out, b_out)
    branch = attn_forward(
        parts, upper.astype(bf16), segs, seg_rows, weights, q, k, v, att, lse
    )
    norm_two, rstd_two = norm_forward(upper + branch)
    norm_two_out[...] = norm_two
    rstd_two_out[...] = rstd_two
    crossed = norm_two * gains[1:2] + shifts[1:2]
    norm_three, rstd_three = norm_forward(
        ffn_forward(crossed, (w_up, b_up, w_down, b_down), act, slope)
    )
    low = (norm_three * gains[2:3] + shifts[2:3]).astype(bf16)
    tok = own_rows // 2
    memory = parts[0][...]
    for number, home in enumerate(homes):
        home[0] = memory[number * tok : (number + 1) * tok]
        home[1] = low[number * tok : (number + 1) * tok]
    dy = jnp.concatenate([cot[...] for cot in cots], axis=0).astype(f32)
    sums = []
    dr, d_gain, d_shift = norm_backward(dy, norm_three, rstd_three, gains[2:3])
    sums += [d_gain, d_shift]
    layout = Layout(table, keep, send, blocks, y_step, 2)
    d_second[...] = ffn_backward(
        dr, crossed.astype(bf16), act, slope, w_up, w_down, layout, layout, blocks, sums
    )
    sums.append(jnp.zeros_like(d_gain))
    vecs[...] = jnp.concatenate(sums, axis=0)


def cross_backward_kernel(part_count, has_mid, seg_rows, blocks, y_step, table, *refs):
    refs = list(refs)
    parts, refs = refs[:part_count], refs[part_count:]
    d_in, norm_two, rstd_two, prev_norm, gains, shifts = refs[:6]
    att, w_out, lse, q, k, v, segs, w_input = refs[6:14]
    refs = refs[14:]
    d_upper, d_own = refs[:2]
    refs = refs[2:]
    d_mid = refs.pop(0) if has_mid else None
    d_far, keep, send, vecs = refs[:4]
    buffers = refs[4:]
    own_rows = prev_norm.shape[0]
    sums = []
    dr, d_gain, d_shift = norm_backward(d_in[...], norm_two[...], rstd_two[...], gains[1:2])
    sums += [d_gain, d_shift]
    xq = (prev_norm[...] * gains[0:1] + shifts[0:1]).astype(bf16)
    layout = Layout(table, keep, send, blocks, y_step, 1)
    d_query, d_key = attn_backward(
        dr, xq, parts, (att, lse, q, k, v), segs, seg_rows, w_input, w_out, layout, 0, buffers, sums
    )
    keys = d_key.shape[0]
    d_upper[...] = dr + d_query
    d_own[...] = d_key[0:own_rows]
    if has_mid:
        d_mid[...] = d_key[own_rows : keys // 2].astype(bf16)
    d_far[...] = d_key[keys // 2 :].astype(bf16)
    vecs[...] = jnp.concatenate(sums, axis=0)


def ffn_backward_kernel(part_count, blocks, y_step, table, *refs):
    parts, refs = refs[:part_count], refs[part_count:]
    norm_two, rstd_two, norm_one, gains, shifts, slope, w_down, act, w_up = refs[:9]
    d_out, keep, send, vecs = refs[9:]
    sums = []
    dy = add_up(parts, norm_one.shape[0])
    dr, d_gain, d_shift = norm_backward(dy, norm_two[...], rstd_two[...], gains[1:2])
    sums += [d_gain, d_shift]
    low = (norm_one[...] * gains[0:1] + shifts[0:1]).astype(bf16)
    layout = Layout(table, keep, send, blocks, y_step, 2)
    d_out[...] = ffn_backward(dr, low, act, slope, w_up, w_down, layout, layout, blocks, sums)
    sums.append(jnp.zeros_like(d_gain))
    vecs[...] = jnp.concatenate(sums, axis=0)


def self_backward_kernel(has_mid, all_seg_rows, blocks, y_step, table, segs, vec_one, vec_two, vec_three, *refs):
    refs = list(refs)
    layers, refs = [refs[:12], refs[12:24]], refs[24:]
    own_outs, refs = refs[:2], refs[2:]
    mid = refs.pop(0) if has_mid else None
    far_out, keep, send, k, v = refs[:5]
    buffers = refs[5:]
    all_sums = [vec_one[...], vec_two[...], vec_three[...]]
    for number, (layer, seg_rows) in enumerate(zip(layers, all_seg_rows)):
        d_in, norm_one, rstd_one, gains, att, w_out, lse, q, near, far, w_input, b_value = layer
        own_rows, width = norm_one.shape
        layout = Layout(table, keep, send, blocks, y_step, 2)
        sums = []
        dr, d_gain, d_shift = norm_backward(d_in[...], norm_one[...], rstd_one[...], gains[0:1])
        sums += [d_gain, d_shift]
        keys_values([near, far], w_input, b_value, k, v)
        xq = near[0:own_rows]
        d_query, d_key = attn_backward(
            dr, xq, [near, far], (att, lse, q, k, v), segs, seg_rows, w_input, w_out, layout,
            number, buffers, sums,
        )
        keys = d_key.shape[0]
        own_outs[number][...] = dr + d_query + d_key[0:own_rows]
        if has_mid:
            mid[number] = d_key[own_rows : keys // 2].astype(bf16)
        far_out[number] = d_key[keys // 2 :].astype(bf16)
        all_sums += sums
    more = keep.shape[0] - 4 * blocks
    rows = keep.shape[1]
    pad = more * rows - sum(piece.shape[0] for piece in all_sums)
    if pad:
        all_sums.append(jnp.zeros((pad, width), f32))
    all_sums = jnp.concatenate(all_sums, axis=0).astype(bf16)
    for number in range(more):
        keep[4 * blocks + number] = all_sums[number * rows : (number + 1) * rows]
        send[4 * blocks + number] = all_sums[number * rows : (number + 1) * rows]


def middle_kernel(own_rows, d_mid, got, *outs):
    for number, out in enumerate(outs):
        mine = slice(number * own_rows, (number + 1) * own_rows)
        far = slice((number + 1) * own_rows, (number + 2) * own_rows)
        for at in range(out.shape[0]):
            out[at] = (d_mid[at, mine].astype(f32) + got[at, far].astype(f32)).astype(bf16)


def homes_kernel(own_count, *refs):
    owns, terms, homes = refs[:own_count], refs[own_count:-2], refs[-2:]
    tok = homes[0].shape[1]
    for number, own in enumerate(owns):
        total = own[...]
        for term in terms:
            total = total + term[number, 0 : 2 * tok].astype(f32)
        total = total.astype(bf16)
        for d_lo, home in enumerate(homes):
            home[number] = total[d_lo * tok : (d_lo + 1) * tok]


def combine_kernel(count, plan, *refs):
    inputs, outputs = refs[:count], refs[count:]
    for out, segments in zip(outputs, plan):
        at = 0
        for chunks, terms in segments:
            total = None
            for number, first in terms:
                term = inputs[number][first : first + chunks].astype(f32)
                total = term if total is None else total + term
            out[at : at + chunks] = total.astype(out.dtype)
            at += chunks


def place_kernel(table, got_one, got_two, *outs):
    for number, out in enumerate(outs):
        out[table[0]] = got_one[number].astype(out.dtype)
        out[lax.bitwise_xor(table[0], 1)] = got_two[number].astype(out.dtype)


def unpack_kernel(kinds, vec_rows, table, *refs):
    refs = list(refs)
    mats = refs[:MATS]
    refs = refs[MATS:]
    vec = refs.pop(0) if vec_rows else None
    scratch = refs.pop()
    for rel in range(MATS):
        scratch[lax.bitwise_xor(table[0], rel)] = mats[rel][...].astype(f32)
    width = mats[0].shape[2]
    rows = mats[0].shape[1]
    for group, kind in enumerate(kinds):
        if kind == "attn":
            w_input, w_out = refs.pop(0), refs.pop(0)
            for mat in range(MATS - 1):
                w_input[mat] = scratch[mat, group]
            w_out[...] = scratch[MATS - 1, group]
        elif kind == "up":
            out = refs.pop(0)
            for mat in range(MATS):
                out[:, mat * width : (mat + 1) * width] = scratch[mat, group]
        else:
            out = refs.pop(0)
            for mat in range(MATS):
                out[mat * rows : (mat + 1) * rows] = scratch[mat, group]
    if vec_rows:
        sums = jnp.concatenate([vec[number] for number in range(vec.shape[0])], axis=0).astype(f32)
        for out, numbers in zip(refs, vec_rows):
            for at, number in enumerate(numbers):
                if out.shape[0] == 1:
                    out[:, at * width : (at + 1) * width] = sums[number : number + 1]
                else:
                    out[at : at + 1] = sums[number : number + 1]


def on_device(
    source,
    target,
    src_lengths,
    tgt_lengths,
    pairing,
    enc_w_input,
    enc_b_query,
    enc_b_value,
    enc_w_out,
    enc_b_out,
    enc_gains,
    enc_shifts,
    enc_w_up,
    enc_b_up,
    enc_w_down,
    enc_b_down,
    dec_w_input,
    dec_b_query,
    dec_b_value,
    dec_w_out,
    dec_b_out,
    cross_w_input,
    cross_b_query,
    cross_b_value,
    cross_w_out,
    cross_b_out,
    dec_gains,
    dec_shifts,
    dec_w_up,
    dec_b_up,
    dec_w_down,
    dec_b_down,
    cotangent,
):
    streams, tok, width = source.shape
    n_batch, n_blk = lax.axis_size("batch"), lax.axis_size("blk")
    half = n_blk // 2
    mids = n_blk // 4
    own_rows = 2 * tok
    total_rows = n_blk * tok
    near_rows = total_rows // 2
    chunk_rows = width // n_blk
    ff = enc_w_up.shape[1]
    b, i = lax.axis_index("batch"), lax.axis_index("blk")
    core, y_bit = b & 1, (b >> 1) & 1
    hi, mid, lo = i // half, (i % half) // 2, i & 1

    def move(values, where):
        pairs = []
        for from_b in range(n_batch):
            for from_i in range(n_blk):
                to_b, to_i = where(from_b, from_i)
                pairs.append((from_b * n_blk + from_i, to_b * n_blk + to_i))
        return lax.ppermute(values, ("batch", "blk"), pairs)

    def regroup(values, d_mid, d_lo):
        def where(fb, fi):
            f_hi, f_mid, f_lo, f_core = fi // half, (fi % half) // 2, fi & 1, fb & 1
            return ((fb & ~1) | f_hi, f_core * half + (f_mid ^ d_mid) * 2 + (f_lo ^ d_lo))

        return move(values, where)

    to_bits = lambda values, d_b, d_i: move(values, lambda fb, fi: (fb ^ d_b, fi ^ d_i))
    to_core = lambda values: to_bits(values, 1, 0)
    to_mid = lambda values, d_mid: to_bits(values, 0, 2 * d_mid)

    last = []

    def call(kernel, outs, args, scratch=(), name=None, passed=(), after=()):
        vmem_bytes = min(total_rows * ROW_BYTES, MOST_BYTES)
        held_back = last[-1:] + list(after)
        got = call_kernel(kernel, outs, args, scratch, name, held_back, list(passed), vmem_bytes)
        last.append(min(got[: len(outs)], key=lambda array: array.size))
        return got

    bits = n_blk.bit_length() - 1
    batch_bits = n_batch.bit_length() - 1
    plane_first = ["y"] + list(range(bits))

    def steps(order):
        return {name: 1 << (bits - at) for at, name in enumerate(order)}

    def table_of(order):
        step = steps(order)
        places = [
            sum((((number ^ i) >> bit) & 1) * step[bit] for bit in range(bits))
            for number in range(n_blk)
        ]
        return jnp.stack([2 * core + y_bit] + places).astype(jnp.int32)

    plane_table = table_of(plane_first)
    runs = [
        (core ^ d_core) * half + (mid ^ d_mid) * 2 + (lo ^ d_lo)
        for d_core in range(2)
        for d_mid in range(mids)
        for d_lo in range(2)
    ]
    place_table = jnp.stack([(hi == core).astype(jnp.int32), lo] + runs).astype(jnp.int32)
    lo_table = jnp.stack([lo, lo]).astype(jnp.int32)
    row = lambda values: values.reshape(1, -1)

    def stream_of(values, number):
        return lax.dynamic_index_in_dim(values, number, 0, keepdims=False)

    def near_parts(values):
        return [
            regroup(stream_of(values, lo ^ d_lo), d_mid, d_lo)
            for d_mid in range(mids)
            for d_lo in range(2)
        ]

    held = lambda arrays: [("v", array) for array in arrays]
    packed = lambda chunks: ((chunks, chunk_rows, width), bf16)
    rows_f32 = ((own_rows, width), f32)
    rows_bf16 = ((own_rows, width), bf16)
    one_f32 = ((own_rows, 1), f32)
    lse_shape = ((H, own_rows), f32)
    all_keys = ((total_rows, width), bf16)
    vec_shape = ((8, width), f32)
    has_mid = near_rows > own_rows
    key_buffers = [pltpu.VMEM(*all_keys), pltpu.VMEM(*all_keys)]
    back_buffers = key_buffers + [pltpu.VMEM((width, own_rows), f32)]
    y_step = steps(plane_first)["y"]

    def pack(parts):
        return call(pack_kernel, [((near_rows, width), bf16)], held(parts), name="pack")[0]

    src_parts = near_parts(source)
    tgt_parts = near_parts(target)
    cot_parts = [regroup(stream_of(cotangent, lo ^ d_lo), 0, d_lo) for d_lo in range(2)]
    lists = jnp.stack([src_lengths, tgt_lengths, pairing])
    (segs,) = call(
        lambda *refs: segments_kernel(tok, *refs),
        [((8, total_rows), f32)],
        [("s", place_table)] + held([lists, to_core(lists)]),
        name="segments",
    )
    src_rows, tgt_rows, pair_rows = (0, 0), (1, 1), (2, 0)
    src_near = pack(src_parts)
    src_far = to_core(src_near)

    def spread_keys(d_mid_rows, d_far):
        got = to_core(d_far)
        if not has_mid:
            return [got]
        totals = call(
            lambda *refs: middle_kernel(own_rows, *refs),
            [((got.shape[0], own_rows, width), bf16)] * (mids - 1),
            held([d_mid_rows, got]),
            name="middle",
        )
        return [got] + [to_mid(total, d_mid) for d_mid, total in enumerate(totals, 1)]

    def homeward(homes):
        return [regroup(home, 0, d_lo) for d_lo, home in enumerate(homes)]

    def place_home(got, kinds):
        outs = [((streams, tok, width), kind) for kind in kinds]
        return call(place_kernel, outs, [("s", lo_table)] + held(got), name="place")

    def combine(plan_outs, passed=()):
        arrays, index, plan, outs = [], {}, [], []
        for segments, kind in plan_outs:
            rows = []
            for chunks, terms in segments:
                named = []
                for array, first in terms:
                    if id(array) not in index:
                        index[id(array)] = len(arrays)
                        arrays.append(array)
                    named.append((index[id(array)], first))
                rows.append((chunks, named))
            plan.append(rows)
            outs.append(((sum(chunks for chunks, _ in rows), chunk_rows, width), kind))
        return call(
            lambda *refs: combine_kernel(len(arrays), plan, *refs),
            outs,
            held(arrays),
            name="combine",
            passed=passed,
        )

    def offset(name):
        if name == "y":
            return (2, 0)
        if isinstance(name, tuple):
            return (name[0], 0)
        return (0, 1 << name)

    def exchange(states, dims, passed=()):
        combos = []
        for number in range(1 << len(dims)):
            combos.append(
                tuple(name for at, name in enumerate(dims) if (number >> (len(dims) - 1 - at)) & 1)
            )
        segments = {combo: [] for combo in combos}
        sizes = {combo: 0 for combo in combos}
        found = []
        for left, chunks, terms in states:
            mine = [] if left is None else [name for name in left if name in dims]
            rest = [] if left is None else [name for name in left if name not in dims]
            assert left is None or list(left[: len(mine)]) == mine
            count = chunks << len(rest)
            places = {}
            for combo in combos:
                if left is not None and not all(name in mine for name in combo):
                    continue
                start = 0
                for at, name in enumerate(mine):
                    if name in combo:
                        start += count << (len(mine) - 1 - at)
                segments[combo].append((count, [(array, first + start) for array, first in terms]))
                places[combo] = sizes[combo]
                sizes[combo] += count
            found.append((None if left is None else rest, chunks, places))
        arrays = combine([(segments[combo], bf16) for combo in combos], passed)
        through = list(arrays[len(combos) :])
        got = {combos[0]: arrays[0]}
        for combo, array in zip(combos[1:], arrays[1:]):
            d_b, d_i = 0, 0
            for name in combo:
                d_b, d_i = d_b ^ offset(name)[0], d_i ^ offset(name)[1]
            got[combo] = to_bits(array, d_b, d_i)
        states = [
            (rest, chunks, [(got[combo], at) for combo, at in places.items()])
            for rest, chunks, places in found
        ]
        return states + through

    def attn_args(w_input, b_query, b_value, w_out, b_out):
        return held([w_input, row(b_query), row(b_value), w_out, row(b_out)])

    def ffn_args(w_up, b_up, w_down, b_down):
        return held([w_up, row(b_up), w_down, row(b_down)])

    enc_q, enc_att, enc_lse, enc_n1, enc_r1, enc_act, enc_slope, enc_n2, enc_r2, memory = call(
        lambda *refs: enc_forward_kernel(src_rows, *refs),
        [rows_bf16, rows_f32, lse_shape, rows_f32, one_f32]
        + [((own_rows, ff), bf16), ((own_rows, ff), bf16), rows_f32, one_f32, rows_bf16],
        held([src_near, src_far, segs])
        + attn_args(enc_w_input, enc_b_query, enc_b_value, enc_w_out, enc_b_out)
        + held([enc_gains, enc_shifts])
        + ffn_args(enc_w_up, enc_b_up, enc_w_down, enc_b_down),
        scratch=key_buffers,
        name="enc_forward",
    )
    places = [(d_core, d_mid) for d_core in range(2) for d_mid in range(mids)]
    mem_parts = [memory] + [
        to_bits(memory, d_core, 2 * d_mid) for d_core, d_mid in places[1:]
    ]
    tgt_near = pack(tgt_parts)
    tgt_far = to_core(tgt_near)
    dec_q, dec_att, dec_lse, dec_n1, dec_r1 = call(
        lambda *refs: dec_forward_kernel(tgt_rows, *refs),
        [rows_bf16, rows_f32, lse_shape, rows_f32, one_f32],
        held([tgt_near, tgt_far, segs])
        + attn_args(dec_w_input, dec_b_query, dec_b_value, dec_w_out, dec_b_out),
        scratch=key_buffers,
        name="dec_forward",
    )

    got = call(
        lambda *refs: cross_forward_kernel(
            len(mem_parts), len(cot_parts), pair_rows, n_blk, y_step, *refs
        ),
        [rows_bf16, all_keys, all_keys, rows_f32, lse_shape, rows_f32, one_f32, rows_f32]
        + [((2, tok, width), bf16)] * 2
        + [packed(4 * n_blk)] * 2
        + [vec_shape],
        [("s", plane_table)]
        + held(mem_parts + cot_parts + [dec_n1, segs])
        + attn_args(cross_w_input, cross_b_query, cross_b_value, cross_w_out, cross_b_out)
        + held([dec_gains, dec_shifts])
        + ffn_args(dec_w_up, dec_b_up, dec_w_down, dec_b_down),
        scratch=[pltpu.VMEM((own_rows, ff), bf16), pltpu.VMEM((own_rows, ff), bf16)],
        name="cross_forward",
    )
    cr_q, cr_k, cr_v, cr_att, cr_lse, dec_n2, dec_r2, d_second = got[:8]
    homes = homeward(got[8:10])
    df_keep, df_send, df_vec = got[10:]
    df_got = to_core(df_send)
    mid_shape = [((near_rows - own_rows, width), bf16)] if has_mid else []
    got = list(
        call(
            lambda *refs: cross_backward_kernel(
                len(mem_parts), has_mid, pair_rows, n_blk, y_step, *refs
            ),
            [rows_f32, rows_f32]
            + mid_shape
            + [((near_rows, width), bf16)]
            + [packed(2 * n_blk)] * 2
            + [vec_shape],
            [("s", plane_table)]
            + held(mem_parts)
            + held([d_second, dec_n2, dec_r2, dec_n1, dec_gains, dec_shifts])
            + held([cr_att, cross_w_out, cr_lse, cr_q, cr_k, cr_v, segs, cross_w_input]),
            scratch=back_buffers,
            name="cross_backward",
        )
    )
    d_upper, d_mem_own = got[:2]
    d_mem_mid = got[2][None] if has_mid else None
    d_mem_far, cr_keep, cr_send, cr_vec = got[2 + len(mid_shape) :]
    plane, line = plane_first[:2], plane_first[2:]
    enc_out, dec_out = place_home(homes, (bf16, bf16))
    (df_state,) = exchange([(plane_first, 2, [(df_keep, 0), (df_got, 0)])], plane)
    mem_terms = [term[0] for term in spread_keys(d_mem_mid, d_mem_far[None])]
    cr_got = to_core(cr_send)

    d_first, ef_keep, ef_send, ef_vec = call(
        lambda *refs: ffn_backward_kernel(1 + len(mem_terms), n_blk, y_step, *refs),
        [rows_f32] + [packed(4 * n_blk)] * 2 + [vec_shape],
        [("s", plane_table)]
        + held([d_mem_own] + mem_terms)
        + held([enc_n2, enc_r2, enc_n1, enc_gains, enc_shifts])
        + held([enc_slope, enc_w_down, enc_act, enc_w_up]),
        name="ffn_backward",
    )
    df_state, ef_send = exchange([df_state], line[:1], passed=[ef_send])
    ef_got = to_core(ef_send)
    ef_state, cr_state = exchange(
        [
            (plane_first, 2, [(ef_keep, 0), (ef_got, 0)]),
            (plane_first, 1, [(cr_keep, 0), (cr_got, 0)]),
        ],
        plane,
    )

    vec_chunks = -(-40 // chunk_rows)
    got = list(
        call(
            lambda *refs: self_backward_kernel(
                has_mid, (src_rows, tgt_rows), n_blk, y_step, *refs
            ),
            [rows_f32, rows_f32]
            + [((2,) + shape, kind) for shape, kind in mid_shape]
            + [((2, near_rows, width), bf16)]
            + [packed(4 * n_blk + vec_chunks)] * 2,
            [("s", plane_table)]
            + held([segs, df_vec, cr_vec, ef_vec])
            + held([d_first, enc_n1, enc_r1, enc_gains, enc_att, enc_w_out, enc_lse, enc_q])
            + held([src_near, src_far, enc_w_input, row(enc_b_value)])
            + held([d_upper, dec_n1, dec_r1, dec_gains, dec_att, dec_w_out, dec_lse, dec_q])
            + held([tgt_near, tgt_far, dec_w_input, row(dec_b_value)]),
            scratch=key_buffers + back_buffers,
            name="self_backward",
        )
    )
    d_own_rows = got[:2]
    d_mid_rows = got[2] if has_mid else None
    d_far_rows, sd_keep, sd_send = got[2 + len(mid_shape) :]

    def gather(own):
        side = to_bits(own, 2, 0)
        return [own, side, to_core(own), to_core(side)]

    def batch_rest(states):
        for bit in range(2, batch_bits):
            whole = [(None, n << len(left or []), terms) for left, n, terms in states]
            states = exchange(whole, [(1 << bit,)])
        return states

    def unpack(kinds, mats, vec=None, vec_rows=(), wide=()):
        outs = []
        for kind in kinds:
            if kind == "attn":
                outs += [((MATS - 1, chunk_rows, width), f32), ((chunk_rows, width), f32)]
            elif kind == "up":
                outs.append(((chunk_rows, MATS * width), f32))
            else:
                outs.append(((MATS * chunk_rows, width), f32))
        for number, numbers in enumerate(vec_rows):
            shape = (len(numbers), width) if number in wide else (1, len(numbers) * width)
            outs.append((shape, f32))
        return call(
            lambda *refs: unpack_kernel(kinds, vec_rows, *refs),
            outs,
            [("s", plane_table)] + held(list(mats) + ([vec] if vec_rows else [])),
            scratch=[pltpu.VMEM((MATS,) + mats[0].shape, f32)],
            name="unpack",
        )

    states = exchange([ef_state, cr_state], line[:1], passed=[sd_send, d_far_rows])
    ef_state, cr_state, sd_send, d_far_rows = states
    sd_got = to_core(sd_send)
    sd_state, ve_state = exchange(
        [
            (plane_first, 2, [(sd_keep, 0), (sd_got, 0)]),
            (None, vec_chunks, [(sd_keep, 4 * n_blk), (sd_got, 4 * n_blk)]),
        ],
        plane,
    )
    terms = spread_keys(d_mid_rows, d_far_rows)
    if line[1:]:
        df_state, ef_state, cr_state = exchange([df_state, ef_state, cr_state], line[1:])
    homes_back = homeward(
        call(
            lambda *refs: homes_kernel(2, *refs),
            [((2, tok, width), bf16)] * 2,
            held(d_own_rows + terms),
            name="homes",
        )
    )
    states = batch_rest([df_state, cr_state, ef_state])
    (early_own,) = combine([([(n, terms) for _, n, terms in states], bf16)])
    early_mats = gather(early_own)
    states = exchange([sd_state, ve_state], line)
    got = unpack(("up", "down", "attn", "up", "down"), early_mats)
    g_df_up, g_df_down, g_cr_in, g_cr_out, g_ef_up, g_ef_down = got
    states = batch_rest(states)
    own, vec = combine(
        [
            ([(n, terms) for _, n, terms in states[:-1]], bf16),
            ([(n, terms) for _, n, terms in states[-1:]], f32),
        ]
    )
    mats = gather(own)
    source_grad, target_grad = place_home(homes_back, (f32, f32))
    df, cr, ef, en, de = 0, 8, 16, 24, 32
    vec_rows = [
        [en + 3],
        [en + 4],
        [en + 2],
        [en, ef],
        [en + 1, ef + 1],
        [ef + 3, ef + 4, ef + 5, ef + 6],
        [ef + 2],
        [de + 3],
        [de + 4],
        [de + 2],
        [cr + 3],
        [cr + 4],
        [cr + 2],
        [de, cr, df],
        [de + 1, cr + 1, df + 1],
        [df + 3, df + 4, df + 5, df + 6],
        [df + 2],
    ]
    wide = (3, 4, 13, 14)
    got = unpack(("attn", "attn"), mats, vec, vec_rows, wide)
    g_en_in, g_en_out, g_de_in, g_de_out = got[:4]
    vectors = [
        values if number in wide else values.reshape(-1) for number, values in enumerate(got[4:])
    ]
    return (
        enc_out,
        dec_out,
        source_grad,
        target_grad,
        g_en_in,
        vectors[0],
        vectors[1],
        g_en_out,
        vectors[2],
        vectors[3],
        vectors[4],
        g_ef_up,
        vectors[5],
        g_ef_down,
        vectors[6],
        g_de_in,
        vectors[7],
        vectors[8],
        g_de_out,
        vectors[9],
        g_cr_in,
        vectors[10],
        vectors[11],
        g_cr_out,
        vectors[12],
        vectors[13],
        vectors[14],
        g_df_up,
        vectors[15],
        g_df_down,
        vectors[16],
    )


def solution(mesh):
    rows = P("batch", "blk", None)
    lists = P("batch", None)
    by_row = P("blk", None)
    stacked = P(None, "blk", None)
    whole = P()
    return jax.shard_map(
        on_device,
        mesh=mesh,
        in_specs=(rows, rows, lists, lists, lists) + (whole,) * 27 + (rows,),
        out_specs=(rows, rows, rows, rows)
        + (stacked, whole, whole, by_row, whole, whole, whole, by_row, whole, by_row, whole)
        + (stacked, whole, whole, by_row, whole)
        + (stacked, whole, whole, by_row, whole, whole, whole, by_row, whole, by_row, whole),
        check_vma=False,
    )
```

```python
import math

import jax
import jax.numpy as jnp
from jax import lax
from jax.experimental import pallas as pl
from jax.experimental.pallas import tpu as pltpu
from jax.sharding import PartitionSpec as P

H = 8
LANES = 128
MATS = 4
negative = -1e30
bf16 = jnp.bfloat16
f32 = jnp.float32
ROW_BYTES = 20 * 1024
MOST_BYTES = 60 * 1024 * 1024


def nn(left, right):
    return lax.dot_general(left, right, (((1,), (0,)), ((), ())), preferred_element_type=f32)


def nt(left, right):
    return lax.dot_general(left, right, (((1,), (1,)), ((), ())), preferred_element_type=f32)


def tn(left, right):
    return lax.dot_general(left, right, (((0,), (0,)), ((), ())), preferred_element_type=f32)


def turned(values):
    return values.astype(f32).T


def norm_forward(rows):
    centred = rows - jnp.mean(rows, axis=-1, keepdims=True)
    spread = jnp.mean(centred * centred, axis=-1, keepdims=True)
    rstd = lax.rsqrt(spread + 1e-05)
    return centred * rstd, rstd


def norm_backward(dy, normed, rstd, gain):
    dn = dy * gain
    dr = (
        dn
        - jnp.mean(dn, axis=-1, keepdims=True)
        - normed * jnp.mean(dn * normed, axis=-1, keepdims=True)
    ) * rstd
    return dr, column_sum(dy * normed), column_sum(dy)


def column_sum(values):
    return jnp.sum(values, axis=0, keepdims=True)


def gelu_pair(values):
    bell = jnp.exp(-0.5 * values * values)
    t = 1.0 / (1.0 + (0.3275911 * math.sqrt(0.5)) * jnp.abs(values))
    poly = 0.5 * 1.061405429
    for number in (-1.453152027, 1.421413741, -0.284496736, 0.254829592):
        poly = poly * t + 0.5 * number
    tail = poly * t * bell
    share = jnp.where(values >= 0, 1.0 - tail, tail)
    return values * share, share + values * bell * (1.0 / math.sqrt(2.0 * math.pi))


class Layout:
    def __init__(self, table, keep, send, blocks, groups):
        self.table, self.keep, self.send = table, keep, send
        self.blocks, self.groups = blocks, groups

    def put(self, values, mat, group, block0=0, count=None):
        count = self.blocks if count is None else count
        low = values.astype(bf16)
        rows = low.shape[0] // count
        first, y_step = self.groups[group]
        rel = lax.bitwise_xor(self.table[0], mat)
        base = lax.bitwise_and(rel, 1) * y_step + group * 2 * self.blocks

        def fill(ref):
            for number in range(count):
                place = base + self.table[first + block0 + number]
                ref[place] = low[number * rows : (number + 1) * rows]

        pl.when(rel < 2)(lambda: fill(self.keep))
        pl.when(rel >= 2)(lambda: fill(self.send))


def head_masks(axis, shape, head_size):
    places = lax.broadcasted_iota(jnp.int32, shape, axis)
    return [places // head_size == number for number in range(LANES // head_size)]


def as_column(row):
    return jnp.broadcast_to(row, (LANES, row.shape[1])).T[:, 0:1]


def segments_kernel(tok, place, lists, far, segs):
    count = lists.shape[2]
    total = segs.shape[1]
    row = lambda number: jnp.where(
        place[0] == 1, lists[number, pl.ds(place[1], 1)], far[number, pl.ds(place[1], 1)]
    ).astype(f32)
    at_row = lax.broadcasted_iota(jnp.int32, (count, count), 0)
    at_col = lax.broadcasted_iota(jnp.int32, (count, count), 1)

    def ends(number):
        return jnp.sum(jnp.where(at_col <= at_row, row(number), 0.0), axis=1, keepdims=True)

    spots = jnp.concatenate(
        [
            lax.broadcasted_iota(jnp.int32, (1, tok), 1) + place[2 + number] * tok
            for number in range(total // tok)
        ],
        axis=1,
    ).astype(f32)
    src = jnp.sum((ends(0) <= spots).astype(f32), axis=0, keepdims=True)
    tgt = jnp.sum((ends(1) <= spots).astype(f32), axis=0, keepdims=True)
    partner = jnp.sum(jnp.where(at_col == at_row, row(2), 0.0), axis=1, keepdims=True)
    numbers = lax.broadcasted_iota(jnp.int32, (count, 1), 0).astype(f32)
    segs[0:1] = src
    segs[1:2] = tgt
    segs[2:3] = jnp.sum(jnp.where(numbers == tgt, partner, 0.0), axis=0, keepdims=True)
    segs[3:8] = jnp.zeros((5, total), f32)


def call_kernel(kernel, outs, args, scratch, name, after, passed, vmem_bytes):
    spaces = {"s": pltpu.SMEM, "v": pltpu.VMEM}
    before = len(args) + len(after)

    def body(*refs):
        made = refs[before + len(passed) :]
        kernel(*refs[: len(args)], *made[: len(outs)], *made[len(outs) + len(passed) :])

    any_space = pl.BlockSpec(memory_space=pl.ANY)
    shapes = [jax.ShapeDtypeStruct(shape, kind) for shape, kind in outs]
    shapes += [jax.ShapeDtypeStruct(array.shape, array.dtype) for array in passed]
    return pl.pallas_call(
        body,
        out_shape=tuple(shapes),
        in_specs=[pl.BlockSpec(memory_space=spaces[mode]) for mode, _ in args]
        + [any_space] * (len(after) + len(passed)),
        out_specs=tuple(
            [pl.BlockSpec(memory_space=pltpu.VMEM)] * len(outs) + [any_space] * len(passed)
        ),
        scratch_shapes=list(scratch),
        input_output_aliases={before + at: len(outs) + at for at in range(len(passed))},
        compiler_params=pltpu.CompilerParams(vmem_limit_bytes=vmem_bytes),
        name=name,
    )(*[array for _, array in args], *after, *passed)


def keys_values(parts, w_input, b_value, k_out, v_out):
    at = 0
    for part in parts:
        rows = part.shape[0]
        piece = part[...]
        k_out[at : at + rows] = nn(piece, w_input[1]).astype(bf16)
        v_out[at : at + rows] = (nn(piece, w_input[2]) + b_value[...]).astype(bf16)
        at += rows


def attn_forward(parts, query, segs, seg_rows, weights, q_out, k_out, v_out, att_out, lse_out):
    w_input, b_query, b_value, w_out, b_out = weights
    own_rows, width = q_out.shape
    head_size = width // H
    keys_values(parts, w_input, b_value, k_out, v_out)
    xq = parts[0][0:own_rows] if query is None else query
    factor = 1.0 / math.sqrt(head_size)
    q = (nn(xq, w_input[0]) + b_query[...]).astype(bf16)
    q_out[...] = (q.astype(f32) * factor).astype(bf16)
    seg_query = as_column(segs[seg_rows[0] : seg_rows[0] + 1, 0:own_rows])
    bias = jnp.where(seg_query == segs[seg_rows[1] : seg_rows[1] + 1], 0.0, negative)
    masks = head_masks(1, (own_rows, LANES), head_size)
    lse_all = jnp.zeros((own_rows, LANES), f32)
    lane = lax.broadcasted_iota(jnp.int32, (own_rows, LANES), 1)
    for pair in range(width // LANES):
        cols = slice(pair * LANES, (pair + 1) * LANES)
        q_pair, k_pair, v_pair = q_out[:, cols], k_out[:, cols], v_out[:, cols]
        merged = None
        for number, mask in enumerate(masks):
            q_head = jnp.where(mask, q_pair, jnp.zeros_like(q_pair))
            scores = nt(q_head, k_pair) + bias
            peak = jnp.max(scores, axis=1, keepdims=True)
            weights = jnp.exp(scores - peak)
            total = jnp.sum(weights, axis=1, keepdims=True)
            out = nn(weights.astype(bf16), v_pair) * (1.0 / total)
            merged = out if merged is None else jnp.where(mask, out, merged)
            head = pair * len(masks) + number
            lse_all = jnp.where(lane == head, peak + jnp.log(total), lse_all)
        att_out[:, cols] = merged
    lse_out[...] = lse_all.T[0:H]
    branch = nn(att_out[...].astype(bf16), w_out[...]) + b_out[...]
    return branch + xq.astype(f32) if query is None else branch


def ffn_forward(values, weights, act_out, slope_out):
    w_up, b_up, w_down, b_down = weights
    width = values.shape[1]
    low = values.astype(bf16)
    total = values + b_down[...]
    for at in range(0, w_up.shape[1], width):
        cols = slice(at, at + width)
        act, slope = gelu_pair(nn(low, w_up[:, cols]) + b_up[:, cols])
        act_low = act.astype(bf16)
        act_out[:, cols] = act_low
        slope_out[:, cols] = slope.astype(bf16)
        total = total + nn(act_low, w_down[cols, :])
    return total


def ffn_backward(dr, low, act, slope, w_up, w_down, up, down, blocks, sums):
    width = dr.shape[1]
    d_ffn = dr.astype(bf16)
    sums.append(column_sum(d_ffn.astype(f32)))
    total = dr
    per_blk = w_down.shape[0] // blocks
    chunk = per_blk // MATS
    for number in range(MATS):
        at = number * width
        cols = slice(at, at + width)
        d_act = nt(d_ffn, w_down[cols, :])
        d_pre = (d_act * slope[:, cols].astype(f32)).astype(bf16)
        sums.append(column_sum(d_pre.astype(f32)))
        total = total + nt(d_pre, w_up[:, cols])
        up.put(tn(low, d_pre), number, 0)
        rows = tn(act[:, cols], d_ffn)
        for row in range(0, width, chunk):
            block, mat = (at + row) // per_blk, (at + row) % per_blk // chunk
            down.put(rows[row : row + chunk], mat, 1, block, 1)
    return total


def attn_backward(dr, xq, xk_parts, saved, segs, seg_rows, w_input, w_out, layout, group, buffers, sums):
    att, lse, q8, k, v = saved
    dk_buf, dv_buf, dq_buf = buffers
    own_rows, width = dr.shape
    head_size = width // H
    factor = 1.0 / math.sqrt(head_size)
    d_branch = dr.astype(bf16)
    att_rows = att[...]
    layout.put(tn(att_rows.astype(bf16), d_branch), 3, group)
    do_turned = nt(w_out[...], d_branch).astype(bf16)
    delta = jnp.sum((do_turned.astype(f32) * att_rows.T).reshape(H, head_size, own_rows), axis=1)
    lse_turned = lse[...]
    q_turned = turned(q8[...]).astype(bf16)
    seg_key = as_column(segs[seg_rows[1] : seg_rows[1] + 1])
    bias = jnp.where(seg_key == segs[seg_rows[0] : seg_rows[0] + 1, 0:own_rows], 0.0, negative)
    masks = head_masks(0, (LANES, own_rows), head_size)
    for pair in range(width // LANES):
        cols = slice(pair * LANES, (pair + 1) * LANES)
        k_pair, v_pair = k[:, cols], v[:, cols]
        k_turned = turned(k_pair).astype(bf16)
        q_pair, do_pair = q_turned[cols], do_turned[cols]
        dk_pair, dv_pair = None, None
        for number, mask in enumerate(masks):
            head = pair * len(masks) + number
            zero = jnp.zeros_like(q_pair)
            q_head = jnp.where(mask, q_pair, zero)
            do_head = jnp.where(mask, do_pair, zero)
            probs = jnp.exp(nn(k_pair, q_head) + bias - lse_turned[head : head + 1])
            d_prob = nn(v_pair, do_head)
            d_score = (probs * (d_prob - delta[head : head + 1])).astype(bf16)
            dv_term = nt(probs.astype(bf16), do_head)
            dk_term = nt(d_score, q_head)
            dv_pair = dv_term if dv_pair is None else dv_pair + dv_term
            dk_pair = dk_term if dk_pair is None else dk_pair + dk_term
            rows = slice(head * head_size, (head + 1) * head_size)
            dq_buf[rows] = nn(k_turned[number * head_size : (number + 1) * head_size], d_score)
        dk_buf[:, cols] = dk_pair.astype(bf16)
        dv_buf[:, cols] = dv_pair.astype(bf16)
    dq = (dq_buf[...].T * factor).astype(bf16)
    layout.put(tn(xq, dq), 0, group)
    dk, dv = dk_buf[...], dv_buf[...]
    grad_key, grad_value = None, None
    at = 0
    for part in xk_parts:
        rows = part.shape[0]
        piece = part[...]
        key_term, value_term = tn(piece, dk[at : at + rows]), tn(piece, dv[at : at + rows])
        grad_key = key_term if grad_key is None else grad_key + key_term
        grad_value = value_term if grad_value is None else grad_value + value_term
        at += rows
    layout.put(grad_key, 1, group)
    layout.put(grad_value, 2, group)
    sums += [
        column_sum(d_branch.astype(f32)),
        column_sum(dq.astype(f32)),
        column_sum(dv.astype(f32)),
        jnp.zeros((3, width), f32),
    ]
    return nt(dq, w_input[0]), nt(dk, w_input[1]) + nt(dv, w_input[2])


def add_up(parts, own_rows):
    total = parts[0][0:own_rows].astype(f32)
    for part in parts[1:]:
        total = total + part[0:own_rows].astype(f32)
    return total


def pack_kernel(*refs):
    at = 0
    for ref in refs[:-1]:
        refs[-1][at : at + ref.shape[0]] = ref[...]
        at += ref.shape[0]


def self_attn(parts, segs, seg_rows, weights, q, att, lse, norm_one, rstd_one, buffers):
    k, v = buffers
    rows = attn_forward(parts, None, segs, seg_rows, weights, q, k, v, att, lse)
    normed, rstd = norm_forward(rows)
    norm_one[...] = normed
    rstd_one[...] = rstd
    return normed


def enc_forward_kernel(seg_rows, *refs):
    near, far, segs, w_input, b_query, b_value, w_out, b_out = refs[:8]
    gains, shifts, w_up, b_up, w_down, b_down = refs[8:14]
    q, att, lse, norm_one, rstd_one, act, slope, norm_two, rstd_two, low, k, v = refs[14:]
    weights = (w_input, b_query, b_value, w_out, b_out)
    normed = self_attn(
        [near, far], segs, seg_rows, weights, q, att, lse, norm_one, rstd_one, (k, v)
    )
    values = normed * gains[0:1] + shifts[0:1]
    normed, rstd = norm_forward(ffn_forward(values, (w_up, b_up, w_down, b_down), act, slope))
    norm_two[...] = normed
    rstd_two[...] = rstd
    low[...] = (normed * gains[1:2] + shifts[1:2]).astype(bf16)


def dec_forward_kernel(seg_rows, *refs):
    near, far, segs, w_input, b_query, b_value, w_out, b_out = refs[:8]
    q, att, lse, norm_one, rstd_one, k, v = refs[8:]
    weights = (w_input, b_query, b_value, w_out, b_out)
    self_attn([near, far], segs, seg_rows, weights, q, att, lse, norm_one, rstd_one, (k, v))


def cross_forward_kernel(part_count, cot_count, seg_rows, blocks, groups, table, *refs):
    refs = list(refs)
    parts, refs = refs[:part_count], refs[part_count:]
    cots, refs = refs[:cot_count], refs[cot_count:]
    prev_norm, segs, w_input, b_query, b_value, w_out, b_out, gains, shifts = refs[:9]
    w_up, b_up, w_down, b_down = refs[9:13]
    q, k, v, att, lse, norm_two_out, rstd_two_out, d_second = refs[13:21]
    homes = refs[21:23]
    keep, send, vecs, act, slope = refs[23:]
    own_rows = prev_norm.shape[0]
    upper = prev_norm[...] * gains[0:1] + shifts[0:1]
    weights = (w_input, b_query, b_value, w_out, b_out)
    branch = attn_forward(
        parts, upper.astype(bf16), segs, seg_rows, weights, q, k, v, att, lse
    )
    norm_two, rstd_two = norm_forward(upper + branch)
    norm_two_out[...] = norm_two
    rstd_two_out[...] = rstd_two
    crossed = norm_two * gains[1:2] + shifts[1:2]
    norm_three, rstd_three = norm_forward(
        ffn_forward(crossed, (w_up, b_up, w_down, b_down), act, slope)
    )
    low = (norm_three * gains[2:3] + shifts[2:3]).astype(bf16)
    tok = own_rows // 2
    memory = parts[0][...]
    for number, home in enumerate(homes):
        home[0] = memory[number * tok : (number + 1) * tok]
        home[1] = low[number * tok : (number + 1) * tok]
    dy = jnp.concatenate([cot[...] for cot in cots], axis=0).astype(f32)
    sums = []
    dr, d_gain, d_shift = norm_backward(dy, norm_three, rstd_three, gains[2:3])
    sums += [d_gain, d_shift]
    layout = Layout(table, keep, send, blocks, groups)
    d_second[...] = ffn_backward(
        dr, crossed.astype(bf16), act, slope, w_up, w_down, layout, layout, blocks, sums
    )
    sums.append(jnp.zeros_like(d_gain))
    vecs[...] = jnp.concatenate(sums, axis=0)


def cross_backward_kernel(part_count, has_mid, seg_rows, blocks, groups, table, *refs):
    refs = list(refs)
    parts, refs = refs[:part_count], refs[part_count:]
    d_in, norm_two, rstd_two, prev_norm, gains, shifts = refs[:6]
    att, w_out, lse, q, k, v, segs, w_input = refs[6:14]
    refs = refs[14:]
    d_upper, d_own = refs[:2]
    refs = refs[2:]
    d_mid = refs.pop(0) if has_mid else None
    d_far, keep, send, vecs = refs[:4]
    buffers = refs[4:]
    own_rows = prev_norm.shape[0]
    sums = []
    dr, d_gain, d_shift = norm_backward(d_in[...], norm_two[...], rstd_two[...], gains[1:2])
    sums += [d_gain, d_shift]
    xq = (prev_norm[...] * gains[0:1] + shifts[0:1]).astype(bf16)
    layout = Layout(table, keep, send, blocks, groups)
    d_query, d_key = attn_backward(
        dr, xq, parts, (att, lse, q, k, v), segs, seg_rows, w_input, w_out, layout, 0, buffers, sums
    )
    keys = d_key.shape[0]
    d_upper[...] = dr + d_query
    d_own[...] = d_key[0:own_rows]
    if has_mid:
        d_mid[...] = d_key[own_rows : keys // 2].astype(bf16)
    d_far[...] = d_key[keys // 2 :].astype(bf16)
    vecs[...] = jnp.concatenate(sums, axis=0)


def ffn_backward_kernel(part_count, blocks, groups, table, *refs):
    parts, refs = refs[:part_count], refs[part_count:]
    norm_two, rstd_two, norm_one, gains, shifts, slope, w_down, act, w_up = refs[:9]
    d_out, keep, send, vecs = refs[9:]
    sums = []
    dy = add_up(parts, norm_one.shape[0])
    dr, d_gain, d_shift = norm_backward(dy, norm_two[...], rstd_two[...], gains[1:2])
    sums += [d_gain, d_shift]
    low = (norm_one[...] * gains[0:1] + shifts[0:1]).astype(bf16)
    layout = Layout(table, keep, send, blocks, groups)
    d_out[...] = ffn_backward(dr, low, act, slope, w_up, w_down, layout, layout, blocks, sums)
    sums.append(jnp.zeros_like(d_gain))
    vecs[...] = jnp.concatenate(sums, axis=0)


def self_backward_kernel(has_mid, vec_count, seg_rows, blocks, groups, table, segs, *refs):
    refs = list(refs)
    vecs_in, refs = refs[:vec_count], refs[vec_count:]
    d_in, norm_one, rstd_one, gains, att, w_out, lse, q, near, far, w_input, b_value = refs[:12]
    refs = refs[12:]
    d_own = refs.pop(0)
    mid = refs.pop(0) if has_mid else None
    far_out, keep, send = refs[:3]
    refs = refs[3:]
    vecs = None if vec_count else refs.pop(0)
    k, v = refs[:2]
    buffers = refs[2:]
    own_rows, width = norm_one.shape
    layout = Layout(table, keep, send, blocks, groups)
    sums = []
    dr, d_gain, d_shift = norm_backward(d_in[...], norm_one[...], rstd_one[...], gains[0:1])
    sums += [d_gain, d_shift]
    keys_values([near, far], w_input, b_value, k, v)
    xq = near[0:own_rows]
    d_query, d_key = attn_backward(
        dr, xq, [near, far], (att, lse, q, k, v), segs, seg_rows, w_input, w_out, layout, 0, buffers, sums
    )
    keys = d_key.shape[0]
    d_own[...] = dr + d_query + d_key[0:own_rows]
    if has_mid:
        mid[0] = d_key[own_rows : keys // 2].astype(bf16)
    far_out[0] = d_key[keys // 2 :].astype(bf16)
    if not vec_count:
        vecs[...] = jnp.concatenate(sums, axis=0)
        return
    all_sums = [vec[...] for vec in vecs_in] + sums
    more = keep.shape[0] - 2 * blocks
    rows = keep.shape[1]
    pad = more * rows - sum(piece.shape[0] for piece in all_sums)
    if pad:
        all_sums.append(jnp.zeros((pad, width), f32))
    all_sums = jnp.concatenate(all_sums, axis=0).astype(bf16)
    for number in range(more):
        keep[2 * blocks + number] = all_sums[number * rows : (number + 1) * rows]
        send[2 * blocks + number] = all_sums[number * rows : (number + 1) * rows]


def middle_kernel(own_rows, pairs, *refs):
    for number, out in enumerate(refs[2 * pairs :]):
        mine = slice(number * own_rows, (number + 1) * own_rows)
        far = slice((number + 1) * own_rows, (number + 2) * own_rows)
        for at in range(pairs):
            total = refs[2 * at][0, mine].astype(f32) + refs[2 * at + 1][0, far].astype(f32)
            out[at] = total.astype(bf16)


def homes_kernel(count, *refs):
    homes = refs[-2:]
    tok = homes[0].shape[1]
    for number in range(count):
        total = refs[2 * number][...] + refs[2 * number + 1][0, 0 : 2 * tok].astype(f32)
        for term in refs[2 * count : -2]:
            total = total + term[number].astype(f32)
        total = total.astype(bf16)
        for d_lo, home in enumerate(homes):
            home[number] = total[d_lo * tok : (d_lo + 1) * tok]


def gate_kernel(out):
    out[...] = jnp.zeros_like(out)


def combine_kernel(count, plan, *refs):
    inputs, outputs = refs[:count], refs[count:]
    for out, segments in zip(outputs, plan):
        at = 0
        for chunks, terms in segments:
            total = None
            for number, first in terms:
                term = inputs[number][first : first + chunks].astype(f32)
                total = term if total is None else total + term
            out[at : at + chunks] = total.astype(out.dtype)
            at += chunks


def place_kernel(table, got_one, got_two, *outs):
    for number, out in enumerate(outs):
        out[table[0]] = got_one[number].astype(out.dtype)
        out[lax.bitwise_xor(table[0], 1)] = got_two[number].astype(out.dtype)


def unpack_kernel(kinds, vec_rows, table, *refs):
    refs = list(refs)
    mats = refs[:MATS]
    refs = refs[MATS:]
    vec = refs.pop(0) if vec_rows else None
    scratch = refs.pop()
    for rel in range(MATS):
        scratch[lax.bitwise_xor(table[0], rel)] = mats[rel][...].astype(f32)
    width = mats[0].shape[2]
    rows = mats[0].shape[1]
    for group, kind in enumerate(kinds):
        if kind == "attn":
            w_input, w_out = refs.pop(0), refs.pop(0)
            for mat in range(MATS - 1):
                w_input[mat] = scratch[mat, group]
            w_out[...] = scratch[MATS - 1, group]
        elif kind == "up":
            out = refs.pop(0)
            for mat in range(MATS):
                out[:, mat * width : (mat + 1) * width] = scratch[mat, group]
        else:
            out = refs.pop(0)
            for mat in range(MATS):
                out[mat * rows : (mat + 1) * rows] = scratch[mat, group]
    if vec_rows:
        sums = jnp.concatenate([vec[number] for number in range(vec.shape[0])], axis=0).astype(f32)
        for out, numbers in zip(refs, vec_rows):
            for at, number in enumerate(numbers):
                if out.shape[0] == 1:
                    out[:, at * width : (at + 1) * width] = sums[number : number + 1]
                else:
                    out[at : at + 1] = sums[number : number + 1]


def on_device(
    source,
    target,
    src_lengths,
    tgt_lengths,
    pairing,
    enc_w_input,
    enc_b_query,
    enc_b_value,
    enc_w_out,
    enc_b_out,
    enc_gains,
    enc_shifts,
    enc_w_up,
    enc_b_up,
    enc_w_down,
    enc_b_down,
    dec_w_input,
    dec_b_query,
    dec_b_value,
    dec_w_out,
    dec_b_out,
    cross_w_input,
    cross_b_query,
    cross_b_value,
    cross_w_out,
    cross_b_out,
    dec_gains,
    dec_shifts,
    dec_w_up,
    dec_b_up,
    dec_w_down,
    dec_b_down,
    cotangent,
):
    streams, tok, width = source.shape
    n_batch, n_blk = lax.axis_size("batch"), lax.axis_size("blk")
    half = n_blk // 2
    mids = n_blk // 4
    own_rows = 2 * tok
    total_rows = n_blk * tok
    near_rows = total_rows // 2
    chunk_rows = width // n_blk
    ff = enc_w_up.shape[1]
    b, i = lax.axis_index("batch"), lax.axis_index("blk")
    core, y_bit = b & 1, (b >> 1) & 1
    hi, mid, lo = i // half, (i % half) // 2, i & 1

    def move(values, where):
        pairs = []
        for from_b in range(n_batch):
            for from_i in range(n_blk):
                to_b, to_i = where(from_b, from_i)
                pairs.append((from_b * n_blk + from_i, to_b * n_blk + to_i))
        return lax.ppermute(values, ("batch", "blk"), pairs)

    def regroup(values, d_mid, d_lo):
        def where(fb, fi):
            f_hi, f_mid, f_lo, f_core = fi // half, (fi % half) // 2, fi & 1, fb & 1
            return ((fb & ~1) | f_hi, f_core * half + (f_mid ^ d_mid) * 2 + (f_lo ^ d_lo))

        return move(values, where)

    to_bits = lambda values, d_b, d_i: move(values, lambda fb, fi: (fb ^ d_b, fi ^ d_i))
    to_core = lambda values: to_bits(values, 1, 0)
    to_mid = lambda values, d_mid: to_bits(values, 0, 2 * d_mid)

    last = []

    def call(kernel, outs, args, scratch=(), name=None, passed=(), after=()):
        vmem_bytes = min(total_rows * ROW_BYTES, MOST_BYTES)
        held_back = last[-1:] + list(after)
        got = call_kernel(kernel, outs, args, scratch, name, held_back, list(passed), vmem_bytes)
        last.append(min(got[: len(outs)], key=lambda array: array.size))
        return got

    bits = n_blk.bit_length() - 1
    batch_bits = n_batch.bit_length() - 1
    more_dims = [(1 << bit,) for bit in range(2, batch_bits)]
    rest = list(range(2, bits))
    orders = {
        "x": [0, "y", 1] + rest,
        "y": ["y", 0, 1] + rest,
        "z": [1] + rest + ["y", 0],
    }

    def group_of(kind):
        at = list(orders).index(kind)
        return (1 + at * n_blk, 1 << (bits - orders[kind].index("y")))

    def places_of(order):
        step = {name: 1 << (bits - at) for at, name in enumerate(order)}
        return [
            sum((((number ^ i) >> bit) & 1) * step[bit] for bit in range(bits))
            for number in range(n_blk)
        ]

    all_places = [place for order in orders.values() for place in places_of(order)]
    mat_table = jnp.stack([2 * core + y_bit] + all_places).astype(jnp.int32)

    def state(kind, keep, got, group):
        first = group * 2 * n_blk
        return (orders[kind] + more_dims, 1, False, [(keep, first), (got, first)])

    runs = [
        (core ^ d_core) * half + (mid ^ d_mid) * 2 + (lo ^ d_lo)
        for d_core in range(2)
        for d_mid in range(mids)
        for d_lo in range(2)
    ]
    place_table = jnp.stack([(hi == core).astype(jnp.int32), lo] + runs).astype(jnp.int32)
    lo_table = jnp.stack([lo, lo]).astype(jnp.int32)
    row = lambda values: values.reshape(1, -1)

    def stream_of(values, number):
        return lax.dynamic_index_in_dim(values, number, 0, keepdims=False)

    def near_parts(values):
        return [
            regroup(stream_of(values, lo ^ d_lo), d_mid, d_lo)
            for d_mid in range(mids)
            for d_lo in range(2)
        ]

    held = lambda arrays: [("v", array) for array in arrays]
    packed = lambda chunks: ((chunks, chunk_rows, width), bf16)
    rows_f32 = ((own_rows, width), f32)
    rows_bf16 = ((own_rows, width), bf16)
    one_f32 = ((own_rows, 1), f32)
    lse_shape = ((H, own_rows), f32)
    all_keys = ((total_rows, width), bf16)
    vec_shape = ((8, width), f32)
    has_mid = near_rows > own_rows
    key_buffers = [pltpu.VMEM(*all_keys), pltpu.VMEM(*all_keys)]
    back_buffers = key_buffers + [pltpu.VMEM((width, own_rows), f32)]
    def pack(parts):
        return call(pack_kernel, [((near_rows, width), bf16)], held(parts), name="pack")[0]

    src_parts = near_parts(source)
    tgt_parts = near_parts(target)
    cot_parts = [regroup(stream_of(cotangent, lo ^ d_lo), 0, d_lo) for d_lo in range(2)]
    lists = jnp.stack([src_lengths, tgt_lengths, pairing])
    (segs,) = call(
        lambda *refs: segments_kernel(tok, *refs),
        [((8, total_rows), f32)],
        [("s", place_table)] + held([lists, to_core(lists)]),
        name="segments",
    )
    src_rows, tgt_rows, pair_rows = (0, 0), (1, 1), (2, 0)
    src_near = pack(src_parts)
    src_far = to_core(src_near)

    def spread_mid(pairs):
        if not has_mid:
            return []
        totals = call(
            lambda *refs: middle_kernel(own_rows, len(pairs), *refs),
            [((len(pairs), own_rows, width), bf16)] * (mids - 1),
            held([array for pair in pairs for array in pair]),
            name="middle",
        )
        return [to_mid(total, d_mid) for d_mid, total in enumerate(totals, 1)]

    def homeward(homes):
        return [regroup(home, 0, d_lo) for d_lo, home in enumerate(homes)]

    def place_home(got, kinds, passed=()):
        outs = [((streams, tok, width), kind) for kind in kinds]
        return call(
            place_kernel, outs, [("s", lo_table)] + held(got), name="place", passed=passed
        )

    def combine(plan_outs, passed=(), after=()):
        arrays, index, plan, outs = [], {}, [], []
        for segments, kind in plan_outs:
            rows = []
            for chunks, terms in segments:
                named = []
                for array, first in terms:
                    if id(array) not in index:
                        index[id(array)] = len(arrays)
                        arrays.append(array)
                    named.append((index[id(array)], first))
                rows.append((chunks, named))
            plan.append(rows)
            outs.append(((sum(chunks for chunks, _ in rows), chunk_rows, width), kind))
        return call(
            lambda *refs: combine_kernel(len(arrays), plan, *refs),
            outs,
            held(arrays),
            name="combine",
            passed=passed,
            after=after,
        )

    def offset(name):
        if name == "y":
            return (2, 0)
        if isinstance(name, tuple):
            return (name[0], 0)
        return (0, 1 << name)

    def step(states, passed=(), after=()):
        mine, away, found = [], {}, []
        sizes = {}
        for left, chunks, whole, terms in states:
            if not left:
                found.append((left, chunks, whole, terms, None, None))
                continue
            name, rest = left[0], left[1:]
            full = whole or isinstance(name, tuple)
            count = chunks << (0 if whole else sum(not isinstance(dim, tuple) for dim in rest))
            own_at = sum(n for n, _ in mine)
            mine.append((count, terms))
            segments = away.setdefault(name, [])
            far_at = sum(n for n, _ in segments)
            start = 0 if full else count
            segments.append((count, [(array, first + start) for array, first in terms]))
            found.append((rest, chunks, whole, own_at, name, far_at))
        plan = [(mine, bf16)] + [(segments, bf16) for segments in away.values()]
        arrays = combine(plan, passed, after)
        got = {}
        for name, array in zip(away, arrays[1:]):
            got[name] = to_bits(array, *offset(name))
        stepped = []
        for rest, chunks, whole, own_at, name, far_at in found:
            terms = own_at if name is None else [(arrays[0], own_at), (got[name], far_at)]
            stepped.append((rest, chunks, whole, terms))
        return stepped + list(arrays[len(plan) :])

    def finish(states):
        while any(left for left, _, _, _ in states):
            states = step(states)
        return states

    def arrived(states):
        return [array for _, _, _, terms in states for array, _ in terms[1:]]

    def sum_of(states):
        return [(chunks, terms) for _, chunks, _, terms in states]

    def attn_args(w_input, b_query, b_value, w_out, b_out):
        return held([w_input, row(b_query), row(b_value), w_out, row(b_out)])

    def ffn_args(w_up, b_up, w_down, b_down):
        return held([w_up, row(b_up), w_down, row(b_down)])

    enc_q, enc_att, enc_lse, enc_n1, enc_r1, enc_act, enc_slope, enc_n2, enc_r2, memory = call(
        lambda *refs: enc_forward_kernel(src_rows, *refs),
        [rows_bf16, rows_f32, lse_shape, rows_f32, one_f32]
        + [((own_rows, ff), bf16), ((own_rows, ff), bf16), rows_f32, one_f32, rows_bf16],
        held([src_near, src_far, segs])
        + attn_args(enc_w_input, enc_b_query, enc_b_value, enc_w_out, enc_b_out)
        + held([enc_gains, enc_shifts])
        + ffn_args(enc_w_up, enc_b_up, enc_w_down, enc_b_down),
        scratch=key_buffers,
        name="enc_forward",
    )
    ffn_groups = [group_of("x"), group_of("y")]
    places = [(d_core, d_mid) for d_core in range(2) for d_mid in range(mids)]
    mem_parts = [memory] + [
        to_bits(memory, d_core, 2 * d_mid) for d_core, d_mid in places[1:]
    ]
    tgt_near = pack(tgt_parts)
    tgt_far = to_core(tgt_near)
    dec_q, dec_att, dec_lse, dec_n1, dec_r1 = call(
        lambda *refs: dec_forward_kernel(tgt_rows, *refs),
        [rows_bf16, rows_f32, lse_shape, rows_f32, one_f32],
        held([tgt_near, tgt_far, segs])
        + attn_args(dec_w_input, dec_b_query, dec_b_value, dec_w_out, dec_b_out),
        scratch=key_buffers,
        name="dec_forward",
    )

    got = call(
        lambda *refs: cross_forward_kernel(
            len(mem_parts), len(cot_parts), pair_rows, n_blk, ffn_groups, *refs
        ),
        [rows_bf16, all_keys, all_keys, rows_f32, lse_shape, rows_f32, one_f32, rows_f32]
        + [((2, tok, width), bf16)] * 2
        + [packed(4 * n_blk)] * 2
        + [vec_shape],
        [("s", mat_table)]
        + held(mem_parts + cot_parts + [dec_n1, segs])
        + attn_args(cross_w_input, cross_b_query, cross_b_value, cross_w_out, cross_b_out)
        + held([dec_gains, dec_shifts])
        + ffn_args(dec_w_up, dec_b_up, dec_w_down, dec_b_down),
        scratch=[pltpu.VMEM((own_rows, ff), bf16), pltpu.VMEM((own_rows, ff), bf16)],
        name="cross_forward",
    )
    cr_q, cr_k, cr_v, cr_att, cr_lse, dec_n2, dec_r2, d_second = got[:8]
    homes = homeward(got[8:10])
    df_keep, df_send, df_vec = got[10:]
    df_got = to_core(df_send)
    mid_shape = [((near_rows - own_rows, width), bf16)] if has_mid else []
    got = list(
        call(
            lambda *refs: cross_backward_kernel(
                len(mem_parts), has_mid, pair_rows, n_blk, [group_of("z")], *refs
            ),
            [rows_f32, rows_f32]
            + mid_shape
            + [((near_rows, width), bf16)]
            + [packed(2 * n_blk)] * 2
            + [vec_shape],
            [("s", mat_table)]
            + held(mem_parts)
            + held([d_second, dec_n2, dec_r2, dec_n1, dec_gains, dec_shifts])
            + held([cr_att, cross_w_out, cr_lse, cr_q, cr_k, cr_v, segs, cross_w_input]),
            scratch=back_buffers,
            name="cross_backward",
        )
    )
    d_upper, d_mem_own = got[:2]
    d_mem_mid = got[2][None] if has_mid else None
    d_mem_far, cr_keep, cr_send, cr_vec = got[2 + len(mid_shape) :]
    df = step([state("x", df_keep, df_got, 0), state("y", df_keep, df_got, 1)])
    mem_got = to_core(d_mem_far[None])
    mem_terms = [mem_got[0]] + [term[0] for term in spread_mid([(d_mem_mid, mem_got)])]
    cr_got = to_core(cr_send)

    d_first, ef_keep, ef_send, ef_vec = call(
        lambda *refs: ffn_backward_kernel(1 + len(mem_terms), n_blk, ffn_groups, *refs),
        [rows_f32] + [packed(4 * n_blk)] * 2 + [vec_shape],
        [("s", mat_table)]
        + held([d_mem_own] + mem_terms)
        + held([enc_n2, enc_r2, enc_n1, enc_gains, enc_shifts])
        + held([enc_slope, enc_w_down, enc_act, enc_w_up]),
        name="ffn_backward",
    )
    _, ef_send = call(
        gate_kernel, [((8, LANES), f32)], [], name="gate", after=arrived(df), passed=[ef_send]
    )
    ef_got = to_core(ef_send)
    early = step(
        [
            state("x", ef_keep, ef_got, 0),
            state("y", ef_keep, ef_got, 1),
            state("z", cr_keep, cr_got, 0),
        ]
    )

    def self_backward(d_in, saved, seg_rows, kind, vecs_in=()):
        more = -(-8 * (len(vecs_in) + 1) // chunk_rows) if vecs_in else 0
        got = call(
            lambda *refs: self_backward_kernel(
                has_mid, len(vecs_in), seg_rows, n_blk, [group_of(kind)], *refs
            ),
            [rows_f32]
            + [((1,) + shape, kind) for shape, kind in mid_shape]
            + [((1, near_rows, width), bf16)]
            + [packed(2 * n_blk + more)] * 2
            + ([] if vecs_in else [vec_shape]),
            [("s", mat_table)] + held([segs] + list(vecs_in) + [d_in] + saved),
            scratch=key_buffers + back_buffers,
            name="self_backward",
        )
        got = list(got)
        if not has_mid:
            got.insert(1, None)
        return got

    d_tgt_own, d_tgt_mid, d_tgt_far, de_keep, de_send, de_vec = self_backward(
        d_upper,
        [dec_n1, dec_r1, dec_gains, dec_att, dec_w_out, dec_lse, dec_q]
        + [tgt_near, tgt_far, dec_w_input, row(dec_b_value)],
        tgt_rows,
        "y",
    )
    *early, de_send, d_tgt_far = step(early + df, passed=[de_send, d_tgt_far], after=homes)
    de_got, tgt_got = to_core(de_send), to_core(d_tgt_far)
    d_src_own, d_src_mid, d_src_far, en_keep, en_send = self_backward(
        d_first,
        [enc_n1, enc_r1, enc_gains, enc_att, enc_w_out, enc_lse, enc_q]
        + [src_near, src_far, enc_w_input, row(enc_b_value)],
        src_rows,
        "x",
        [df_vec, cr_vec, de_vec, ef_vec],
    )

    def gather(own):
        side = to_bits(own, 2, 0)
        return [own, side, to_core(own), to_core(side)]

    def unpack(kinds, mats, vec=None, vec_rows=(), wide=()):
        outs = []
        for kind in kinds:
            if kind == "attn":
                outs += [((MATS - 1, chunk_rows, width), f32), ((chunk_rows, width), f32)]
            elif kind == "up":
                outs.append(((chunk_rows, MATS * width), f32))
            else:
                outs.append(((MATS * chunk_rows, width), f32))
        for number, numbers in enumerate(vec_rows):
            shape = (len(numbers), width) if number in wide else (1, len(numbers) * width)
            outs.append((shape, f32))
        return call(
            lambda *refs: unpack_kernel(kinds, vec_rows, *refs),
            outs,
            [("s", mat_table)] + held(list(mats) + ([vec] if vec_rows else [])),
            scratch=[pltpu.VMEM((MATS,) + mats[0].shape, f32)],
            name="unpack",
        )

    _, en_send, d_src_far = call(
        gate_kernel,
        [((8, LANES), f32)],
        [],
        name="gate",
        after=arrived(early) + [de_got, tgt_got],
        passed=[en_send, d_src_far],
    )
    cr = early[2:3]
    early = early[:2] + early[3:]
    en_got, src_got = to_core(en_send), to_core(d_src_far)
    enc_out, dec_out = place_home(homes, (bf16, bf16))
    sums_at = 2 * n_blk
    late = step(
        [
            state("x", en_keep, en_got, 0),
            state("y", de_keep, de_got, 0),
            (
                orders["x"] + more_dims,
                en_keep.shape[0] - sums_at,
                True,
                [(en_keep, sums_at), (en_got, sums_at)],
            ),
        ]
    )
    terms = spread_mid([(d_src_mid, src_got), (d_tgt_mid, tgt_got)])
    homes_back = homeward(
        call(
            lambda *refs: homes_kernel(2, *refs),
            [((2, tok, width), bf16)] * 2,
            held([d_src_own, src_got, d_tgt_own, tgt_got] + terms),
            name="homes",
        )
    )
    early = step(early)
    late = step(late + cr)
    late = step(late)
    late, cr = late[:3], late[3:]
    early = step(early, after=homes_back)
    late = step(late)
    early = finish(early + cr)
    (early_own,) = combine([(sum_of(early), bf16)])
    early_mats = gather(early_own)
    late = finish(late)
    own, vec = combine([(sum_of(late[:2]), bf16), (sum_of(late[2:]), f32)])
    mats = [own] + [to_bits(own, d_b, 0) for d_b in (2, 1, 3)]
    source_grad, target_grad = place_home(homes_back, (f32, f32))
    got = unpack(("up", "down", "up", "down", "attn"), early_mats)
    g_ef_up, g_ef_down, g_df_up, g_df_down, g_cr_in, g_cr_out = got
    df, cr, de, ef, en = 0, 8, 16, 24, 32
    vec_rows = [
        [en + 3],
        [en + 4],
        [en + 2],
        [en, ef],
        [en + 1, ef + 1],
        [ef + 3, ef + 4, ef + 5, ef + 6],
        [ef + 2],
        [de + 3],
        [de + 4],
        [de + 2],
        [cr + 3],
        [cr + 4],
        [cr + 2],
        [de, cr, df],
        [de + 1, cr + 1, df + 1],
        [df + 3, df + 4, df + 5, df + 6],
        [df + 2],
    ]
    wide = (3, 4, 13, 14)
    got = unpack(("attn", "attn"), mats, vec, vec_rows, wide)
    g_en_in, g_en_out, g_de_in, g_de_out = got[:4]
    vectors = [
        values if number in wide else values.reshape(-1) for number, values in enumerate(got[4:])
    ]
    return (
        enc_out,
        dec_out,
        source_grad,
        target_grad,
        g_en_in,
        vectors[0],
        vectors[1],
        g_en_out,
        vectors[2],
        vectors[3],
        vectors[4],
        g_ef_up,
        vectors[5],
        g_ef_down,
        vectors[6],
        g_de_in,
        vectors[7],
        vectors[8],
        g_de_out,
        vectors[9],
        g_cr_in,
        vectors[10],
        vectors[11],
        g_cr_out,
        vectors[12],
        vectors[13],
        vectors[14],
        g_df_up,
        vectors[15],
        g_df_down,
        vectors[16],
    )


def solution(mesh):
    rows = P("batch", "blk", None)
    lists = P("batch", None)
    by_row = P("blk", None)
    stacked = P(None, "blk", None)
    whole = P()
    return jax.shard_map(
        on_device,
        mesh=mesh,
        in_specs=(rows, rows, lists, lists, lists) + (whole,) * 27 + (rows,),
        out_specs=(rows, rows, rows, rows)
        + (stacked, whole, whole, by_row, whole, whole, whole, by_row, whole, by_row, whole)
        + (stacked, whole, whole, by_row, whole)
        + (stacked, whole, whole, by_row, whole, whole, whole, by_row, whole, by_row, whole),
        check_vma=False,
    )
```

```python
import math

import jax
import jax.numpy as jnp
from jax import lax
from jax.experimental import pallas as pl
from jax.experimental.pallas import tpu as pltpu
from jax.sharding import PartitionSpec as P

H = 8
LANES = 128
WORK = dict(segments=1, pack=1, enc_forward=10, dec_forward=6, cross_forward=16, cross_backward=11, ffn_backward=6, self_backward=11)
MATS = 4
negative = -1e30
bf16 = jnp.bfloat16
f32 = jnp.float32
ROW_BYTES = 20 * 1024
MOST_BYTES = 60 * 1024 * 1024


def nn(left, right):
    return lax.dot_general(left, right, (((1,), (0,)), ((), ())), preferred_element_type=f32)


def nt(left, right):
    return lax.dot_general(left, right, (((1,), (1,)), ((), ())), preferred_element_type=f32)


def tn(left, right):
    return lax.dot_general(left, right, (((0,), (0,)), ((), ())), preferred_element_type=f32)


def turned(values):
    return values.astype(f32).T


def norm_forward(rows):
    centred = rows - jnp.mean(rows, axis=-1, keepdims=True)
    spread = jnp.mean(centred * centred, axis=-1, keepdims=True)
    rstd = lax.rsqrt(spread + 1e-05)
    return centred * rstd, rstd


def norm_backward(dy, normed, rstd, gain):
    dn = dy * gain
    dr = (
        dn
        - jnp.mean(dn, axis=-1, keepdims=True)
        - normed * jnp.mean(dn * normed, axis=-1, keepdims=True)
    ) * rstd
    return dr, column_sum(dy * normed), column_sum(dy)


def column_sum(values):
    return jnp.sum(values, axis=0, keepdims=True)


def gelu_pair(values):
    bell = jnp.exp(-0.5 * values * values)
    t = 1.0 / (1.0 + (0.3275911 * math.sqrt(0.5)) * jnp.abs(values))
    poly = 0.5 * 1.061405429
    for number in (-1.453152027, 1.421413741, -0.284496736, 0.254829592):
        poly = poly * t + 0.5 * number
    tail = poly * t * bell
    share = jnp.where(values >= 0, 1.0 - tail, tail)
    return values * share, share + values * bell * (1.0 / math.sqrt(2.0 * math.pi))


class Layout:
    def __init__(self, table, keep, send, blocks, groups):
        self.table, self.keep, self.send = table, keep, send
        self.blocks, self.groups = blocks, groups

    def put(self, values, mat, group, block0=0, count=None):
        count = self.blocks if count is None else count
        low = values.astype(bf16)
        rows = low.shape[0] // count
        first, y_step = self.groups[group]
        rel = lax.bitwise_xor(self.table[0], mat)
        base = lax.bitwise_and(rel, 1) * y_step + group * 2 * self.blocks

        def fill(ref):
            for number in range(count):
                place = base + self.table[first + block0 + number]
                ref[place] = low[number * rows : (number + 1) * rows]

        pl.when(rel < 2)(lambda: fill(self.keep))
        pl.when(rel >= 2)(lambda: fill(self.send))


def head_masks(axis, shape, head_size):
    places = lax.broadcasted_iota(jnp.int32, shape, axis)
    return [places // head_size == number for number in range(LANES // head_size)]


def as_column(row):
    return jnp.broadcast_to(row, (LANES, row.shape[1])).T[:, 0:1]


def segments_kernel(tok, place, lists, far, segs):
    count = lists.shape[2]
    total = segs.shape[1]
    row = lambda number: jnp.where(
        place[0] == 1, lists[number, pl.ds(place[1], 1)], far[number, pl.ds(place[1], 1)]
    ).astype(f32)
    at_row = lax.broadcasted_iota(jnp.int32, (count, count), 0)
    at_col = lax.broadcasted_iota(jnp.int32, (count, count), 1)

    def ends(number):
        return jnp.sum(jnp.where(at_col <= at_row, row(number), 0.0), axis=1, keepdims=True)

    spots = jnp.concatenate(
        [
            lax.broadcasted_iota(jnp.int32, (1, tok), 1) + place[2 + number] * tok
            for number in range(total // tok)
        ],
        axis=1,
    ).astype(f32)
    src = jnp.sum((ends(0) <= spots).astype(f32), axis=0, keepdims=True)
    tgt = jnp.sum((ends(1) <= spots).astype(f32), axis=0, keepdims=True)
    partner = jnp.sum(jnp.where(at_col == at_row, row(2), 0.0), axis=1, keepdims=True)
    numbers = lax.broadcasted_iota(jnp.int32, (count, 1), 0).astype(f32)
    segs[0:1] = src
    segs[1:2] = tgt
    segs[2:3] = jnp.sum(jnp.where(numbers == tgt, partner, 0.0), axis=0, keepdims=True)
    segs[3:8] = jnp.zeros((5, total), f32)


def call_kernel(kernel, outs, args, scratch, name, after, passed, vmem_bytes):
    spaces = {"s": pltpu.SMEM, "v": pltpu.VMEM}
    before = len(args) + len(after)

    def body(*refs):
        made = refs[before + len(passed) :]
        kernel(*refs[: len(args)], *made[: len(outs)], *made[len(outs) + len(passed) :])

    cost = None
    if name in WORK:
        work = WORK[name]
        cost = pl.CostEstimate(
            flops=work * 10**9, bytes_accessed=work * 10**6, transcendentals=0
        )
    any_space = pl.BlockSpec(memory_space=pl.ANY)
    shapes = [jax.ShapeDtypeStruct(shape, kind) for shape, kind in outs]
    shapes += [jax.ShapeDtypeStruct(array.shape, array.dtype) for array in passed]
    return pl.pallas_call(
        body,
        out_shape=tuple(shapes),
        in_specs=[pl.BlockSpec(memory_space=spaces[mode]) for mode, _ in args]
        + [any_space] * (len(after) + len(passed)),
        out_specs=tuple(
            [pl.BlockSpec(memory_space=pltpu.VMEM)] * len(outs) + [any_space] * len(passed)
        ),
        scratch_shapes=list(scratch),
        input_output_aliases={before + at: len(outs) + at for at in range(len(passed))},
        compiler_params=pltpu.CompilerParams(vmem_limit_bytes=vmem_bytes),
        cost_estimate=cost,
        name=name,
    )(*[array for _, array in args], *after, *passed)


def keys_values(parts, w_input, b_value, k_out, v_out):
    at = 0
    for part in parts:
        rows = part.shape[0]
        piece = part[...]
        k_out[at : at + rows] = nn(piece, w_input[1]).astype(bf16)
        v_out[at : at + rows] = (nn(piece, w_input[2]) + b_value[...]).astype(bf16)
        at += rows


def attn_forward(parts, query, segs, seg_rows, weights, q_out, k_out, v_out, att_out, lse_out):
    w_input, b_query, b_value, w_out, b_out = weights
    own_rows, width = q_out.shape
    head_size = width // H
    keys_values(parts, w_input, b_value, k_out, v_out)
    xq = parts[0][0:own_rows] if query is None else query
    factor = 1.0 / math.sqrt(head_size)
    q = (nn(xq, w_input[0]) + b_query[...]).astype(bf16)
    q_out[...] = (q.astype(f32) * factor).astype(bf16)
    seg_query = as_column(segs[seg_rows[0] : seg_rows[0] + 1, 0:own_rows])
    bias = jnp.where(seg_query == segs[seg_rows[1] : seg_rows[1] + 1], 0.0, negative)
    masks = head_masks(1, (own_rows, LANES), head_size)
    lse_all = jnp.zeros((own_rows, LANES), f32)
    lane = lax.broadcasted_iota(jnp.int32, (own_rows, LANES), 1)
    for pair in range(width // LANES):
        cols = slice(pair * LANES, (pair + 1) * LANES)
        q_pair, k_pair, v_pair = q_out[:, cols], k_out[:, cols], v_out[:, cols]
        merged = None
        for number, mask in enumerate(masks):
            q_head = jnp.where(mask, q_pair, jnp.zeros_like(q_pair))
            scores = nt(q_head, k_pair) + bias
            peak = jnp.max(scores, axis=1, keepdims=True)
            weights = jnp.exp(scores - peak)
            total = jnp.sum(weights, axis=1, keepdims=True)
            out = nn(weights.astype(bf16), v_pair) * (1.0 / total)
            merged = out if merged is None else jnp.where(mask, out, merged)
            head = pair * len(masks) + number
            lse_all = jnp.where(lane == head, peak + jnp.log(total), lse_all)
        att_out[:, cols] = merged
    lse_out[...] = lse_all.T[0:H]
    branch = nn(att_out[...].astype(bf16), w_out[...]) + b_out[...]
    return branch + xq.astype(f32) if query is None else branch


def ffn_forward(values, weights, act_out, slope_out):
    w_up, b_up, w_down, b_down = weights
    width = values.shape[1]
    low = values.astype(bf16)
    total = values + b_down[...]
    for at in range(0, w_up.shape[1], width):
        cols = slice(at, at + width)
        act, slope = gelu_pair(nn(low, w_up[:, cols]) + b_up[:, cols])
        act_low = act.astype(bf16)
        act_out[:, cols] = act_low
        slope_out[:, cols] = slope.astype(bf16)
        total = total + nn(act_low, w_down[cols, :])
    return total


def ffn_backward(dr, low, act, slope, w_up, w_down, up, down, blocks, sums):
    width = dr.shape[1]
    d_ffn = dr.astype(bf16)
    sums.append(column_sum(d_ffn.astype(f32)))
    total = dr
    per_blk = w_down.shape[0] // blocks
    chunk = per_blk // MATS
    for number in range(MATS):
        at = number * width
        cols = slice(at, at + width)
        d_act = nt(d_ffn, w_down[cols, :])
        d_pre = (d_act * slope[:, cols].astype(f32)).astype(bf16)
        sums.append(column_sum(d_pre.astype(f32)))
        total = total + nt(d_pre, w_up[:, cols])
        up.put(tn(low, d_pre), number, 0)
        rows = tn(act[:, cols], d_ffn)
        for row in range(0, width, chunk):
            block, mat = (at + row) // per_blk, (at + row) % per_blk // chunk
            down.put(rows[row : row + chunk], mat, 1, block, 1)
    return total


def attn_backward(dr, xq, xk_parts, saved, segs, seg_rows, w_input, w_out, layout, group, buffers, sums):
    att, lse, q8, k, v = saved
    dk_buf, dv_buf, dq_buf = buffers
    own_rows, width = dr.shape
    head_size = width // H
    factor = 1.0 / math.sqrt(head_size)
    d_branch = dr.astype(bf16)
    att_rows = att[...]
    layout.put(tn(att_rows.astype(bf16), d_branch), 3, group)
    do_turned = nt(w_out[...], d_branch).astype(bf16)
    delta = jnp.sum((do_turned.astype(f32) * att_rows.T).reshape(H, head_size, own_rows), axis=1)
    lse_turned = lse[...]
    q_turned = turned(q8[...]).astype(bf16)
    seg_key = as_column(segs[seg_rows[1] : seg_rows[1] + 1])
    bias = jnp.where(seg_key == segs[seg_rows[0] : seg_rows[0] + 1, 0:own_rows], 0.0, negative)
    masks = head_masks(0, (LANES, own_rows), head_size)
    for pair in range(width // LANES):
        cols = slice(pair * LANES, (pair + 1) * LANES)
        k_pair, v_pair = k[:, cols], v[:, cols]
        k_turned = turned(k_pair).astype(bf16)
        q_pair, do_pair = q_turned[cols], do_turned[cols]
        dk_pair, dv_pair = None, None
        for number, mask in enumerate(masks):
            head = pair * len(masks) + number
            zero = jnp.zeros_like(q_pair)
            q_head = jnp.where(mask, q_pair, zero)
            do_head = jnp.where(mask, do_pair, zero)
            probs = jnp.exp(nn(k_pair, q_head) + bias - lse_turned[head : head + 1])
            d_prob = nn(v_pair, do_head)
            d_score = (probs * (d_prob - delta[head : head + 1])).astype(bf16)
            dv_term = nt(probs.astype(bf16), do_head)
            dk_term = nt(d_score, q_head)
            dv_pair = dv_term if dv_pair is None else dv_pair + dv_term
            dk_pair = dk_term if dk_pair is None else dk_pair + dk_term
            rows = slice(head * head_size, (head + 1) * head_size)
            dq_buf[rows] = nn(k_turned[number * head_size : (number + 1) * head_size], d_score)
        dk_buf[:, cols] = dk_pair.astype(bf16)
        dv_buf[:, cols] = dv_pair.astype(bf16)
    dq = (dq_buf[...].T * factor).astype(bf16)
    layout.put(tn(xq, dq), 0, group)
    dk, dv = dk_buf[...], dv_buf[...]
    grad_key, grad_value = None, None
    at = 0
    for part in xk_parts:
        rows = part.shape[0]
        piece = part[...]
        key_term, value_term = tn(piece, dk[at : at + rows]), tn(piece, dv[at : at + rows])
        grad_key = key_term if grad_key is None else grad_key + key_term
        grad_value = value_term if grad_value is None else grad_value + value_term
        at += rows
    layout.put(grad_key, 1, group)
    layout.put(grad_value, 2, group)
    sums += [
        column_sum(d_branch.astype(f32)),
        column_sum(dq.astype(f32)),
        column_sum(dv.astype(f32)),
        jnp.zeros((3, width), f32),
    ]
    return nt(dq, w_input[0]), nt(dk, w_input[1]) + nt(dv, w_input[2])


def add_up(parts, own_rows):
    total = parts[0][0:own_rows].astype(f32)
    for part in parts[1:]:
        total = total + part[0:own_rows].astype(f32)
    return total


def pack_kernel(*refs):
    at = 0
    for ref in refs[:-1]:
        refs[-1][at : at + ref.shape[0]] = ref[...]
        at += ref.shape[0]


def self_attn(parts, segs, seg_rows, weights, q, att, lse, norm_one, rstd_one, buffers):
    k, v = buffers
    rows = attn_forward(parts, None, segs, seg_rows, weights, q, k, v, att, lse)
    normed, rstd = norm_forward(rows)
    norm_one[...] = normed
    rstd_one[...] = rstd
    return normed


def enc_forward_kernel(seg_rows, *refs):
    near, far, segs, w_input, b_query, b_value, w_out, b_out = refs[:8]
    gains, shifts, w_up, b_up, w_down, b_down = refs[8:14]
    q, att, lse, norm_one, rstd_one, act, slope, norm_two, rstd_two, low, k, v = refs[14:]
    weights = (w_input, b_query, b_value, w_out, b_out)
    normed = self_attn(
        [near, far], segs, seg_rows, weights, q, att, lse, norm_one, rstd_one, (k, v)
    )
    values = normed * gains[0:1] + shifts[0:1]
    normed, rstd = norm_forward(ffn_forward(values, (w_up, b_up, w_down, b_down), act, slope))
    norm_two[...] = normed
    rstd_two[...] = rstd
    low[...] = (normed * gains[1:2] + shifts[1:2]).astype(bf16)


def dec_forward_kernel(seg_rows, *refs):
    near, far, segs, w_input, b_query, b_value, w_out, b_out = refs[:8]
    q, att, lse, norm_one, rstd_one, k, v = refs[8:]
    weights = (w_input, b_query, b_value, w_out, b_out)
    self_attn([near, far], segs, seg_rows, weights, q, att, lse, norm_one, rstd_one, (k, v))


def cross_forward_kernel(part_count, cot_count, seg_rows, blocks, groups, table, *refs):
    refs = list(refs)
    parts, refs = refs[:part_count], refs[part_count:]
    cots, refs = refs[:cot_count], refs[cot_count:]
    prev_norm, segs, w_input, b_query, b_value, w_out, b_out, gains, shifts = refs[:9]
    w_up, b_up, w_down, b_down = refs[9:13]
    q, k, v, att, lse, norm_two_out, rstd_two_out, d_second = refs[13:21]
    homes = refs[21:23]
    keep, send, vecs, act, slope = refs[23:]
    own_rows = prev_norm.shape[0]
    upper = prev_norm[...] * gains[0:1] + shifts[0:1]
    weights = (w_input, b_query, b_value, w_out, b_out)
    branch = attn_forward(
        parts, upper.astype(bf16), segs, seg_rows, weights, q, k, v, att, lse
    )
    norm_two, rstd_two = norm_forward(upper + branch)
    norm_two_out[...] = norm_two
    rstd_two_out[...] = rstd_two
    crossed = norm_two * gains[1:2] + shifts[1:2]
    norm_three, rstd_three = norm_forward(
        ffn_forward(crossed, (w_up, b_up, w_down, b_down), act, slope)
    )
    low = (norm_three * gains[2:3] + shifts[2:3]).astype(bf16)
    tok = own_rows // 2
    memory = parts[0][...]
    for number, home in enumerate(homes):
        home[0] = memory[number * tok : (number + 1) * tok]
        home[1] = low[number * tok : (number + 1) * tok]
    dy = jnp.concatenate([cot[...] for cot in cots], axis=0).astype(f32)
    sums = []
    dr, d_gain, d_shift = norm_backward(dy, norm_three, rstd_three, gains[2:3])
    sums += [d_gain, d_shift]
    layout = Layout(table, keep, send, blocks, groups)
    d_second[...] = ffn_backward(
        dr, crossed.astype(bf16), act, slope, w_up, w_down, layout, layout, blocks, sums
    )
    sums.append(jnp.zeros_like(d_gain))
    vecs[...] = jnp.concatenate(sums, axis=0)


def cross_backward_kernel(part_count, has_mid, seg_rows, blocks, groups, table, *refs):
    refs = list(refs)
    parts, refs = refs[:part_count], refs[part_count:]
    d_in, norm_two, rstd_two, prev_norm, gains, shifts = refs[:6]
    att, w_out, lse, q, k, v, segs, w_input = refs[6:14]
    refs = refs[14:]
    d_upper, d_own = refs[:2]
    refs = refs[2:]
    d_mid = refs.pop(0) if has_mid else None
    d_far, keep, send, vecs = refs[:4]
    buffers = refs[4:]
    own_rows = prev_norm.shape[0]
    sums = []
    dr, d_gain, d_shift = norm_backward(d_in[...], norm_two[...], rstd_two[...], gains[1:2])
    sums += [d_gain, d_shift]
    xq = (prev_norm[...] * gains[0:1] + shifts[0:1]).astype(bf16)
    layout = Layout(table, keep, send, blocks, groups)
    d_query, d_key = attn_backward(
        dr, xq, parts, (att, lse, q, k, v), segs, seg_rows, w_input, w_out, layout, 0, buffers, sums
    )
    keys = d_key.shape[0]
    d_upper[...] = dr + d_query
    d_own[...] = d_key[0:own_rows]
    if has_mid:
        d_mid[...] = d_key[own_rows : keys // 2].astype(bf16)
    d_far[...] = d_key[keys // 2 :].astype(bf16)
    vecs[...] = jnp.concatenate(sums, axis=0)


def ffn_backward_kernel(part_count, blocks, groups, table, *refs):
    parts, refs = refs[:part_count], refs[part_count:]
    norm_two, rstd_two, norm_one, gains, shifts, slope, w_down, act, w_up = refs[:9]
    d_out, keep, send, vecs = refs[9:]
    sums = []
    dy = add_up(parts, norm_one.shape[0])
    dr, d_gain, d_shift = norm_backward(dy, norm_two[...], rstd_two[...], gains[1:2])
    sums += [d_gain, d_shift]
    low = (norm_one[...] * gains[0:1] + shifts[0:1]).astype(bf16)
    layout = Layout(table, keep, send, blocks, groups)
    d_out[...] = ffn_backward(dr, low, act, slope, w_up, w_down, layout, layout, blocks, sums)
    sums.append(jnp.zeros_like(d_gain))
    vecs[...] = jnp.concatenate(sums, axis=0)


def self_backward_kernel(has_mid, vec_count, seg_rows, blocks, groups, table, segs, *refs):
    refs = list(refs)
    vecs_in, refs = refs[:vec_count], refs[vec_count:]
    d_in, norm_one, rstd_one, gains, att, w_out, lse, q, near, far, w_input, b_value = refs[:12]
    refs = refs[12:]
    d_own = refs.pop(0)
    mid = refs.pop(0) if has_mid else None
    far_out, keep, send = refs[:3]
    refs = refs[3:]
    vecs = None if vec_count else refs.pop(0)
    k, v = refs[:2]
    buffers = refs[2:]
    own_rows, width = norm_one.shape
    layout = Layout(table, keep, send, blocks, groups)
    sums = []
    dr, d_gain, d_shift = norm_backward(d_in[...], norm_one[...], rstd_one[...], gains[0:1])
    sums += [d_gain, d_shift]
    keys_values([near, far], w_input, b_value, k, v)
    xq = near[0:own_rows]
    d_query, d_key = attn_backward(
        dr, xq, [near, far], (att, lse, q, k, v), segs, seg_rows, w_input, w_out, layout, 0, buffers, sums
    )
    keys = d_key.shape[0]
    d_own[...] = dr + d_query + d_key[0:own_rows]
    if has_mid:
        mid[0] = d_key[own_rows : keys // 2].astype(bf16)
    far_out[0] = d_key[keys // 2 :].astype(bf16)
    if not vec_count:
        vecs[...] = jnp.concatenate(sums, axis=0)
        return
    all_sums = [vec[...] for vec in vecs_in] + sums
    more = keep.shape[0] - 2 * blocks
    rows = keep.shape[1]
    pad = more * rows - sum(piece.shape[0] for piece in all_sums)
    if pad:
        all_sums.append(jnp.zeros((pad, width), f32))
    all_sums = jnp.concatenate(all_sums, axis=0).astype(bf16)
    for number in range(more):
        keep[2 * blocks + number] = all_sums[number * rows : (number + 1) * rows]
        send[2 * blocks + number] = all_sums[number * rows : (number + 1) * rows]


def middle_kernel(own_rows, pairs, *refs):
    for number, out in enumerate(refs[2 * pairs :]):
        mine = slice(number * own_rows, (number + 1) * own_rows)
        far = slice((number + 1) * own_rows, (number + 2) * own_rows)
        for at in range(pairs):
            total = refs[2 * at][0, mine].astype(f32) + refs[2 * at + 1][0, far].astype(f32)
            out[at] = total.astype(bf16)


def homes_kernel(count, *refs):
    homes = refs[-2:]
    tok = homes[0].shape[1]
    for number in range(count):
        total = refs[2 * number][...] + refs[2 * number + 1][0, 0 : 2 * tok].astype(f32)
        for term in refs[2 * count : -2]:
            total = total + term[number].astype(f32)
        total = total.astype(bf16)
        for d_lo, home in enumerate(homes):
            home[number] = total[d_lo * tok : (d_lo + 1) * tok]


def gate_kernel(out):
    out[...] = jnp.zeros_like(out)


def combine_kernel(count, plan, *refs):
    inputs, outputs = refs[:count], refs[count:]
    for out, segments in zip(outputs, plan):
        at = 0
        for chunks, terms in segments:
            total = None
            for number, first in terms:
                term = inputs[number][first : first + chunks].astype(f32)
                total = term if total is None else total + term
            out[at : at + chunks] = total.astype(out.dtype)
            at += chunks


def place_kernel(table, got_one, got_two, *outs):
    for number, out in enumerate(outs):
        out[table[0]] = got_one[number].astype(out.dtype)
        out[lax.bitwise_xor(table[0], 1)] = got_two[number].astype(out.dtype)


def unpack_kernel(kinds, vec_rows, table, *refs):
    refs = list(refs)
    mats = refs[:MATS]
    refs = refs[MATS:]
    vec = refs.pop(0) if vec_rows else None
    scratch = refs.pop()
    for rel in range(MATS):
        scratch[lax.bitwise_xor(table[0], rel)] = mats[rel][...].astype(f32)
    width = mats[0].shape[2]
    rows = mats[0].shape[1]
    for group, kind in enumerate(kinds):
        if kind == "attn":
            w_input, w_out = refs.pop(0), refs.pop(0)
            for mat in range(MATS - 1):
                w_input[mat] = scratch[mat, group]
            w_out[...] = scratch[MATS - 1, group]
        elif kind == "up":
            out = refs.pop(0)
            for mat in range(MATS):
                out[:, mat * width : (mat + 1) * width] = scratch[mat, group]
        else:
            out = refs.pop(0)
            for mat in range(MATS):
                out[mat * rows : (mat + 1) * rows] = scratch[mat, group]
    if vec_rows:
        sums = jnp.concatenate([vec[number] for number in range(vec.shape[0])], axis=0).astype(f32)
        for out, numbers in zip(refs, vec_rows):
            for at, number in enumerate(numbers):
                if out.shape[0] == 1:
                    out[:, at * width : (at + 1) * width] = sums[number : number + 1]
                else:
                    out[at : at + 1] = sums[number : number + 1]


def on_device(
    source,
    target,
    src_lengths,
    tgt_lengths,
    pairing,
    enc_w_input,
    enc_b_query,
    enc_b_value,
    enc_w_out,
    enc_b_out,
    enc_gains,
    enc_shifts,
    enc_w_up,
    enc_b_up,
    enc_w_down,
    enc_b_down,
    dec_w_input,
    dec_b_query,
    dec_b_value,
    dec_w_out,
    dec_b_out,
    cross_w_input,
    cross_b_query,
    cross_b_value,
    cross_w_out,
    cross_b_out,
    dec_gains,
    dec_shifts,
    dec_w_up,
    dec_b_up,
    dec_w_down,
    dec_b_down,
    cotangent,
):
    streams, tok, width = source.shape
    n_batch, n_blk = lax.axis_size("batch"), lax.axis_size("blk")
    half = n_blk // 2
    mids = n_blk // 4
    own_rows = 2 * tok
    total_rows = n_blk * tok
    near_rows = total_rows // 2
    chunk_rows = width // n_blk
    ff = enc_w_up.shape[1]
    b, i = lax.axis_index("batch"), lax.axis_index("blk")
    core, y_bit = b & 1, (b >> 1) & 1
    hi, mid, lo = i // half, (i % half) // 2, i & 1

    def move(values, where):
        pairs = []
        for from_b in range(n_batch):
            for from_i in range(n_blk):
                to_b, to_i = where(from_b, from_i)
                pairs.append((from_b * n_blk + from_i, to_b * n_blk + to_i))
        return lax.ppermute(values, ("batch", "blk"), pairs)

    def regroup(values, d_mid, d_lo):
        def where(fb, fi):
            f_hi, f_mid, f_lo, f_core = fi // half, (fi % half) // 2, fi & 1, fb & 1
            return ((fb & ~1) | f_hi, f_core * half + (f_mid ^ d_mid) * 2 + (f_lo ^ d_lo))

        return move(values, where)

    to_bits = lambda values, d_b, d_i: move(values, lambda fb, fi: (fb ^ d_b, fi ^ d_i))
    to_core = lambda values: to_bits(values, 1, 0)
    to_mid = lambda values, d_mid: to_bits(values, 0, 2 * d_mid)

    last = []

    def call(kernel, outs, args, scratch=(), name=None, passed=(), after=()):
        vmem_bytes = min(total_rows * ROW_BYTES, MOST_BYTES)
        held_back = last[-1:] + list(after)
        got = call_kernel(kernel, outs, args, scratch, name, held_back, list(passed), vmem_bytes)
        last.append(min(got[: len(outs)], key=lambda array: array.size))
        return got

    bits = n_blk.bit_length() - 1
    batch_bits = n_batch.bit_length() - 1
    more_dims = [(1 << bit,) for bit in range(2, batch_bits)]
    rest = list(range(2, bits))
    orders = {
        "x": [0, "y", 1] + rest,
        "y": ["y", 0, 1] + rest,
        "z": [1] + rest + ["y", 0],
    }

    def group_of(kind):
        at = list(orders).index(kind)
        return (1 + at * n_blk, 1 << (bits - orders[kind].index("y")))

    def places_of(order):
        step = {name: 1 << (bits - at) for at, name in enumerate(order)}
        return [
            sum((((number ^ i) >> bit) & 1) * step[bit] for bit in range(bits))
            for number in range(n_blk)
        ]

    all_places = [place for order in orders.values() for place in places_of(order)]
    mat_table = jnp.stack([2 * core + y_bit] + all_places).astype(jnp.int32)

    def state(kind, keep, got, group):
        first = group * 2 * n_blk
        return (orders[kind] + more_dims, 1, False, [(keep, first), (got, first)])

    runs = [
        (core ^ d_core) * half + (mid ^ d_mid) * 2 + (lo ^ d_lo)
        for d_core in range(2)
        for d_mid in range(mids)
        for d_lo in range(2)
    ]
    place_table = jnp.stack([(hi == core).astype(jnp.int32), lo] + runs).astype(jnp.int32)
    lo_table = jnp.stack([lo, lo]).astype(jnp.int32)
    row = lambda values: values.reshape(1, -1)

    def stream_of(values, number):
        return lax.dynamic_index_in_dim(values, number, 0, keepdims=False)

    def near_parts(values):
        return [
            regroup(stream_of(values, lo ^ d_lo), d_mid, d_lo)
            for d_mid in range(mids)
            for d_lo in range(2)
        ]

    held = lambda arrays: [("v", array) for array in arrays]
    packed = lambda chunks: ((chunks, chunk_rows, width), bf16)
    rows_f32 = ((own_rows, width), f32)
    rows_bf16 = ((own_rows, width), bf16)
    one_f32 = ((own_rows, 1), f32)
    lse_shape = ((H, own_rows), f32)
    all_keys = ((total_rows, width), bf16)
    vec_shape = ((8, width), f32)
    has_mid = near_rows > own_rows
    key_buffers = [pltpu.VMEM(*all_keys), pltpu.VMEM(*all_keys)]
    back_buffers = key_buffers + [pltpu.VMEM((width, own_rows), f32)]
    def pack(parts):
        return call(pack_kernel, [((near_rows, width), bf16)], held(parts), name="pack")[0]

    src_parts = near_parts(source)
    tgt_parts = near_parts(target)
    cot_parts = [regroup(stream_of(cotangent, lo ^ d_lo), 0, d_lo) for d_lo in range(2)]
    lists = jnp.stack([src_lengths, tgt_lengths, pairing])
    (segs,) = call(
        lambda *refs: segments_kernel(tok, *refs),
        [((8, total_rows), f32)],
        [("s", place_table)] + held([lists, to_core(lists)]),
        name="segments",
    )
    src_rows, tgt_rows, pair_rows = (0, 0), (1, 1), (2, 0)
    src_near = pack(src_parts)
    src_far = to_core(src_near)

    def spread_mid(pairs, after=()):
        if not has_mid:
            return []
        totals = call(
            lambda *refs: middle_kernel(own_rows, len(pairs), *refs),
            [((len(pairs), own_rows, width), bf16)] * (mids - 1),
            held([array for pair in pairs for array in pair]),
            name="middle",
            after=after,
        )
        return [to_mid(total, d_mid) for d_mid, total in enumerate(totals, 1)]

    def homeward(homes):
        return [regroup(home, 0, d_lo) for d_lo, home in enumerate(homes)]

    def place_home(got, kinds, passed=()):
        outs = [((streams, tok, width), kind) for kind in kinds]
        return call(
            place_kernel, outs, [("s", lo_table)] + held(got), name="place", passed=passed
        )

    def combine(plan_outs, passed=(), after=()):
        arrays, index, plan, outs = [], {}, [], []
        for segments, kind in plan_outs:
            rows = []
            for chunks, terms in segments:
                named = []
                for array, first in terms:
                    if id(array) not in index:
                        index[id(array)] = len(arrays)
                        arrays.append(array)
                    named.append((index[id(array)], first))
                rows.append((chunks, named))
            plan.append(rows)
            outs.append(((sum(chunks for chunks, _ in rows), chunk_rows, width), kind))
        return call(
            lambda *refs: combine_kernel(len(arrays), plan, *refs),
            outs,
            held(arrays),
            name="combine",
            passed=passed,
            after=after,
        )

    def offset(name):
        if name == "y":
            return (2, 0)
        if isinstance(name, tuple):
            return (name[0], 0)
        return (0, 1 << name)

    def step(states, passed=(), after=()):
        mine, away, found = [], {}, []
        sizes = {}
        for left, chunks, whole, terms in states:
            if not left:
                found.append((left, chunks, whole, terms, None, None))
                continue
            name, rest = left[0], left[1:]
            full = whole or isinstance(name, tuple)
            count = chunks << (0 if whole else sum(not isinstance(dim, tuple) for dim in rest))
            own_at = sum(n for n, _ in mine)
            mine.append((count, terms))
            segments = away.setdefault(name, [])
            far_at = sum(n for n, _ in segments)
            start = 0 if full else count
            segments.append((count, [(array, first + start) for array, first in terms]))
            found.append((rest, chunks, whole, own_at, name, far_at))
        plan = [(mine, bf16)] + [(segments, bf16) for segments in away.values()]
        arrays = combine(plan, passed, after)
        got = {}
        for name, array in zip(away, arrays[1:]):
            got[name] = to_bits(array, *offset(name))
        stepped = []
        for rest, chunks, whole, own_at, name, far_at in found:
            terms = own_at if name is None else [(arrays[0], own_at), (got[name], far_at)]
            stepped.append((rest, chunks, whole, terms))
        return stepped + list(arrays[len(plan) :])

    def finish(states):
        while any(left for left, _, _, _ in states):
            states = step(states)
        return states

    def arrived(states):
        return [array for _, _, _, terms in states for array, _ in terms[1:]]

    def sum_of(states):
        return [(chunks, terms) for _, chunks, _, terms in states]

    def attn_args(w_input, b_query, b_value, w_out, b_out):
        return held([w_input, row(b_query), row(b_value), w_out, row(b_out)])

    def ffn_args(w_up, b_up, w_down, b_down):
        return held([w_up, row(b_up), w_down, row(b_down)])

    enc_q, enc_att, enc_lse, enc_n1, enc_r1, enc_act, enc_slope, enc_n2, enc_r2, memory = call(
        lambda *refs: enc_forward_kernel(src_rows, *refs),
        [rows_bf16, rows_f32, lse_shape, rows_f32, one_f32]
        + [((own_rows, ff), bf16), ((own_rows, ff), bf16), rows_f32, one_f32, rows_bf16],
        held([src_near, src_far, segs])
        + attn_args(enc_w_input, enc_b_query, enc_b_value, enc_w_out, enc_b_out)
        + held([enc_gains, enc_shifts])
        + ffn_args(enc_w_up, enc_b_up, enc_w_down, enc_b_down),
        scratch=key_buffers,
        name="enc_forward",
    )
    ffn_groups = [group_of("x"), group_of("y")]
    places = [(d_core, d_mid) for d_core in range(2) for d_mid in range(mids)]
    mem_parts = [memory] + [
        to_bits(memory, d_core, 2 * d_mid) for d_core, d_mid in places[1:]
    ]
    tgt_near = pack(tgt_parts)
    tgt_far = to_core(tgt_near)
    dec_q, dec_att, dec_lse, dec_n1, dec_r1 = call(
        lambda *refs: dec_forward_kernel(tgt_rows, *refs),
        [rows_bf16, rows_f32, lse_shape, rows_f32, one_f32],
        held([tgt_near, tgt_far, segs])
        + attn_args(dec_w_input, dec_b_query, dec_b_value, dec_w_out, dec_b_out),
        scratch=key_buffers,
        name="dec_forward",
    )

    got = call(
        lambda *refs: cross_forward_kernel(
            len(mem_parts), len(cot_parts), pair_rows, n_blk, ffn_groups, *refs
        ),
        [rows_bf16, all_keys, all_keys, rows_f32, lse_shape, rows_f32, one_f32, rows_f32]
        + [((2, tok, width), bf16)] * 2
        + [packed(4 * n_blk)] * 2
        + [vec_shape],
        [("s", mat_table)]
        + held(mem_parts + cot_parts + [dec_n1, segs])
        + attn_args(cross_w_input, cross_b_query, cross_b_value, cross_w_out, cross_b_out)
        + held([dec_gains, dec_shifts])
        + ffn_args(dec_w_up, dec_b_up, dec_w_down, dec_b_down),
        scratch=[pltpu.VMEM((own_rows, ff), bf16), pltpu.VMEM((own_rows, ff), bf16)],
        name="cross_forward",
    )
    cr_q, cr_k, cr_v, cr_att, cr_lse, dec_n2, dec_r2, d_second = got[:8]
    homes = homeward(got[8:10])
    df_keep, df_send, df_vec = got[10:]
    df_got = to_core(df_send)
    mid_shape = [((near_rows - own_rows, width), bf16)] if has_mid else []
    got = list(
        call(
            lambda *refs: cross_backward_kernel(
                len(mem_parts), has_mid, pair_rows, n_blk, [group_of("z")], *refs
            ),
            [rows_f32, rows_f32]
            + mid_shape
            + [((near_rows, width), bf16)]
            + [packed(2 * n_blk)] * 2
            + [vec_shape],
            [("s", mat_table)]
            + held(mem_parts)
            + held([d_second, dec_n2, dec_r2, dec_n1, dec_gains, dec_shifts])
            + held([cr_att, cross_w_out, cr_lse, cr_q, cr_k, cr_v, segs, cross_w_input]),
            scratch=back_buffers,
            name="cross_backward",
        )
    )
    d_upper, d_mem_own = got[:2]
    d_mem_mid = got[2][None] if has_mid else None
    d_mem_far, cr_keep, cr_send, cr_vec = got[2 + len(mid_shape) :]
    df = step([state("x", df_keep, df_got, 0), state("y", df_keep, df_got, 1)])
    mem_got = to_core(d_mem_far[None])
    mem_terms = [mem_got[0]] + [term[0] for term in spread_mid([(d_mem_mid, mem_got)])]
    cr_got = to_core(cr_send)

    d_first, ef_keep, ef_send, ef_vec = call(
        lambda *refs: ffn_backward_kernel(1 + len(mem_terms), n_blk, ffn_groups, *refs),
        [rows_f32] + [packed(4 * n_blk)] * 2 + [vec_shape],
        [("s", mat_table)]
        + held([d_mem_own] + mem_terms)
        + held([enc_n2, enc_r2, enc_n1, enc_gains, enc_shifts])
        + held([enc_slope, enc_w_down, enc_act, enc_w_up]),
        name="ffn_backward",
    )
    _, ef_send = call(
        gate_kernel, [((8, LANES), f32)], [], name="gate", after=arrived(df), passed=[ef_send]
    )
    ef_got = to_core(ef_send)
    early = step(
        [
            state("x", ef_keep, ef_got, 0),
            state("y", ef_keep, ef_got, 1),
            state("z", cr_keep, cr_got, 0),
        ]
    )

    def self_backward(d_in, saved, seg_rows, kind, vecs_in=()):
        more = -(-8 * (len(vecs_in) + 1) // chunk_rows) if vecs_in else 0
        got = call(
            lambda *refs: self_backward_kernel(
                has_mid, len(vecs_in), seg_rows, n_blk, [group_of(kind)], *refs
            ),
            [rows_f32]
            + [((1,) + shape, kind) for shape, kind in mid_shape]
            + [((1, near_rows, width), bf16)]
            + [packed(2 * n_blk + more)] * 2
            + ([] if vecs_in else [vec_shape]),
            [("s", mat_table)] + held([segs] + list(vecs_in) + [d_in] + saved),
            scratch=key_buffers + back_buffers,
            name="self_backward",
        )
        got = list(got)
        if not has_mid:
            got.insert(1, None)
        return got

    d_tgt_own, d_tgt_mid, d_tgt_far, de_keep, de_send, de_vec = self_backward(
        d_upper,
        [dec_n1, dec_r1, dec_gains, dec_att, dec_w_out, dec_lse, dec_q]
        + [tgt_near, tgt_far, dec_w_input, row(dec_b_value)],
        tgt_rows,
        "y",
    )
    *early, de_send, d_tgt_far = step(early + df, passed=[de_send, d_tgt_far], after=homes)
    de_got, tgt_got = to_core(de_send), to_core(d_tgt_far)
    d_src_own, d_src_mid, d_src_far, en_keep, en_send = self_backward(
        d_first,
        [enc_n1, enc_r1, enc_gains, enc_att, enc_w_out, enc_lse, enc_q]
        + [src_near, src_far, enc_w_input, row(enc_b_value)],
        src_rows,
        "x",
        [df_vec, cr_vec, de_vec, ef_vec],
    )

    def gather(own):
        side = to_bits(own, 2, 0)
        return [own, side, to_core(own), to_core(side)]

    def unpack(kinds, mats, vec=None, vec_rows=(), wide=()):
        outs = []
        for kind in kinds:
            if kind == "attn":
                outs += [((MATS - 1, chunk_rows, width), f32), ((chunk_rows, width), f32)]
            elif kind == "up":
                outs.append(((chunk_rows, MATS * width), f32))
            else:
                outs.append(((MATS * chunk_rows, width), f32))
        for number, numbers in enumerate(vec_rows):
            shape = (len(numbers), width) if number in wide else (1, len(numbers) * width)
            outs.append((shape, f32))
        return call(
            lambda *refs: unpack_kernel(kinds, vec_rows, *refs),
            outs,
            [("s", mat_table)] + held(list(mats) + ([vec] if vec_rows else [])),
            scratch=[pltpu.VMEM((MATS,) + mats[0].shape, f32)],
            name="unpack",
        )

    ef, cr, df = early[:2], early[2:3], early[3:]
    *df, en_send, d_src_far = step(
        df, passed=[en_send, d_src_far], after=arrived(ef + cr) + [de_got, tgt_got]
    )
    en_got, src_got = to_core(en_send), to_core(d_src_far)
    sums_at = 2 * n_blk
    late = step(
        [
            state("x", en_keep, en_got, 0),
            state("y", de_keep, de_got, 0),
            (
                orders["x"] + more_dims,
                en_keep.shape[0] - sums_at,
                True,
                [(en_keep, sums_at), (en_got, sums_at)],
            ),
        ]
        + cr
    )
    terms = spread_mid([(d_src_mid, src_got), (d_tgt_mid, tgt_got)], arrived(df))
    enc_out, dec_out = place_home(homes, (bf16, bf16))
    ef = step(ef)
    late = step(late)
    homes_back = homeward(
        call(
            lambda *refs: homes_kernel(2, *refs),
            [((2, tok, width), bf16)] * 2,
            held([d_src_own, src_got, d_tgt_own, tgt_got] + terms),
            name="homes",
        )
    )
    late, cr = late[:3], late[3:]
    late = step(late)
    early = step(ef + df, after=homes_back)
    late = step(late)
    early = finish(early + cr)
    (early_own,) = combine([(sum_of(early), bf16)])
    early_mats = gather(early_own)
    late = finish(late)
    own, vec = combine([(sum_of(late[:2]), bf16), (sum_of(late[2:]), f32)])
    mats = [own] + [to_bits(own, d_b, 0) for d_b in (2, 1, 3)]
    source_grad, target_grad = place_home(homes_back, (f32, f32))
    got = unpack(("up", "down", "up", "down", "attn"), early_mats)
    g_ef_up, g_ef_down, g_df_up, g_df_down, g_cr_in, g_cr_out = got
    df, cr, de, ef, en = 0, 8, 16, 24, 32
    vec_rows = [
        [en + 3],
        [en + 4],
        [en + 2],
        [en, ef],
        [en + 1, ef + 1],
        [ef + 3, ef + 4, ef + 5, ef + 6],
        [ef + 2],
        [de + 3],
        [de + 4],
        [de + 2],
        [cr + 3],
        [cr + 4],
        [cr + 2],
        [de, cr, df],
        [de + 1, cr + 1, df + 1],
        [df + 3, df + 4, df + 5, df + 6],
        [df + 2],
    ]
    wide = (3, 4, 13, 14)
    got = unpack(("attn", "attn"), mats, vec, vec_rows, wide)
    g_en_in, g_en_out, g_de_in, g_de_out = got[:4]
    vectors = [
        values if number in wide else values.reshape(-1) for number, values in enumerate(got[4:])
    ]
    return (
        enc_out,
        dec_out,
        source_grad,
        target_grad,
        g_en_in,
        vectors[0],
        vectors[1],
        g_en_out,
        vectors[2],
        vectors[3],
        vectors[4],
        g_ef_up,
        vectors[5],
        g_ef_down,
        vectors[6],
        g_de_in,
        vectors[7],
        vectors[8],
        g_de_out,
        vectors[9],
        g_cr_in,
        vectors[10],
        vectors[11],
        g_cr_out,
        vectors[12],
        vectors[13],
        vectors[14],
        g_df_up,
        vectors[15],
        g_df_down,
        vectors[16],
    )


def solution(mesh):
    rows = P("batch", "blk", None)
    lists = P("batch", None)
    by_row = P("blk", None)
    stacked = P(None, "blk", None)
    whole = P()
    return jax.shard_map(
        on_device,
        mesh=mesh,
        in_specs=(rows, rows, lists, lists, lists) + (whole,) * 27 + (rows,),
        out_specs=(rows, rows, rows, rows)
        + (stacked, whole, whole, by_row, whole, whole, whole, by_row, whole, by_row, whole)
        + (stacked, whole, whole, by_row, whole)
        + (stacked, whole, whole, by_row, whole, whole, whole, by_row, whole, by_row, whole),
        check_vma=False,
    )
```

```python
import math

import jax
import jax.numpy as jnp
from jax import lax
from jax.experimental import pallas as pl
from jax.experimental.pallas import tpu as pltpu
from jax.sharding import PartitionSpec as P

H = 8
LANES = 128
WORK = dict(segments=2, pack=3, enc_forward=20, dec_forward=12, cross_forward=24, cross_backward=11, ffn_backward=6, self_backward=11)
MATS = 4
negative = -1e30
bf16 = jnp.bfloat16
f32 = jnp.float32
ROW_BYTES = 20 * 1024
MOST_BYTES = 60 * 1024 * 1024


def nn(left, right):
    return lax.dot_general(left, right, (((1,), (0,)), ((), ())), preferred_element_type=f32)


def nt(left, right):
    return lax.dot_general(left, right, (((1,), (1,)), ((), ())), preferred_element_type=f32)


def tn(left, right):
    return lax.dot_general(left, right, (((0,), (0,)), ((), ())), preferred_element_type=f32)


def turned(values):
    return values.astype(f32).T


def norm_forward(rows):
    centred = rows - jnp.mean(rows, axis=-1, keepdims=True)
    spread = jnp.mean(centred * centred, axis=-1, keepdims=True)
    rstd = lax.rsqrt(spread + 1e-05)
    return centred * rstd, rstd


def norm_backward(dy, normed, rstd, gain):
    dn = dy * gain
    dr = (
        dn
        - jnp.mean(dn, axis=-1, keepdims=True)
        - normed * jnp.mean(dn * normed, axis=-1, keepdims=True)
    ) * rstd
    return dr, column_sum(dy * normed), column_sum(dy)


def column_sum(values):
    return jnp.sum(values, axis=0, keepdims=True)


def gelu_pair(values):
    bell = jnp.exp(-0.5 * values * values)
    t = 1.0 / (1.0 + (0.3275911 * math.sqrt(0.5)) * jnp.abs(values))
    poly = 0.5 * 1.061405429
    for number in (-1.453152027, 1.421413741, -0.284496736, 0.254829592):
        poly = poly * t + 0.5 * number
    tail = poly * t * bell
    share = jnp.where(values >= 0, 1.0 - tail, tail)
    return values * share, share + values * bell * (1.0 / math.sqrt(2.0 * math.pi))


class Layout:
    def __init__(self, table, keep, send, blocks, groups):
        self.table, self.keep, self.send = table, keep, send
        self.blocks, self.groups = blocks, groups

    def put(self, values, mat, group, block0=0, count=None):
        count = self.blocks if count is None else count
        low = values.astype(bf16)
        rows = low.shape[0] // count
        first, y_step = self.groups[group]
        rel = lax.bitwise_xor(self.table[0], mat)
        base = lax.bitwise_and(rel, 1) * y_step + group * 2 * self.blocks

        def fill(ref):
            for number in range(count):
                place = base + self.table[first + block0 + number]
                ref[place] = low[number * rows : (number + 1) * rows]

        pl.when(rel < 2)(lambda: fill(self.keep))
        pl.when(rel >= 2)(lambda: fill(self.send))


def head_masks(axis, shape, head_size):
    places = lax.broadcasted_iota(jnp.int32, shape, axis)
    return [places // head_size == number for number in range(LANES // head_size)]


def as_column(row):
    return jnp.broadcast_to(row, (LANES, row.shape[1])).T[:, 0:1]


def segments_kernel(tok, place, lists, far, segs):
    count = lists.shape[2]
    total = segs.shape[1]
    row = lambda number: jnp.where(
        place[0] == 1, lists[number, pl.ds(place[1], 1)], far[number, pl.ds(place[1], 1)]
    ).astype(f32)
    at_row = lax.broadcasted_iota(jnp.int32, (count, count), 0)
    at_col = lax.broadcasted_iota(jnp.int32, (count, count), 1)

    def ends(number):
        return jnp.sum(jnp.where(at_col <= at_row, row(number), 0.0), axis=1, keepdims=True)

    spots = jnp.concatenate(
        [
            lax.broadcasted_iota(jnp.int32, (1, tok), 1) + place[2 + number] * tok
            for number in range(total // tok)
        ],
        axis=1,
    ).astype(f32)
    src = jnp.sum((ends(0) <= spots).astype(f32), axis=0, keepdims=True)
    tgt = jnp.sum((ends(1) <= spots).astype(f32), axis=0, keepdims=True)
    partner = jnp.sum(jnp.where(at_col == at_row, row(2), 0.0), axis=1, keepdims=True)
    numbers = lax.broadcasted_iota(jnp.int32, (count, 1), 0).astype(f32)
    segs[0:1] = src
    segs[1:2] = tgt
    segs[2:3] = jnp.sum(jnp.where(numbers == tgt, partner, 0.0), axis=0, keepdims=True)
    segs[3:8] = jnp.zeros((5, total), f32)


def call_kernel(kernel, outs, args, scratch, name, after, passed, vmem_bytes):
    spaces = {"s": pltpu.SMEM, "v": pltpu.VMEM}
    before = len(args) + len(after)

    def body(*refs):
        made = refs[before + len(passed) :]
        kernel(*refs[: len(args)], *made[: len(outs)], *made[len(outs) + len(passed) :])

    cost = None
    if name in WORK:
        work = WORK[name]
        cost = pl.CostEstimate(
            flops=work * 10**9, bytes_accessed=work * 10**6, transcendentals=0
        )
    any_space = pl.BlockSpec(memory_space=pl.ANY)
    shapes = [jax.ShapeDtypeStruct(shape, kind) for shape, kind in outs]
    shapes += [jax.ShapeDtypeStruct(array.shape, array.dtype) for array in passed]
    return pl.pallas_call(
        body,
        out_shape=tuple(shapes),
        in_specs=[pl.BlockSpec(memory_space=spaces[mode]) for mode, _ in args]
        + [any_space] * (len(after) + len(passed)),
        out_specs=tuple(
            [pl.BlockSpec(memory_space=pltpu.VMEM)] * len(outs) + [any_space] * len(passed)
        ),
        scratch_shapes=list(scratch),
        input_output_aliases={before + at: len(outs) + at for at in range(len(passed))},
        compiler_params=pltpu.CompilerParams(vmem_limit_bytes=vmem_bytes),
        cost_estimate=cost,
        name=name,
    )(*[array for _, array in args], *after, *passed)


def keys_values(parts, w_input, b_value, k_out, v_out):
    at = 0
    for part in parts:
        rows = part.shape[0]
        piece = part[...]
        k_out[at : at + rows] = nn(piece, w_input[1]).astype(bf16)
        v_out[at : at + rows] = (nn(piece, w_input[2]) + b_value[...]).astype(bf16)
        at += rows


def attn_forward(parts, query, segs, seg_rows, weights, q_out, k_out, v_out, att_out, lse_out):
    w_input, b_query, b_value, w_out, b_out = weights
    own_rows, width = q_out.shape
    head_size = width // H
    keys_values(parts, w_input, b_value, k_out, v_out)
    xq = parts[0][0:own_rows] if query is None else query
    factor = 1.0 / math.sqrt(head_size)
    q = (nn(xq, w_input[0]) + b_query[...]).astype(bf16)
    q_out[...] = (q.astype(f32) * factor).astype(bf16)
    seg_query = as_column(segs[seg_rows[0] : seg_rows[0] + 1, 0:own_rows])
    bias = jnp.where(seg_query == segs[seg_rows[1] : seg_rows[1] + 1], 0.0, negative)
    masks = head_masks(1, (own_rows, LANES), head_size)
    lse_all = jnp.zeros((own_rows, LANES), f32)
    lane = lax.broadcasted_iota(jnp.int32, (own_rows, LANES), 1)
    for pair in range(width // LANES):
        cols = slice(pair * LANES, (pair + 1) * LANES)
        q_pair, k_pair, v_pair = q_out[:, cols], k_out[:, cols], v_out[:, cols]
        merged = None
        for number, mask in enumerate(masks):
            q_head = jnp.where(mask, q_pair, jnp.zeros_like(q_pair))
            scores = nt(q_head, k_pair) + bias
            peak = jnp.max(scores, axis=1, keepdims=True)
            weights = jnp.exp(scores - peak)
            total = jnp.sum(weights, axis=1, keepdims=True)
            out = nn(weights.astype(bf16), v_pair) * (1.0 / total)
            merged = out if merged is None else jnp.where(mask, out, merged)
            head = pair * len(masks) + number
            lse_all = jnp.where(lane == head, peak + jnp.log(total), lse_all)
        att_out[:, cols] = merged
    lse_out[...] = lse_all.T[0:H]
    branch = nn(att_out[...].astype(bf16), w_out[...]) + b_out[...]
    return branch + xq.astype(f32) if query is None else branch


def ffn_forward(values, weights, act_out, slope_out):
    w_up, b_up, w_down, b_down = weights
    width = values.shape[1]
    low = values.astype(bf16)
    total = values + b_down[...]
    for at in range(0, w_up.shape[1], width):
        cols = slice(at, at + width)
        act, slope = gelu_pair(nn(low, w_up[:, cols]) + b_up[:, cols])
        act_low = act.astype(bf16)
        act_out[:, cols] = act_low
        slope_out[:, cols] = slope.astype(bf16)
        total = total + nn(act_low, w_down[cols, :])
    return total


def ffn_backward(dr, low, act, slope, w_up, w_down, up, down, blocks, sums):
    width = dr.shape[1]
    d_ffn = dr.astype(bf16)
    sums.append(column_sum(d_ffn.astype(f32)))
    total = dr
    per_blk = w_down.shape[0] // blocks
    chunk = per_blk // MATS
    for number in range(MATS):
        at = number * width
        cols = slice(at, at + width)
        d_act = nt(d_ffn, w_down[cols, :])
        d_pre = (d_act * slope[:, cols].astype(f32)).astype(bf16)
        sums.append(column_sum(d_pre.astype(f32)))
        total = total + nt(d_pre, w_up[:, cols])
        up.put(tn(low, d_pre), number, 0)
        rows = tn(act[:, cols], d_ffn)
        for row in range(0, width, chunk):
            block, mat = (at + row) // per_blk, (at + row) % per_blk // chunk
            down.put(rows[row : row + chunk], mat, 1, block, 1)
    return total


def attn_backward(dr, xq, xk_parts, saved, segs, seg_rows, w_input, w_out, layout, group, buffers, sums):
    att, lse, q8, k, v = saved
    dk_buf, dv_buf, dq_buf = buffers
    own_rows, width = dr.shape
    head_size = width // H
    factor = 1.0 / math.sqrt(head_size)
    d_branch = dr.astype(bf16)
    att_rows = att[...]
    layout.put(tn(att_rows.astype(bf16), d_branch), 3, group)
    do_turned = nt(w_out[...], d_branch).astype(bf16)
    delta = jnp.sum((do_turned.astype(f32) * att_rows.T).reshape(H, head_size, own_rows), axis=1)
    lse_turned = lse[...]
    q_turned = turned(q8[...]).astype(bf16)
    seg_key = as_column(segs[seg_rows[1] : seg_rows[1] + 1])
    bias = jnp.where(seg_key == segs[seg_rows[0] : seg_rows[0] + 1, 0:own_rows], 0.0, negative)
    masks = head_masks(0, (LANES, own_rows), head_size)
    for pair in range(width // LANES):
        cols = slice(pair * LANES, (pair + 1) * LANES)
        k_pair, v_pair = k[:, cols], v[:, cols]
        k_turned = turned(k_pair).astype(bf16)
        q_pair, do_pair = q_turned[cols], do_turned[cols]
        dk_pair, dv_pair = None, None
        for number, mask in enumerate(masks):
            head = pair * len(masks) + number
            zero = jnp.zeros_like(q_pair)
            q_head = jnp.where(mask, q_pair, zero)
            do_head = jnp.where(mask, do_pair, zero)
            probs = jnp.exp(nn(k_pair, q_head) + bias - lse_turned[head : head + 1])
            d_prob = nn(v_pair, do_head)
            d_score = (probs * (d_prob - delta[head : head + 1])).astype(bf16)
            dv_term = nt(probs.astype(bf16), do_head)
            dk_term = nt(d_score, q_head)
            dv_pair = dv_term if dv_pair is None else dv_pair + dv_term
            dk_pair = dk_term if dk_pair is None else dk_pair + dk_term
            rows = slice(head * head_size, (head + 1) * head_size)
            dq_buf[rows] = nn(k_turned[number * head_size : (number + 1) * head_size], d_score)
        dk_buf[:, cols] = dk_pair.astype(bf16)
        dv_buf[:, cols] = dv_pair.astype(bf16)
    dq = (dq_buf[...].T * factor).astype(bf16)
    layout.put(tn(xq, dq), 0, group)
    dk, dv = dk_buf[...], dv_buf[...]
    grad_key, grad_value = None, None
    at = 0
    for part in xk_parts:
        rows = part.shape[0]
        piece = part[...]
        key_term, value_term = tn(piece, dk[at : at + rows]), tn(piece, dv[at : at + rows])
        grad_key = key_term if grad_key is None else grad_key + key_term
        grad_value = value_term if grad_value is None else grad_value + value_term
        at += rows
    layout.put(grad_key, 1, group)
    layout.put(grad_value, 2, group)
    sums += [
        column_sum(d_branch.astype(f32)),
        column_sum(dq.astype(f32)),
        column_sum(dv.astype(f32)),
        jnp.zeros((3, width), f32),
    ]
    return nt(dq, w_input[0]), nt(dk, w_input[1]) + nt(dv, w_input[2])


def add_up(parts, own_rows):
    total = parts[0][0:own_rows].astype(f32)
    for part in parts[1:]:
        total = total + part[0:own_rows].astype(f32)
    return total


def pack_kernel(*refs):
    at = 0
    for ref in refs[:-1]:
        refs[-1][at : at + ref.shape[0]] = ref[...]
        at += ref.shape[0]


def self_attn(parts, segs, seg_rows, weights, q, att, lse, norm_one, rstd_one, buffers):
    k, v = buffers
    rows = attn_forward(parts, None, segs, seg_rows, weights, q, k, v, att, lse)
    normed, rstd = norm_forward(rows)
    norm_one[...] = normed
    rstd_one[...] = rstd
    return normed


def enc_forward_kernel(seg_rows, *refs):
    near, far, segs, w_input, b_query, b_value, w_out, b_out = refs[:8]
    gains, shifts, w_up, b_up, w_down, b_down = refs[8:14]
    q, att, lse, norm_one, rstd_one, act, slope, norm_two, rstd_two, low, k, v = refs[14:]
    weights = (w_input, b_query, b_value, w_out, b_out)
    normed = self_attn(
        [near, far], segs, seg_rows, weights, q, att, lse, norm_one, rstd_one, (k, v)
    )
    values = normed * gains[0:1] + shifts[0:1]
    normed, rstd = norm_forward(ffn_forward(values, (w_up, b_up, w_down, b_down), act, slope))
    norm_two[...] = normed
    rstd_two[...] = rstd
    low[...] = (normed * gains[1:2] + shifts[1:2]).astype(bf16)


def dec_forward_kernel(seg_rows, *refs):
    near, far, segs, w_input, b_query, b_value, w_out, b_out = refs[:8]
    q, att, lse, norm_one, rstd_one, k, v = refs[8:]
    weights = (w_input, b_query, b_value, w_out, b_out)
    self_attn([near, far], segs, seg_rows, weights, q, att, lse, norm_one, rstd_one, (k, v))


def cross_forward_kernel(part_count, cot_count, seg_rows, blocks, groups, table, *refs):
    refs = list(refs)
    parts, refs = refs[:part_count], refs[part_count:]
    cots, refs = refs[:cot_count], refs[cot_count:]
    prev_norm, segs, w_input, b_query, b_value, w_out, b_out, gains, shifts = refs[:9]
    w_up, b_up, w_down, b_down = refs[9:13]
    q, k, v, att, lse, norm_two_out, rstd_two_out, d_second = refs[13:21]
    homes = refs[21:23]
    keep, send, vecs, act, slope = refs[23:]
    own_rows = prev_norm.shape[0]
    upper = prev_norm[...] * gains[0:1] + shifts[0:1]
    weights = (w_input, b_query, b_value, w_out, b_out)
    branch = attn_forward(
        parts, upper.astype(bf16), segs, seg_rows, weights, q, k, v, att, lse
    )
    norm_two, rstd_two = norm_forward(upper + branch)
    norm_two_out[...] = norm_two
    rstd_two_out[...] = rstd_two
    crossed = norm_two * gains[1:2] + shifts[1:2]
    norm_three, rstd_three = norm_forward(
        ffn_forward(crossed, (w_up, b_up, w_down, b_down), act, slope)
    )
    low = (norm_three * gains[2:3] + shifts[2:3]).astype(bf16)
    tok = own_rows // 2
    memory = parts[0][...]
    for number, home in enumerate(homes):
        home[0] = memory[number * tok : (number + 1) * tok]
        home[1] = low[number * tok : (number + 1) * tok]
    dy = jnp.concatenate([cot[...] for cot in cots], axis=0).astype(f32)
    sums = []
    dr, d_gain, d_shift = norm_backward(dy, norm_three, rstd_three, gains[2:3])
    sums += [d_gain, d_shift]
    layout = Layout(table, keep, send, blocks, groups)
    d_second[...] = ffn_backward(
        dr, crossed.astype(bf16), act, slope, w_up, w_down, layout, layout, blocks, sums
    )
    sums.append(jnp.zeros_like(d_gain))
    vecs[...] = jnp.concatenate(sums, axis=0)


def cross_backward_kernel(part_count, has_mid, seg_rows, blocks, groups, table, *refs):
    refs = list(refs)
    parts, refs = refs[:part_count], refs[part_count:]
    d_in, norm_two, rstd_two, prev_norm, gains, shifts = refs[:6]
    att, w_out, lse, q, k, v, segs, w_input = refs[6:14]
    refs = refs[14:]
    d_upper, d_own = refs[:2]
    refs = refs[2:]
    d_mid = refs.pop(0) if has_mid else None
    d_far, keep, send, vecs = refs[:4]
    buffers = refs[4:]
    own_rows = prev_norm.shape[0]
    sums = []
    dr, d_gain, d_shift = norm_backward(d_in[...], norm_two[...], rstd_two[...], gains[1:2])
    sums += [d_gain, d_shift]
    xq = (prev_norm[...] * gains[0:1] + shifts[0:1]).astype(bf16)
    layout = Layout(table, keep, send, blocks, groups)
    d_query, d_key = attn_backward(
        dr, xq, parts, (att, lse, q, k, v), segs, seg_rows, w_input, w_out, layout, 0, buffers, sums
    )
    keys = d_key.shape[0]
    d_upper[...] = dr + d_query
    d_own[...] = d_key[0:own_rows]
    if has_mid:
        d_mid[...] = d_key[own_rows : keys // 2].astype(bf16)
    d_far[...] = d_key[keys // 2 :].astype(bf16)
    vecs[...] = jnp.concatenate(sums, axis=0)


def ffn_backward_kernel(part_count, blocks, groups, table, *refs):
    parts, refs = refs[:part_count], refs[part_count:]
    norm_two, rstd_two, norm_one, gains, shifts, slope, w_down, act, w_up = refs[:9]
    d_out, keep, send, vecs = refs[9:]
    sums = []
    dy = add_up(parts, norm_one.shape[0])
    dr, d_gain, d_shift = norm_backward(dy, norm_two[...], rstd_two[...], gains[1:2])
    sums += [d_gain, d_shift]
    low = (norm_one[...] * gains[0:1] + shifts[0:1]).astype(bf16)
    layout = Layout(table, keep, send, blocks, groups)
    d_out[...] = ffn_backward(dr, low, act, slope, w_up, w_down, layout, layout, blocks, sums)
    sums.append(jnp.zeros_like(d_gain))
    vecs[...] = jnp.concatenate(sums, axis=0)


def self_backward_kernel(has_mid, vec_count, seg_rows, blocks, groups, table, segs, *refs):
    refs = list(refs)
    vecs_in, refs = refs[:vec_count], refs[vec_count:]
    d_in, norm_one, rstd_one, gains, att, w_out, lse, q, near, far, w_input, b_value = refs[:12]
    refs = refs[12:]
    d_own = refs.pop(0)
    mid = refs.pop(0) if has_mid else None
    far_out, keep, send = refs[:3]
    refs = refs[3:]
    vecs = None if vec_count else refs.pop(0)
    k, v = refs[:2]
    buffers = refs[2:]
    own_rows, width = norm_one.shape
    layout = Layout(table, keep, send, blocks, groups)
    sums = []
    dr, d_gain, d_shift = norm_backward(d_in[...], norm_one[...], rstd_one[...], gains[0:1])
    sums += [d_gain, d_shift]
    keys_values([near, far], w_input, b_value, k, v)
    xq = near[0:own_rows]
    d_query, d_key = attn_backward(
        dr, xq, [near, far], (att, lse, q, k, v), segs, seg_rows, w_input, w_out, layout, 0, buffers, sums
    )
    keys = d_key.shape[0]
    d_own[...] = dr + d_query + d_key[0:own_rows]
    if has_mid:
        mid[0] = d_key[own_rows : keys // 2].astype(bf16)
    far_out[0] = d_key[keys // 2 :].astype(bf16)
    if not vec_count:
        vecs[...] = jnp.concatenate(sums, axis=0)
        return
    all_sums = [vec[...] for vec in vecs_in] + sums
    more = keep.shape[0] - 2 * blocks
    rows = keep.shape[1]
    pad = more * rows - sum(piece.shape[0] for piece in all_sums)
    if pad:
        all_sums.append(jnp.zeros((pad, width), f32))
    all_sums = jnp.concatenate(all_sums, axis=0).astype(bf16)
    for number in range(more):
        keep[2 * blocks + number] = all_sums[number * rows : (number + 1) * rows]
        send[2 * blocks + number] = all_sums[number * rows : (number + 1) * rows]


def middle_kernel(own_rows, pairs, *refs):
    for number, out in enumerate(refs[2 * pairs :]):
        mine = slice(number * own_rows, (number + 1) * own_rows)
        far = slice((number + 1) * own_rows, (number + 2) * own_rows)
        for at in range(pairs):
            total = refs[2 * at][0, mine].astype(f32) + refs[2 * at + 1][0, far].astype(f32)
            out[at] = total.astype(bf16)


def homes_kernel(count, *refs):
    homes = refs[-2:]
    tok = homes[0].shape[1]
    for number in range(count):
        total = refs[2 * number][...] + refs[2 * number + 1][0, 0 : 2 * tok].astype(f32)
        for term in refs[2 * count : -2]:
            total = total + term[number].astype(f32)
        total = total.astype(bf16)
        for d_lo, home in enumerate(homes):
            home[number] = total[d_lo * tok : (d_lo + 1) * tok]


def gate_kernel(out):
    out[...] = jnp.zeros_like(out)


def combine_kernel(count, plan, *refs):
    inputs, outputs = refs[:count], refs[count:]
    for out, segments in zip(outputs, plan):
        at = 0
        for chunks, terms in segments:
            total = None
            for number, first in terms:
                term = inputs[number][first : first + chunks].astype(f32)
                total = term if total is None else total + term
            out[at : at + chunks] = total.astype(out.dtype)
            at += chunks


def place_kernel(table, got_one, got_two, *outs):
    for number, out in enumerate(outs):
        out[table[0]] = got_one[number].astype(out.dtype)
        out[lax.bitwise_xor(table[0], 1)] = got_two[number].astype(out.dtype)


def unpack_kernel(kinds, vec_rows, table, *refs):
    refs = list(refs)
    mats = refs[:MATS]
    refs = refs[MATS:]
    vec = refs.pop(0) if vec_rows else None
    scratch = refs.pop()
    for rel in range(MATS):
        scratch[lax.bitwise_xor(table[0], rel)] = mats[rel][...].astype(f32)
    width = mats[0].shape[2]
    rows = mats[0].shape[1]
    for group, kind in enumerate(kinds):
        if kind == "attn":
            w_input, w_out = refs.pop(0), refs.pop(0)
            for mat in range(MATS - 1):
                w_input[mat] = scratch[mat, group]
            w_out[...] = scratch[MATS - 1, group]
        elif kind == "up":
            out = refs.pop(0)
            for mat in range(MATS):
                out[:, mat * width : (mat + 1) * width] = scratch[mat, group]
        else:
            out = refs.pop(0)
            for mat in range(MATS):
                out[mat * rows : (mat + 1) * rows] = scratch[mat, group]
    if vec_rows:
        sums = jnp.concatenate([vec[number] for number in range(vec.shape[0])], axis=0).astype(f32)
        for out, numbers in zip(refs, vec_rows):
            for at, number in enumerate(numbers):
                if out.shape[0] == 1:
                    out[:, at * width : (at + 1) * width] = sums[number : number + 1]
                else:
                    out[at : at + 1] = sums[number : number + 1]


def on_device(
    source,
    target,
    src_lengths,
    tgt_lengths,
    pairing,
    enc_w_input,
    enc_b_query,
    enc_b_value,
    enc_w_out,
    enc_b_out,
    enc_gains,
    enc_shifts,
    enc_w_up,
    enc_b_up,
    enc_w_down,
    enc_b_down,
    dec_w_input,
    dec_b_query,
    dec_b_value,
    dec_w_out,
    dec_b_out,
    cross_w_input,
    cross_b_query,
    cross_b_value,
    cross_w_out,
    cross_b_out,
    dec_gains,
    dec_shifts,
    dec_w_up,
    dec_b_up,
    dec_w_down,
    dec_b_down,
    cotangent,
):
    streams, tok, width = source.shape
    n_batch, n_blk = lax.axis_size("batch"), lax.axis_size("blk")
    half = n_blk // 2
    mids = n_blk // 4
    own_rows = 2 * tok
    total_rows = n_blk * tok
    near_rows = total_rows // 2
    chunk_rows = width // n_blk
    ff = enc_w_up.shape[1]
    b, i = lax.axis_index("batch"), lax.axis_index("blk")
    core, y_bit = b & 1, (b >> 1) & 1
    hi, mid, lo = i // half, (i % half) // 2, i & 1

    def move(values, where):
        pairs = []
        for from_b in range(n_batch):
            for from_i in range(n_blk):
                to_b, to_i = where(from_b, from_i)
                pairs.append((from_b * n_blk + from_i, to_b * n_blk + to_i))
        return lax.ppermute(values, ("batch", "blk"), pairs)

    def regroup(values, d_mid, d_lo):
        def where(fb, fi):
            f_hi, f_mid, f_lo, f_core = fi // half, (fi % half) // 2, fi & 1, fb & 1
            return ((fb & ~1) | f_hi, f_core * half + (f_mid ^ d_mid) * 2 + (f_lo ^ d_lo))

        return move(values, where)

    to_bits = lambda values, d_b, d_i: move(values, lambda fb, fi: (fb ^ d_b, fi ^ d_i))
    to_core = lambda values: to_bits(values, 1, 0)
    to_mid = lambda values, d_mid: to_bits(values, 0, 2 * d_mid)

    last = []

    def call(kernel, outs, args, scratch=(), name=None, passed=(), after=()):
        vmem_bytes = min(total_rows * ROW_BYTES, MOST_BYTES)
        held_back = last[-1:] + list(after)
        got = call_kernel(kernel, outs, args, scratch, name, held_back, list(passed), vmem_bytes)
        last.append(min(got[: len(outs)], key=lambda array: array.size))
        return got

    bits = n_blk.bit_length() - 1
    batch_bits = n_batch.bit_length() - 1
    more_dims = [(1 << bit,) for bit in range(2, batch_bits)]
    rest = list(range(2, bits))
    orders = {
        "x": [0, "y", 1] + rest,
        "y": ["y", 0, 1] + rest,
        "z": [1] + rest + ["y", 0],
    }

    def group_of(kind):
        at = list(orders).index(kind)
        return (1 + at * n_blk, 1 << (bits - orders[kind].index("y")))

    def places_of(order):
        step = {name: 1 << (bits - at) for at, name in enumerate(order)}
        return [
            sum((((number ^ i) >> bit) & 1) * step[bit] for bit in range(bits))
            for number in range(n_blk)
        ]

    all_places = [place for order in orders.values() for place in places_of(order)]
    mat_table = jnp.stack([2 * core + y_bit] + all_places).astype(jnp.int32)

    def state(kind, keep, got, group):
        first = group * 2 * n_blk
        return (orders[kind] + more_dims, 1, False, [(keep, first), (got, first)])

    runs = [
        (core ^ d_core) * half + (mid ^ d_mid) * 2 + (lo ^ d_lo)
        for d_core in range(2)
        for d_mid in range(mids)
        for d_lo in range(2)
    ]
    place_table = jnp.stack([(hi == core).astype(jnp.int32), lo] + runs).astype(jnp.int32)
    lo_table = jnp.stack([lo, lo]).astype(jnp.int32)
    row = lambda values: values.reshape(1, -1)

    def stream_of(values, number):
        return lax.dynamic_index_in_dim(values, number, 0, keepdims=False)

    def near_parts(values):
        return [
            regroup(stream_of(values, lo ^ d_lo), d_mid, d_lo)
            for d_mid in range(mids)
            for d_lo in range(2)
        ]

    held = lambda arrays: [("v", array) for array in arrays]
    packed = lambda chunks: ((chunks, chunk_rows, width), bf16)
    rows_f32 = ((own_rows, width), f32)
    rows_bf16 = ((own_rows, width), bf16)
    one_f32 = ((own_rows, 1), f32)
    lse_shape = ((H, own_rows), f32)
    all_keys = ((total_rows, width), bf16)
    vec_shape = ((8, width), f32)
    has_mid = near_rows > own_rows
    key_buffers = [pltpu.VMEM(*all_keys), pltpu.VMEM(*all_keys)]
    back_buffers = key_buffers + [pltpu.VMEM((width, own_rows), f32)]
    def pack(parts):
        return call(pack_kernel, [((near_rows, width), bf16)], held(parts), name="pack")[0]

    src_parts = near_parts(source)
    tgt_parts = near_parts(target)
    cot_parts = [regroup(stream_of(cotangent, lo ^ d_lo), 0, d_lo) for d_lo in range(2)]
    lists = jnp.stack([src_lengths, tgt_lengths, pairing])
    (segs,) = call(
        lambda *refs: segments_kernel(tok, *refs),
        [((8, total_rows), f32)],
        [("s", place_table)] + held([lists, to_core(lists)]),
        name="segments",
    )
    src_rows, tgt_rows, pair_rows = (0, 0), (1, 1), (2, 0)
    src_near = pack(src_parts)
    src_far = to_core(src_near)

    def spread_mid(pairs, after=()):
        if not has_mid:
            return []
        totals = call(
            lambda *refs: middle_kernel(own_rows, len(pairs), *refs),
            [((len(pairs), own_rows, width), bf16)] * (mids - 1),
            held([array for pair in pairs for array in pair]),
            name="middle",
            after=after,
        )
        return [to_mid(total, d_mid) for d_mid, total in enumerate(totals, 1)]

    def homeward(homes):
        return [regroup(home, 0, d_lo) for d_lo, home in enumerate(homes)]

    def place_home(got, kinds, passed=()):
        outs = [((streams, tok, width), kind) for kind in kinds]
        return call(
            place_kernel, outs, [("s", lo_table)] + held(got), name="place", passed=passed
        )

    def combine(plan_outs, passed=(), after=()):
        arrays, index, plan, outs = [], {}, [], []
        for segments, kind in plan_outs:
            rows = []
            for chunks, terms in segments:
                named = []
                for array, first in terms:
                    if id(array) not in index:
                        index[id(array)] = len(arrays)
                        arrays.append(array)
                    named.append((index[id(array)], first))
                rows.append((chunks, named))
            plan.append(rows)
            outs.append(((sum(chunks for chunks, _ in rows), chunk_rows, width), kind))
        return call(
            lambda *refs: combine_kernel(len(arrays), plan, *refs),
            outs,
            held(arrays),
            name="combine",
            passed=passed,
            after=after,
        )

    def offset(name):
        if name == "y":
            return (2, 0)
        if isinstance(name, tuple):
            return (name[0], 0)
        return (0, 1 << name)

    def step(states, passed=(), after=()):
        mine, away, found = [], {}, []
        sizes = {}
        for left, chunks, whole, terms in states:
            if not left:
                found.append((left, chunks, whole, terms, None, None))
                continue
            name, rest = left[0], left[1:]
            full = whole or isinstance(name, tuple)
            count = chunks << (0 if whole else sum(not isinstance(dim, tuple) for dim in rest))
            own_at = sum(n for n, _ in mine)
            mine.append((count, terms))
            segments = away.setdefault(name, [])
            far_at = sum(n for n, _ in segments)
            start = 0 if full else count
            segments.append((count, [(array, first + start) for array, first in terms]))
            found.append((rest, chunks, whole, own_at, name, far_at))
        plan = [(mine, bf16)] + [(segments, bf16) for segments in away.values()]
        arrays = combine(plan, passed, after)
        got = {}
        for name, array in zip(away, arrays[1:]):
            got[name] = to_bits(array, *offset(name))
        stepped = []
        for rest, chunks, whole, own_at, name, far_at in found:
            terms = own_at if name is None else [(arrays[0], own_at), (got[name], far_at)]
            stepped.append((rest, chunks, whole, terms))
        return stepped + list(arrays[len(plan) :])

    def finish(states):
        while any(left for left, _, _, _ in states):
            states = step(states)
        return states

    def arrived(states):
        return [array for _, _, _, terms in states for array, _ in terms[1:]]

    def sum_of(states):
        return [(chunks, terms) for _, chunks, _, terms in states]

    def attn_args(w_input, b_query, b_value, w_out, b_out):
        return held([w_input, row(b_query), row(b_value), w_out, row(b_out)])

    def ffn_args(w_up, b_up, w_down, b_down):
        return held([w_up, row(b_up), w_down, row(b_down)])

    enc_q, enc_att, enc_lse, enc_n1, enc_r1, enc_act, enc_slope, enc_n2, enc_r2, memory = call(
        lambda *refs: enc_forward_kernel(src_rows, *refs),
        [rows_bf16, rows_f32, lse_shape, rows_f32, one_f32]
        + [((own_rows, ff), bf16), ((own_rows, ff), bf16), rows_f32, one_f32, rows_bf16],
        held([src_near, src_far, segs])
        + attn_args(enc_w_input, enc_b_query, enc_b_value, enc_w_out, enc_b_out)
        + held([enc_gains, enc_shifts])
        + ffn_args(enc_w_up, enc_b_up, enc_w_down, enc_b_down),
        scratch=key_buffers,
        name="enc_forward",
    )
    ffn_groups = [group_of("x"), group_of("y")]
    places = [(d_core, d_mid) for d_core in range(2) for d_mid in range(mids)]
    mem_parts = [memory] + [
        to_bits(memory, d_core, 2 * d_mid) for d_core, d_mid in places[1:]
    ]
    tgt_near = pack(tgt_parts)
    tgt_far = to_core(tgt_near)
    dec_q, dec_att, dec_lse, dec_n1, dec_r1 = call(
        lambda *refs: dec_forward_kernel(tgt_rows, *refs),
        [rows_bf16, rows_f32, lse_shape, rows_f32, one_f32],
        held([tgt_near, tgt_far, segs])
        + attn_args(dec_w_input, dec_b_query, dec_b_value, dec_w_out, dec_b_out),
        scratch=key_buffers,
        name="dec_forward",
    )

    got = call(
        lambda *refs: cross_forward_kernel(
            len(mem_parts), len(cot_parts), pair_rows, n_blk, ffn_groups, *refs
        ),
        [rows_bf16, all_keys, all_keys, rows_f32, lse_shape, rows_f32, one_f32, rows_f32]
        + [((2, tok, width), bf16)] * 2
        + [packed(4 * n_blk)] * 2
        + [vec_shape],
        [("s", mat_table)]
        + held(mem_parts + cot_parts + [dec_n1, segs])
        + attn_args(cross_w_input, cross_b_query, cross_b_value, cross_w_out, cross_b_out)
        + held([dec_gains, dec_shifts])
        + ffn_args(dec_w_up, dec_b_up, dec_w_down, dec_b_down),
        scratch=[pltpu.VMEM((own_rows, ff), bf16), pltpu.VMEM((own_rows, ff), bf16)],
        name="cross_forward",
    )
    cr_q, cr_k, cr_v, cr_att, cr_lse, dec_n2, dec_r2, d_second = got[:8]
    homes = homeward(got[8:10])
    df_keep, df_send, df_vec = got[10:]
    df_got = to_core(df_send)
    mid_shape = [((near_rows - own_rows, width), bf16)] if has_mid else []
    got = list(
        call(
            lambda *refs: cross_backward_kernel(
                len(mem_parts), has_mid, pair_rows, n_blk, [group_of("z")], *refs
            ),
            [rows_f32, rows_f32]
            + mid_shape
            + [((near_rows, width), bf16)]
            + [packed(2 * n_blk)] * 2
            + [vec_shape],
            [("s", mat_table)]
            + held(mem_parts)
            + held([d_second, dec_n2, dec_r2, dec_n1, dec_gains, dec_shifts])
            + held([cr_att, cross_w_out, cr_lse, cr_q, cr_k, cr_v, segs, cross_w_input]),
            scratch=back_buffers,
            name="cross_backward",
        )
    )
    d_upper, d_mem_own = got[:2]
    d_mem_mid = got[2][None] if has_mid else None
    d_mem_far, cr_keep, cr_send, cr_vec = got[2 + len(mid_shape) :]
    df = step([state("x", df_keep, df_got, 0), state("y", df_keep, df_got, 1)])
    mem_got = to_core(d_mem_far[None])
    mem_terms = [mem_got[0]] + [term[0] for term in spread_mid([(d_mem_mid, mem_got)])]
    cr_got = to_core(cr_send)

    d_first, ef_keep, ef_send, ef_vec = call(
        lambda *refs: ffn_backward_kernel(1 + len(mem_terms), n_blk, ffn_groups, *refs),
        [rows_f32] + [packed(4 * n_blk)] * 2 + [vec_shape],
        [("s", mat_table)]
        + held([d_mem_own] + mem_terms)
        + held([enc_n2, enc_r2, enc_n1, enc_gains, enc_shifts])
        + held([enc_slope, enc_w_down, enc_act, enc_w_up]),
        name="ffn_backward",
    )
    _, ef_send = call(
        gate_kernel, [((8, LANES), f32)], [], name="gate", after=arrived(df), passed=[ef_send]
    )
    ef_got = to_core(ef_send)
    early = step(
        [
            state("x", ef_keep, ef_got, 0),
            state("y", ef_keep, ef_got, 1),
            state("z", cr_keep, cr_got, 0),
        ]
    )

    def self_backward(d_in, saved, seg_rows, kind, vecs_in=()):
        more = -(-8 * (len(vecs_in) + 1) // chunk_rows) if vecs_in else 0
        got = call(
            lambda *refs: self_backward_kernel(
                has_mid, len(vecs_in), seg_rows, n_blk, [group_of(kind)], *refs
            ),
            [rows_f32]
            + [((1,) + shape, kind) for shape, kind in mid_shape]
            + [((1, near_rows, width), bf16)]
            + [packed(2 * n_blk + more)] * 2
            + ([] if vecs_in else [vec_shape]),
            [("s", mat_table)] + held([segs] + list(vecs_in) + [d_in] + saved),
            scratch=key_buffers + back_buffers,
            name="self_backward",
        )
        got = list(got)
        if not has_mid:
            got.insert(1, None)
        return got

    d_tgt_own, d_tgt_mid, d_tgt_far, de_keep, de_send, de_vec = self_backward(
        d_upper,
        [dec_n1, dec_r1, dec_gains, dec_att, dec_w_out, dec_lse, dec_q]
        + [tgt_near, tgt_far, dec_w_input, row(dec_b_value)],
        tgt_rows,
        "y",
    )
    *early, de_send, d_tgt_far = step(early + df, passed=[de_send, d_tgt_far], after=homes)
    de_got, tgt_got = to_core(de_send), to_core(d_tgt_far)
    d_src_own, d_src_mid, d_src_far, en_keep, en_send = self_backward(
        d_first,
        [enc_n1, enc_r1, enc_gains, enc_att, enc_w_out, enc_lse, enc_q]
        + [src_near, src_far, enc_w_input, row(enc_b_value)],
        src_rows,
        "x",
        [df_vec, cr_vec, de_vec, ef_vec],
    )

    def gather(own):
        side = to_bits(own, 2, 0)
        return [own, side, to_core(own), to_core(side)]

    def unpack(kinds, mats, vec=None, vec_rows=(), wide=()):
        outs = []
        for kind in kinds:
            if kind == "attn":
                outs += [((MATS - 1, chunk_rows, width), f32), ((chunk_rows, width), f32)]
            elif kind == "up":
                outs.append(((chunk_rows, MATS * width), f32))
            else:
                outs.append(((MATS * chunk_rows, width), f32))
        for number, numbers in enumerate(vec_rows):
            shape = (len(numbers), width) if number in wide else (1, len(numbers) * width)
            outs.append((shape, f32))
        return call(
            lambda *refs: unpack_kernel(kinds, vec_rows, *refs),
            outs,
            [("s", mat_table)] + held(list(mats) + ([vec] if vec_rows else [])),
            scratch=[pltpu.VMEM((MATS,) + mats[0].shape, f32)],
            name="unpack",
        )

    ef, cr, df = early[:2], early[2:3], early[3:]
    *df, en_send, d_src_far = step(
        df, passed=[en_send, d_src_far], after=arrived(ef + cr) + [de_got, tgt_got]
    )
    en_got, src_got = to_core(en_send), to_core(d_src_far)
    sums_at = 2 * n_blk
    late = step(
        [
            state("x", en_keep, en_got, 0),
            state("y", de_keep, de_got, 0),
            (
                orders["x"] + more_dims,
                en_keep.shape[0] - sums_at,
                True,
                [(en_keep, sums_at), (en_got, sums_at)],
            ),
        ]
        + cr
    )
    terms = spread_mid([(d_src_mid, src_got), (d_tgt_mid, tgt_got)], arrived(df))
    enc_out, dec_out = place_home(homes, (bf16, bf16))
    ef = step(ef)
    late = step(late)
    homes_back = homeward(
        call(
            lambda *refs: homes_kernel(2, *refs),
            [((2, tok, width), bf16)] * 2,
            held([d_src_own, src_got, d_tgt_own, tgt_got] + terms),
            name="homes",
        )
    )
    late, cr = late[:3], late[3:]
    late = step(late)
    early = step(ef + df, after=homes_back)
    late = step(late)
    early = finish(early + cr)
    (early_own,) = combine([(sum_of(early), bf16)])
    early_mats = gather(early_own)
    late = finish(late)
    own, vec = combine([(sum_of(late[:2]), bf16), (sum_of(late[2:]), f32)])
    mats = [own] + [to_bits(own, d_b, 0) for d_b in (2, 1, 3)]
    source_grad, target_grad = place_home(homes_back, (f32, f32))
    got = unpack(("up", "down", "up", "down", "attn"), early_mats)
    g_ef_up, g_ef_down, g_df_up, g_df_down, g_cr_in, g_cr_out = got
    df, cr, de, ef, en = 0, 8, 16, 24, 32
    vec_rows = [
        [en + 3],
        [en + 4],
        [en + 2],
        [en, ef],
        [en + 1, ef + 1],
        [ef + 3, ef + 4, ef + 5, ef + 6],
        [ef + 2],
        [de + 3],
        [de + 4],
        [de + 2],
        [cr + 3],
        [cr + 4],
        [cr + 2],
        [de, cr, df],
        [de + 1, cr + 1, df + 1],
        [df + 3, df + 4, df + 5, df + 6],
        [df + 2],
    ]
    wide = (3, 4, 13, 14)
    got = unpack(("attn", "attn"), mats, vec, vec_rows, wide)
    g_en_in, g_en_out, g_de_in, g_de_out = got[:4]
    vectors = [
        values if number in wide else values.reshape(-1) for number, values in enumerate(got[4:])
    ]
    return (
        enc_out,
        dec_out,
        source_grad,
        target_grad,
        g_en_in,
        vectors[0],
        vectors[1],
        g_en_out,
        vectors[2],
        vectors[3],
        vectors[4],
        g_ef_up,
        vectors[5],
        g_ef_down,
        vectors[6],
        g_de_in,
        vectors[7],
        vectors[8],
        g_de_out,
        vectors[9],
        g_cr_in,
        vectors[10],
        vectors[11],
        g_cr_out,
        vectors[12],
        vectors[13],
        vectors[14],
        g_df_up,
        vectors[15],
        g_df_down,
        vectors[16],
    )


def solution(mesh):
    rows = P("batch", "blk", None)
    lists = P("batch", None)
    by_row = P("blk", None)
    stacked = P(None, "blk", None)
    whole = P()
    return jax.shard_map(
        on_device,
        mesh=mesh,
        in_specs=(rows, rows, lists, lists, lists) + (whole,) * 27 + (rows,),
        out_specs=(rows, rows, rows, rows)
        + (stacked, whole, whole, by_row, whole, whole, whole, by_row, whole, by_row, whole)
        + (stacked, whole, whole, by_row, whole)
        + (stacked, whole, whole, by_row, whole, whole, whole, by_row, whole, by_row, whole),
        check_vma=False,
    )
```
